256 devices in a mesh: gx: 16 (over z_hi, y), gy: 16 (over z_lo, x, core).
Axes of the slice: x: 4, y: 4, z: 8 (z_hi: 4, z_lo: 2; z = z_hi * 2 + z_lo), core: 2. Of those that a mesh axis runs over, the one named last changes fastest.
Arguments:
- prior_kelvin_state: float32 [512, 512, 128], P('gx', 'gy'), may hold values from 0 to 6
- substance_identifier: int32 [512, 512, 128], P('gx', 'gy'), may hold values from 0 to 3
- chip_touch_indicator: int32 [512, 512, 128], P('gx', 'gy'), may hold values from 0 to 1
- substance_reference_diffusivity: float32 [4], replicated, may hold values from 1 to 8
- substance_diffusivity_gradient: float32 [4], replicated, may hold values from -0.5 to 0.5
- substance_storage_coefficient: float32 [4], replicated, may hold values from 0.5 to 2
- clearance_point_indices: int32 [262144], P(('gx', 'gy')), may hold values from 0 to 262143, as said below
- clearance_face_pressure: float32 [262144], P(('gx', 'gy')), may hold values from 0.5 to 2
Outputs:
- temperature: float32 [512, 512, 128], P('gx', 'gy')
- clearance_abrasion_growth: float32 [262144], P(('gx', 'gy'))
The draws below stay inside these ranges and needn't reach their ends.
Inputs may be any that keep to these rules, and one draw needn't show every extreme that they name: `clearance_point_indices`: each surface cell i * 512 + j is named by exactly one flank site.
All inputs are finite; a program needn't handle non-finite values.
Results may differ from the reference program's by a relative error of at most 0.0001.
Values sent between devices are 32-bit elements; how exact they have to be, the bound alone decides.
No kernel may reach another device: no remote copies, remote signals or barrier semaphores. Data moves between devices by JAX's collectives and lax.ppermute only.
A program may use at most 64 MiB of HBM per device.

```python
import math
import jax
import jax.numpy as jnp

CX = 32
CY = 32
NZ = 128
ITERS = 3
MATS = 4
NX = 512
NY = 512
SITES = 262144


def draw_prior_kelvin_state(key, part):
    key = jax.random.fold_in(key, 3)
    row_index = jnp.arange(NX, dtype=jnp.float32).reshape(NX, 1, 1)
    ramp_up = 1.0 + 2.0 * row_index / max(NX - 1, 1)
    roughness = jnp.clip(0.4 * jax.random.normal(key, (NX, NY, NZ), jnp.float32), -0.8, 0.8)
    return ramp_up * (1.0 + roughness)


def draw_chip_touch_indicator(key, part):
    key = jax.random.fold_in(key, 11)
    column_index = jnp.arange(NY, dtype=jnp.int32).reshape(1, NY, 1)
    contact_level = jnp.where(column_index * 4 < NY, 9, jnp.where(column_index * 2 < NY, 3, 0))
    random_rolls = jax.random.randint(key, (NX, NY, NZ), 0, 10)
    return (random_rolls < contact_level).astype(jnp.int32)


def draw_clearance_point_indices(key, part):
    key = jax.random.fold_in(key, 23)
    block_cells = CX * CY
    owners = SITES // block_cells
    owner_cols = NY // CY
    key_owner, key_whole, key_pick, key_rows, key_pool = jax.random.split(key, 5)
    owner_order = jax.random.permutation(key_owner, owners).astype(jnp.int32)
    within_block = jnp.arange(block_cells, dtype=jnp.int32).reshape(1, block_cells)
    owner_row = (owner_order // owner_cols).reshape(owners, 1)
    owner_col = (owner_order % owner_cols).reshape(owners, 1)
    cell_index = (owner_row * CX + within_block // CY) * NY + owner_col * CY + within_block % CY
    cell_index = jax.random.permutation(key_rows, cell_index, axis=1, independent=True)
    whole_rows = jax.random.randint(key_whole, (owners,), 0, 2).astype(jnp.int32)
    whole_rows = whole_rows.at[jax.random.randint(key_pick, (), 0, owners)].set(1)
    pooled = jnp.repeat(1 - whole_rows, block_cells, total_repeat_length=SITES)
    flat_cells = cell_index.reshape(-1).astype(jnp.int32)
    position = jnp.arange(SITES, dtype=jnp.int32)
    random_rank = jax.random.permutation(key_pool, SITES).astype(jnp.int32)
    natural_order = jnp.argsort((1 - pooled) * SITES + position, stable=True)
    random_order = jnp.argsort(jnp.where(pooled == 1, random_rank, SITES + position), stable=True)
    return jnp.zeros((SITES,), jnp.int32).at[natural_order].set(flat_cells[random_order])


def place_ends(drawn, rng, least, high):
    extent = drawn.shape
    index_at = [jax.random.randint(jax.random.fold_in(rng, axis), (), 0, extent[axis]) for axis in range(len(extent))]
    drawn = drawn.at[tuple(index_at)].set(least)
    longest = extent.index(max(extent))
    index_at[longest] = (index_at[longest] + 1) % extent[longest]
    return drawn.at[tuple(index_at)].set(high)


def block_levels(stream_key, extent, cuts, smallest, high):
    level = 1.0
    for dim, parts in cuts:
        heights = jax.random.uniform(jax.random.fold_in(jax.random.fold_in(stream_key, 6), dim), (parts,), jnp.float32, smallest / len(cuts), high / len(cuts))
        level = level * jnp.repeat(jnp.exp(heights), extent[dim] // parts).reshape((-1,) + (1,) * (len(extent) - 1 - dim))
    return level


def setup_inputs(seed: int = 0) -> dict:
    keys = jax.random.split(jax.random.key(seed), 9)
    return {
        "prior_kelvin_state": draw_prior_kelvin_state(jax.random.fold_in(keys[8], 71), 0),
        "substance_identifier": place_ends(jax.random.randint(keys[1], (NX, NY, NZ), 0, MATS), jax.random.fold_in(keys[1], 1), 0, MATS - 1).astype(jnp.int32),
        "chip_touch_indicator": draw_chip_touch_indicator(jax.random.fold_in(keys[8], 71), 0),
        "substance_reference_diffusivity": jnp.clip(jnp.exp(jax.random.uniform(keys[3], (MATS,), jnp.float32, math.log(1.0), math.log(8.0))), 1.0, 8.0),
        "substance_diffusivity_gradient": jnp.clip(jax.random.uniform(keys[4], (MATS,), jnp.float32, -0.5, 0.5), -0.5, 0.5),
        "substance_storage_coefficient": jnp.clip(jnp.exp(jax.random.uniform(keys[5], (MATS,), jnp.float32, math.log(0.5), math.log(2.0))), 0.5, 2.0),
        "clearance_point_indices": draw_clearance_point_indices(jax.random.fold_in(keys[8], 71), 0),
        "clearance_face_pressure": jnp.clip(jnp.exp(math.log(2.0) - 1.3862944 * jax.random.uniform(keys[7], (SITES,), jnp.float32) ** block_levels(keys[7], (SITES,), ((0, 256),), -0.2, 0.2)), 0.5, 2.0),
    }


clock_advance = 2.0
interface_warming_rate = 3.0
usui_rate = 3.0
usui_energy = 4.0
kelvin_shift_amount = 2.0


def substance_indexer(substance_identifier, entries):
    result = jnp.zeros(substance_identifier.shape, entries.dtype)
    for number in range(MATS):
        result = result + jnp.where(substance_identifier == number, entries[number], 0.0)
    return result


def neighbours(padded):
    return [padded[2:, 1:-1, 1:-1], padded[:-2, 1:-1, 1:-1], padded[1:-1, 2:, 1:-1], padded[1:-1, :-2, 1:-1], padded[1:-1, 1:-1, 2:], padded[1:-1, 1:-1, :-2]]


def apply_system_matrix(values_in, matrix_main_entries, side_coupling_entries):
    others = neighbours(jnp.pad(values_in, 1))
    summed = side_coupling_entries[0] * others[0]
    for number in range(1, 6):
        summed = summed + side_coupling_entries[number] * others[number]
    return matrix_main_entries * values_in - clock_advance * summed


def reference(prior_kelvin_state, substance_identifier, chip_touch_indicator, substance_reference_diffusivity, substance_diffusivity_gradient, substance_storage_coefficient, clearance_point_indices, clearance_face_pressure):
    diffusivity_distribution = substance_indexer(substance_identifier, substance_reference_diffusivity) * (1.0 + substance_indexer(substance_identifier, substance_diffusivity_gradient) * jnp.tanh(prior_kelvin_state - kelvin_shift_amount))
    storage_coefficient_map = substance_indexer(substance_identifier, substance_storage_coefficient)
    side_coupling_entries = [0.5 * (diffusivity_distribution + neighbour) for neighbour in neighbours(jnp.pad(diffusivity_distribution, 1))]
    coupled = side_coupling_entries[0]
    for number in range(1, 6):
        coupled = coupled + side_coupling_entries[number]
    matrix_main_entries = storage_coefficient_map + clock_advance * coupled
    generation_right_side = storage_coefficient_map * prior_kelvin_state + clock_advance * interface_warming_rate * chip_touch_indicator.astype(prior_kelvin_state.dtype)
    updated_kelvin_state = prior_kelvin_state
    equation_mismatch = generation_right_side - apply_system_matrix(updated_kelvin_state, matrix_main_entries, side_coupling_entries)
    precond = equation_mismatch / matrix_main_entries
    search_vector = precond
    inner_sum = jnp.sum(equation_mismatch * precond)
    for iteration in range(ITERS):
        applied = apply_system_matrix(search_vector, matrix_main_entries, side_coupling_entries)
        descent_scalar = inner_sum / jnp.sum(search_vector * applied)
        updated_kelvin_state = updated_kelvin_state + descent_scalar * search_vector
        equation_mismatch = equation_mismatch - descent_scalar * applied
        precond = equation_mismatch / matrix_main_entries
        new_inner = jnp.sum(equation_mismatch * precond)
        search_vector = precond + (new_inner / inner_sum) * search_vector
        inner_sum = new_inner
    outer_boundary_complete = updated_kelvin_state[:, :, 0].reshape(-1)
    flank_temp = outer_boundary_complete[clearance_point_indices]
    clearance_abrasion_growth = usui_rate * clearance_face_pressure * jnp.exp(-usui_energy / (1.0 + jax.nn.softplus(flank_temp)))
    return (updated_kelvin_state, clearance_abrasion_growth)
```

```python
import jax
import jax.numpy as jnp
from jax import lax
from jax.experimental import pallas as pl
from jax.experimental.pallas import tpu as pltpu
from jax.sharding import PartitionSpec as P

clock_advance = 2.0
interface_warming_rate = 3.0
usui_rate = 3.0
usui_energy = 4.0
kelvin_shift_amount = 2.0

LOW = 3
HIGH = 4
NX = 32
NY = 32
NZ = 128
PX = NX + HIGH + LOW
PY = NY + 8
FIELDS = 4
TILE = 8
PAIRS = 20
VMEM_LIMIT = 48 * 1024 * 1024
f32 = jnp.float32


def shift_pairs(count):
    forward = [(i, i + 1) for i in range(count - 1)]
    backward = [(target, source) for source, target in forward]
    return forward, backward


def sublane(shape):
    return lax.broadcasted_iota(jnp.int32, shape, len(shape) - 2)


def lane(shape):
    return lax.broadcasted_iota(jnp.int32, shape, len(shape) - 1)


def pack_tile(low_sub, t_first, id_first, t_last, id_last, chip_last):
    to_low = jnp.where(low_sub < 4, t_first, pltpu.roll(id_first, 4, 0))
    to_high = jnp.where(
        low_sub >= 5,
        t_last,
        jnp.where(low_sub >= 2, pltpu.roll(id_last, 5, 0), pltpu.roll(chip_last, 2, 0)),
    )
    return to_low, to_high


def pack_kernel(t_ref, id_ref, chip_ref, xp_ref, xm_ref, low_ref, high_ref):
    sub = sublane((TILE, NZ))
    zero = jnp.zeros((TILE, NZ), f32)

    def chip_first(q):
        if q < NX:
            return chip_ref[q, 0:TILE, :].astype(f32)
        if q < NX + 3:
            return xp_ref[8 + q - NX, 0:TILE, :]
        if q in (37, 38):
            return xm_ref[6 + q - 37, 0:TILE, :]
        return zero

    def own(q, _):
        a, b = pack_tile(
            sub,
            t_ref[q, 0:TILE, :],
            id_ref[q, 0:TILE, :].astype(f32),
            t_ref[q, NY - TILE :, :],
            id_ref[q, NY - TILE :, :].astype(f32),
            chip_ref[q, NY - TILE :, :].astype(f32),
        )
        low_ref[q] = a
        high_ref[q] = b
        return 0

    lax.fori_loop(0, NX, own, 0, unroll=4)
    for k in range(HIGH):
        a, b = pack_tile(
            sub,
            xp_ref[k, 0:TILE, :],
            xp_ref[4 + k, 0:TILE, :],
            xp_ref[k, NY - TILE :, :],
            xp_ref[4 + k, NY - TILE :, :],
            xp_ref[8 + k, NY - TILE :, :] if k < 3 else zero,
        )
        low_ref[NX + k] = a
        high_ref[NX + k] = b
    for k in range(LOW):
        a, b = pack_tile(
            sub,
            xm_ref[k, 0:TILE, :],
            xm_ref[3 + k, 0:TILE, :],
            xm_ref[k, NY - TILE :, :],
            xm_ref[3 + k, NY - TILE :, :],
            xm_ref[5 + k, NY - TILE :, :] if k > 0 else zero,
        )
        low_ref[NX + HIGH + k] = a
        high_ref[NX + HIGH + k] = b
    for j in range(PAIRS):
        second = chip_first(j + PAIRS) if j + PAIRS < PX else zero
        low_ref[PX + j] = jnp.where(sub < 4, chip_first(j), pltpu.roll(second, 4, 0))


def krylov_kernel(
    ref_ref,
    grad_ref,
    store_ref,
    t_ref,
    id_ref,
    chip_ref,
    xp_ref,
    xm_ref,
    yp_ref,
    ym_ref,
    w0_ref,
    w1_ref,
    w2_ref,
    send_ref,
    tp,
    cp,
    capp,
    chp,
    ex,
    ey,
    ez,
    dinv,
):
    ix = lax.axis_index("gx")
    iy = lax.axis_index("gy")
    last_x = lax.axis_size("gx") - 1
    last_y = lax.axis_size("gy") - 1
    sub = sublane((TILE, NZ))
    one = jnp.ones((), f32)
    low_x = jnp.where(ix > 0, 1.0, 0.0).astype(f32)
    high_x = jnp.where(ix < last_x, 1.0, 0.0).astype(f32)
    low_y = jnp.where(iy > 0, 1.0, 0.0).astype(f32)
    high_y = jnp.where(iy < last_y, 1.0, 0.0).astype(f32)
    rows_halo = jnp.where(sub < 4, high_y, low_y)

    def pick(ident, table):
        low = jnp.where(ident == 1, table[1], table[0])
        high = jnp.where(ident == 3, table[3], table[2])
        return jnp.where(ident >= 2, high, low)

    def element(temp, ident):
        conduct = pick(ident, ref_ref) * (
            1.0 + pick(ident, grad_ref) * jnp.tanh(temp - kelvin_shift_amount)
        )
        return conduct, pick(ident, store_ref)

    rate = clock_advance * interface_warming_rate

    def halo_tile(q, chip_high):
        low = ym_ref[q]
        high = yp_ref[q]
        temp = jnp.where(sub < 4, high, low)
        ident = jnp.where(sub < 4, pltpu.roll(high, 4, 0), pltpu.roll(low, 3, 0))
        chip = jnp.where(sub < 4, chip_high, pltpu.roll(low, 6, 0))
        return temp, ident, chip

    def put_halo(q, chip_high, plane_in):
        temp, ident, chip = halo_tile(q, chip_high)
        conduct, store = element(temp, ident)
        tp[q, NY:, :] = temp
        cp[q, NY:, :] = conduct * (rows_halo * plane_in)
        capp[q, NY:, :] = store
        chp[q, NY:, :] = rate * chip

    def own_plane(q, _):
        temp = t_ref[q]
        conduct, store = element(temp, id_ref[q])
        tp[q, :NY, :] = temp
        cp[q, :NY, :] = conduct
        capp[q, :NY, :] = store
        chp[q, :NY, :] = rate * chip_ref[q].astype(f32)
        return 0

    lax.fori_loop(0, NX, own_plane, 0, unroll=2)

    def own_halo_first(q, _):
        put_halo(q, yp_ref[PX + q], one)
        return 0

    def own_halo_second(q, _):
        put_halo(q, pltpu.roll(yp_ref[PX + q - PAIRS], 4, 0), one)
        return 0

    lax.fori_loop(0, PAIRS, own_halo_first, 0, unroll=4)
    lax.fori_loop(PAIRS, NX, own_halo_second, 0, unroll=4)

    zero_plane = jnp.zeros((NY, NZ), f32)

    def side_plane(q, temp, ident, chip, plane_in):
        conduct, store = element(temp, ident)
        tp[q, :NY, :] = temp
        cp[q, :NY, :] = conduct * plane_in
        capp[q, :NY, :] = store
        chp[q, :NY, :] = rate * chip
        put_halo(q, pltpu.roll(yp_ref[PX + q - PAIRS], 4, 0), plane_in)

    for k in range(HIGH):
        side_plane(
            NX + k, xp_ref[k], xp_ref[4 + k], xp_ref[8 + k] if k < 3 else zero_plane, high_x
        )
    for k in range(LOW):
        side_plane(
            NX + HIGH + k,
            xm_ref[k],
            xm_ref[3 + k],
            xm_ref[5 + k] if k > 0 else zero_plane,
            low_x,
        )

    lanes = lane((PY, NZ))
    subs = sublane((PY, NZ))
    inner_z = jnp.where(lanes < NZ - 1, 1.0, 0.0).astype(f32)
    edge_z = jnp.where((lanes == 0) | (lanes == NZ - 1), 1.0, 0.0).astype(f32)
    rows_in = jnp.where(subs < NY, 1.0, jnp.where(subs < NY + 4, high_y, low_y)).astype(f32)
    lane_tile = lane((TILE, NZ))

    def up_y(v):
        return pltpu.roll(v, PY - 1, 0)

    def down_y(v):
        return pltpu.roll(v, 1, 0)

    def up_z(v):
        return pltpu.roll(v, NZ - 1, 1)

    def down_z(v):
        return pltpu.roll(v, 1, 1)

    def fold(v):
        return (v[0:8] + v[8:16]) + (v[16:24] + v[24:32])

    def surface(acc, plane, x):
        for t in range(NY // TILE):
            part = plane[TILE * t : TILE * (t + 1)]
            acc = jnp.where(
                lane_tile == x * 4 + t, jnp.broadcast_to(part[:, 0:1], (TILE, NZ)), acc
            )
        return acc

    def faces(q, nxt, ex_before, fx_before, plane_in):
        c0 = cp[q]
        t0 = tp[q]
        e_x = c0 + cp[nxt]
        f_x = e_x * (tp[nxt] - t0)
        e_y = c0 + up_y(c0)
        f_y = e_y * (up_y(t0) - t0)
        e_z = (c0 + up_z(c0)) * inner_z
        f_z = e_z * (up_z(t0) - t0)
        c_b = c0 * edge_z
        diag = (capp[q] + c_b) + (
            (e_x + ex_before) + ((e_y + down_y(e_y)) + (e_z + down_z(e_z)))
        )
        inverse = (rows_in * plane_in) / diag
        resid = (chp[q] - c_b * t0) + (
            (f_x - fx_before) + ((f_y - down_y(f_y)) + (f_z - down_z(f_z)))
        )
        first = resid * inverse
        ex[q] = e_x
        ey[q] = e_y
        ez[q] = e_z
        dinv[q] = inverse
        w0_ref[q] = first
        return e_x, f_x, resid, first

    zero_tile = jnp.zeros((TILE, NZ), f32)
    e_first = cp[36] + cp[37]
    carry = (e_first, e_first * (tp[37] - tp[36]))
    for q, nxt in ((37, 38), (38, 0)):
        carry = faces(q, nxt, carry[0], carry[1], low_x)[:2]

    def faces_own(q, state):
        e_b, f_b, m0, s_t, s_0 = state
        e_x, f_x, resid, first = faces(q, q + 1, e_b, f_b, one)
        m0 = m0 + fold(resid[:NY] * first[:NY])
        return e_x, f_x, m0, surface(s_t, tp[q, :NY, :], q), surface(s_0, first, q)

    e_b, f_b, m0, surf_t, surf_0 = lax.fori_loop(
        0, NX, faces_own, (carry[0], carry[1], zero_tile, zero_tile, zero_tile)
    )
    carry = (e_b, f_b)
    for q in (32, 33, 34):
        carry = faces(q, q + 1, carry[0], carry[1], high_x)[:2]

    def neighbours(src, q, nxt, g_before):
        v = src[q]
        e_x = ex[q]
        e_y = ey[q]
        e_z = ez[q]
        total = (e_x * src[nxt] + g_before) + (
            (e_y * up_y(v) + down_y(e_y * v)) + (e_z * up_z(v) + down_z(e_z * v))
        )
        return total, v, e_x * v

    def advance(src, dst, before, prologue, epilogue):
        carry = ex[before] * src[before]
        for q, nxt in prologue:
            total, _, carry = neighbours(src, q, nxt, carry)
            dst[q] = dinv[q] * total

        def step(q, state):
            g, ma, mb, surf = state
            total, v, g = neighbours(src, q, q + 1, g)
            new = dinv[q] * total
            dst[q] = new
            ma = ma + fold(total[:NY] * v[:NY])
            mb = mb + fold(total[:NY] * new[:NY])
            return g, ma, mb, surface(surf, new, q)

        carry, ma, mb, surf = lax.fori_loop(
            0, NX, step, (carry, zero_tile, zero_tile, zero_tile)
        )
        for q, nxt in epilogue:
            total, _, carry = neighbours(src, q, nxt, carry)
            dst[q] = dinv[q] * total
        return ma, mb, surf

    m1, m2, surf_1 = advance(w0_ref, w1_ref, 37, ((38, 0),), ((32, 33), (33, 34)))
    m3, m4, surf_2 = advance(w1_ref, w2_ref, 38, (), ((32, 33),))

    def last(q, acc):
        v = w2_ref[q]
        half = ex[q] * w2_ref[q + 1] + (ey[q] * up_y(v) + ez[q] * up_z(v))
        return acc + fold(half[:NY] * v[:NY])

    m5 = lax.fori_loop(0, NX, last, zero_tile)
    m5 = m5 + m5

    moments = zero_tile
    for k, m in enumerate((m0, m1, m2, m3, m4, m5)):
        moments = jnp.where(sub == k, jnp.sum(m, axis=0, keepdims=True), moments)
    for k in range(send_ref.shape[0]):
        for j, tile in enumerate((surf_t, surf_0, surf_1, surf_2, moments)):
            send_ref[k, TILE * j : TILE * (j + 1), :] = tile


def lookup_kernel(site_ref, table_ref, out_ref, row_s, lane_s):
    iy = lax.axis_index("gy")
    blocks = table_ref.shape[0]
    targets = site_ref.shape[0]
    width = NY * lax.axis_size("gy")
    group = 4

    def places(b, _):
        site = site_ref[b]
        row = site // width
        col = site - row * width
        here = (col // NY) == iy
        x = row % NX
        y = col % NY
        place = (row // NX) * TILE + y % TILE
        row_s[b] = jnp.where(here, place, -1)
        lane_s[b] = x * 4 + y // TILE
        return 0

    lax.fori_loop(0, targets, places, 0)

    zero = jnp.zeros((TILE, NZ), f32)

    def one_group(g, _):
        rows = [row_s[g * group + i] for i in range(group)]
        lanes = [lane_s[g * group + i] for i in range(group)]

        def one_block(a, acc):
            acc = list(acc)
            for s in range(TILE):
                r = a * TILE + s
                hit = [rows[i] == r for i in range(group)]
                for f in range(FIELDS):
                    line = jnp.broadcast_to(
                        table_ref[a, TILE * f + s : TILE * f + s + 1, :], (TILE, NZ)
                    )
                    for i in range(group):
                        got = jnp.take_along_axis(line, lanes[i], axis=1)
                        acc[f * group + i] = jnp.where(hit[i], got, acc[f * group + i])
            return tuple(acc)

        acc = lax.fori_loop(0, blocks, one_block, tuple([zero] * (FIELDS * group)))
        for i in range(group):
            for f in range(FIELDS):
                out_ref[g * group + i, TILE * f : TILE * (f + 1), :] = acc[f * group + i]
        return 0

    lax.fori_loop(0, targets // group, one_group, 0)

    def add(a, acc):
        return acc + table_ref[a, TILE * FIELDS :, :]

    total = lax.fori_loop(0, blocks, add, zero)
    for b in range(targets):
        out_ref[b, TILE * FIELDS :, :] = total


def cg_coefficients(m):
    a = [m[j] - m[j + 1] for j in range(5)]

    def quadratic(v, h):
        total = None
        for i in range(3):
            for j in range(3):
                if v[i] is None or v[j] is None:
                    continue
                term = v[i] * v[j] * h[i + j]
                total = term if total is None else total + term
        return total

    def add(u, v):
        return v if u is None else u if v is None else u + v

    def scale(s, v):
        return [None if e is None else s * e for e in v]

    one = jnp.ones_like(m[0])
    z = [one, None, None]
    p = [one, None, None]
    rz = m[0]
    x = [None, None, None]
    for step in range(3):
        alpha = rz / quadratic(p, a)
        x = [add(e, g) for e, g in zip(x, scale(alpha, p))]
        if step < 2:
            ap = scale(alpha, p)
            moved = [None] + ap[:2]
            z = [
                add(add(z[i], None if ap[i] is None else -ap[i]), moved[i]) for i in range(3)
            ]
            new = quadratic(z, m)
            p = [add(z[i], e) for i, e in enumerate(scale(new / rz, p))]
            rz = new
    return x


def final_kernel(got_ref, pressure_ref, t_ref, w0_ref, w1_ref, w2_ref, temp_ref, growth_ref):
    total = got_ref[0]
    for b in range(1, got_ref.shape[0]):
        total = total + got_ref[b]
    sums = jnp.sum(total[TILE * FIELDS :], axis=1, keepdims=True)
    m = [sums[k : k + 1] for k in range(6)]
    c = cg_coefficients(m)
    c_tile = [jnp.broadcast_to(e, (TILE, NZ)) for e in c]
    c_plane = [jnp.broadcast_to(e, (NY, NZ)) for e in c]
    flank = total[0:TILE]
    for k in range(3):
        flank = flank + c_tile[k] * total[TILE * (k + 1) : TILE * (k + 2)]
    soft = jnp.maximum(flank, 0.0) + jnp.log1p(jnp.exp(-jnp.abs(flank)))
    growth_ref[...] = usui_rate * pressure_ref[...] * jnp.exp(-usui_energy / (1.0 + soft))

    def plane(q, _):
        temp_ref[q] = (
            t_ref[q]
            + c_plane[0] * w0_ref[q]
            + c_plane[1] * w1_ref[q]
            + c_plane[2] * w2_ref[q]
        )
        return 0

    lax.fori_loop(0, NX, plane, 0, unroll=2)


def local(
    prior_kelvin_state,
    substance_identifier,
    chip_touch_indicator,
    substance_reference_diffusivity,
    substance_diffusivity_gradient,
    substance_storage_coefficient,
    clearance_point_indices,
    clearance_face_pressure,
):
    size_x = lax.axis_size("gx")
    size_y = lax.axis_size("gy")
    temp, ident, chip = prior_kelvin_state, substance_identifier, chip_touch_indicator
    vmem = pl.BlockSpec(memory_space=pltpu.VMEM)
    smem = pl.BlockSpec(memory_space=pltpu.SMEM)
    params = pltpu.CompilerParams(vmem_limit_bytes=VMEM_LIMIT)

    sites = lax.all_gather(clearance_point_indices, "gy")
    sites = sites.reshape(size_y, TILE, NZ)

    forward, backward = shift_pairs(size_x)
    to_low = jnp.concatenate(
        [temp[:HIGH], ident[:HIGH].astype(f32), chip[: HIGH - 1].astype(f32)], axis=0
    )
    to_high = jnp.concatenate(
        [temp[NX - LOW :], ident[NX - LOW :].astype(f32), chip[NX - LOW + 1 :].astype(f32)],
        axis=0,
    )
    xp = lax.ppermute(to_low, "gx", backward)
    xm = lax.ppermute(to_high, "gx", forward)

    low_rows, high_rows = pl.pallas_call(
        pack_kernel,
        name="pack_rows",
        in_specs=[vmem] * 5,
        out_specs=[vmem] * 2,
        out_shape=[
            jax.ShapeDtypeStruct((PX + PAIRS, TILE, NZ), f32),
            jax.ShapeDtypeStruct((PX, TILE, NZ), f32),
        ],
        compiler_params=params,
    )(temp, ident, chip, xp, xm)
    forward, backward = shift_pairs(size_y)
    yp = lax.ppermute(low_rows, "gy", backward)
    ym = lax.ppermute(high_rows, "gy", forward)

    padded = jax.ShapeDtypeStruct((PX, PY, NZ), f32)
    payload = TILE * (FIELDS + 1)
    w0, w1, w2, send = pl.pallas_call(
        krylov_kernel,
        name="krylov",
        in_specs=[smem] * 3 + [vmem] * 7,
        out_specs=[vmem] * 4,
        out_shape=[padded] * 3 + [jax.ShapeDtypeStruct((size_x, payload, NZ), f32)],
        scratch_shapes=[pltpu.VMEM((PX, PY, NZ), f32)] * 8,
        compiler_params=params,
    )(
        substance_reference_diffusivity,
        substance_diffusivity_gradient,
        substance_storage_coefficient,
        temp,
        ident,
        chip,
        xp,
        xm,
        yp,
        ym,
    )
    table = lax.all_to_all(send, "gx", 0, 0)
    found = pl.pallas_call(
        lookup_kernel,
        name="lookup",
        in_specs=[vmem] * 2,
        out_specs=vmem,
        out_shape=jax.ShapeDtypeStruct((size_y, payload, NZ), f32),
        scratch_shapes=[pltpu.VMEM((size_y, TILE, NZ), jnp.int32)] * 2,
        compiler_params=params,
    )(sites, table)
    got = lax.all_to_all(found, "gy", 0, 0)
    block = pl.BlockSpec((NX, NY, NZ), lambda i: (0, 0, 0))
    temperature, growth = pl.pallas_call(
        final_kernel,
        name="finish",
        grid=(1,),
        in_specs=[
            pl.BlockSpec((size_y, payload, NZ), lambda i: (0, 0, 0)),
            pl.BlockSpec((TILE, NZ), lambda i: (0, 0)),
            block,
            block,
            block,
            block,
        ],
        out_specs=[block, pl.BlockSpec((TILE, NZ), lambda i: (0, 0))],
        out_shape=[
            jax.ShapeDtypeStruct((NX, NY, NZ), f32),
            jax.ShapeDtypeStruct((TILE, NZ), f32),
        ],
        compiler_params=params,
    )(got, clearance_face_pressure.reshape(TILE, NZ), temp, w0, w1, w2)
    return temperature, growth.reshape(-1)


def solution(mesh):
    in_specs = (
        P("gx", "gy", None),
        P("gx", "gy", None),
        P("gx", "gy", None),
        P(),
        P(),
        P(),
        P(("gx", "gy")),
        P(("gx", "gy")),
    )
    out_specs = (P("gx", "gy", None), P(("gx", "gy")))
    return jax.shard_map(local, mesh=mesh, in_specs=in_specs, out_specs=out_specs, check_vma=False)
```

```python
import jax
import jax.numpy as jnp
from jax import lax
from jax.experimental import pallas as pl
from jax.experimental.pallas import tpu as pltpu
from jax.sharding import PartitionSpec as P

clock_advance = 2.0
interface_warming_rate = 3.0
usui_rate = 3.0
usui_energy = 4.0
kelvin_shift_amount = 2.0

LOW = 3
HIGH = 4
NX = 32
NY = 32
NZ = 128
PX = NX + HIGH + LOW
PY = NY + 8
FIELDS = 4
TILE = 8
PAIRS = 16
MIB = 1024 * 1024
f32 = jnp.float32
bf16 = jnp.bfloat16


def sublane(shape):
    return lax.broadcasted_iota(jnp.int32, shape, len(shape) - 2)


def lane(shape):
    return lax.broadcasted_iota(jnp.int32, shape, len(shape) - 1)


def pack_kernel(
    t_hbm,
    id_hbm,
    chip_hbm,
    x_low,
    x_high,
    y_low,
    y_high,
    low_low,
    low_high,
    high_low,
    high_high,
    t_a,
    t_b,
    i_a,
    i_b,
    c_a,
    c_b,
    t_p,
    t_m,
    i_p,
    i_m,
    c_p,
    c_m,
    sems,
):
    copies = []
    for k, (src, dst) in enumerate(
        (
            (t_hbm.at[pl.ds(0, HIGH)], t_p),
            (id_hbm.at[pl.ds(0, HIGH)], i_p),
            (chip_hbm.at[pl.ds(0, HIGH)], c_p),
            (t_hbm.at[pl.ds(NX - HIGH, HIGH)], t_m),
            (id_hbm.at[pl.ds(NX - HIGH, HIGH)], i_m),
            (chip_hbm.at[pl.ds(NX - HIGH, HIGH)], c_m),
            (t_hbm.at[:, pl.ds(0, TILE)], t_a),
            (id_hbm.at[:, pl.ds(0, TILE)], i_a),
            (chip_hbm.at[:, pl.ds(0, TILE)], c_a),
            (t_hbm.at[:, pl.ds(NY - TILE, TILE)], t_b),
            (id_hbm.at[:, pl.ds(NY - TILE, TILE)], i_b),
            (chip_hbm.at[:, pl.ds(NY - TILE, TILE)], c_b),
        )
    ):
        copies.append(pltpu.make_async_copy(src, dst, sems.at[k]))
        copies[-1].start()
    for copy in copies:
        copy.wait()

    sub = sublane((TILE, NZ))
    for k in range(HIGH):
        x_low[k] = t_p[k]
        x_low[4 + k] = i_p[k].astype(f32)
        if k < 3:
            x_low[8 + k] = c_p[k].astype(f32)
            x_high[k] = t_m[1 + k]
            x_high[3 + k] = i_m[1 + k].astype(f32)
        if k < 2:
            x_high[6 + k] = c_m[2 + k].astype(f32)

    def first_rows(q):
        return jnp.where(sub < 4, t_a[q], pltpu.roll(i_a[q].astype(f32), 4, 0))

    def last_rows(q):
        return jnp.where(
            sub >= 5,
            t_b[q],
            jnp.where(
                sub >= 2,
                pltpu.roll(i_b[q].astype(f32), 5, 0),
                pltpu.roll(c_b[q].astype(f32), 2, 0),
            ),
        )

    def own(q, _):
        y_low[q] = first_rows(q)
        y_high[q] = last_rows(q)
        return 0

    lax.fori_loop(0, NX, own, 0, unroll=8)

    def pair(j, _):
        y_low[NX + j] = jnp.where(
            sub < 4, c_a[j].astype(f32), pltpu.roll(c_a[j + PAIRS].astype(f32), 4, 0)
        )
        return 0

    lax.fori_loop(0, PAIRS, pair, 0, unroll=8)
    for k in range(HIGH):
        low_low[k] = first_rows(k)
        low_high[k] = last_rows(k)
        if k < 3:
            low_low[4 + k] = c_a[k].astype(f32)
            high_low[k] = first_rows(NX - 3 + k)
            high_high[k] = last_rows(NX - 3 + k)
        if k < 2:
            high_low[3 + k] = c_a[NX - 2 + k].astype(f32)


def pick(ident, table):
    low = jnp.where(ident == 1, table[1], table[0])
    high = jnp.where(ident == 3, table[3], table[2])
    return jnp.where(ident >= 2, high, low)


def element(temp, ident, ref_ref, grad_ref, store_ref):
    conduct = pick(ident, ref_ref) * (
        1.0 + pick(ident, grad_ref) * jnp.tanh(temp - kelvin_shift_amount)
    )
    return conduct, pick(ident, store_ref)


def own_kernel(ref_ref, grad_ref, store_ref, t_ref, id_ref, chip_ref, tp, cp, capp, chp):
    def own_plane(q, _):
        temp = t_ref[q]
        conduct, store = element(temp, id_ref[q], ref_ref, grad_ref, store_ref)
        tp[q, :NY, :] = temp
        cp[q, :NY, :] = conduct
        capp[q, :NY, :] = store
        chp[q, :NY, :] = clock_advance * interface_warming_rate * chip_ref[q].astype(f32)
        return 0

    lax.fori_loop(0, NX, own_plane, 0, unroll=4)


def krylov_kernel(
    ref_ref,
    grad_ref,
    store_ref,
    tp_in,
    cp_in,
    capp_in,
    chp_in,
    xp_ref,
    xm_ref,
    yp_ref,
    ym_ref,
    pp_ref,
    pm_ref,
    mp_ref,
    mm_ref,
    tp,
    cp,
    capp,
    chp,
    w0_ref,
    w1_ref,
    w2_ref,
    send_ref,
    ex,
    ey,
    ez,
    dinv,
):
    del tp_in, cp_in, capp_in, chp_in
    ix = lax.axis_index("gx")
    iy = lax.axis_index("gy")
    last_x = lax.axis_size("gx") - 1
    last_y = lax.axis_size("gy") - 1
    sub = sublane((TILE, NZ))
    one = jnp.ones((), f32)
    low_x = jnp.where(ix > 0, 1.0, 0.0).astype(f32)
    high_x = jnp.where(ix < last_x, 1.0, 0.0).astype(f32)
    low_y = jnp.where(iy > 0, 1.0, 0.0).astype(f32)
    high_y = jnp.where(iy < last_y, 1.0, 0.0).astype(f32)
    rows_halo = jnp.where(sub < 4, high_y, low_y)
    rate = clock_advance * interface_warming_rate

    def put_halo(q, high, low, chip_high, plane_in):
        temp = jnp.where(sub < 4, high, low)
        ident = jnp.where(sub < 4, pltpu.roll(high, 4, 0), pltpu.roll(low, 3, 0))
        chip = jnp.where(sub < 4, chip_high, pltpu.roll(low, 6, 0))
        conduct, store = element(temp, ident, ref_ref, grad_ref, store_ref)
        tp[q, NY:, :] = temp
        cp[q, NY:, :] = conduct * (rows_halo * plane_in)
        capp[q, NY:, :] = store
        chp[q, NY:, :] = rate * chip

    def own_halo(j, _):
        chips = yp_ref[NX + j]
        put_halo(j, yp_ref[j], ym_ref[j], chips, one)
        q = j + PAIRS
        put_halo(q, yp_ref[q], ym_ref[q], pltpu.roll(chips, 4, 0), one)
        return 0

    lax.fori_loop(0, PAIRS, own_halo, 0, unroll=4)

    zero_plane = jnp.zeros((NY, NZ), f32)
    zero_tile = jnp.zeros((TILE, NZ), f32)

    def side_plane(q, temp, ident, chip, high, low, chip_high, plane_in):
        conduct, store = element(temp, ident, ref_ref, grad_ref, store_ref)
        tp[q, :NY, :] = temp
        cp[q, :NY, :] = conduct * plane_in
        capp[q, :NY, :] = store
        chp[q, :NY, :] = rate * chip
        put_halo(q, high, low, chip_high, plane_in)

    for k in range(HIGH):
        side_plane(
            NX + k,
            xp_ref[k],
            xp_ref[4 + k],
            xp_ref[8 + k] if k < 3 else zero_plane,
            pp_ref[k],
            pm_ref[k],
            pp_ref[4 + k] if k < 3 else zero_tile,
            high_x,
        )
    for k in range(LOW):
        side_plane(
            NX + HIGH + k,
            xm_ref[k],
            xm_ref[3 + k],
            xm_ref[5 + k] if k > 0 else zero_plane,
            mp_ref[k],
            mm_ref[k],
            mp_ref[2 + k] if k > 0 else zero_tile,
            low_x,
        )

    lanes = lane((PY, NZ))
    subs = sublane((PY, NZ))
    inner_z = jnp.where(lanes < NZ - 1, 1.0, 0.0).astype(f32)
    edge_z = jnp.where((lanes == 0) | (lanes == NZ - 1), 1.0, 0.0).astype(f32)
    rows_in = jnp.where(subs < NY, 1.0, jnp.where(subs < NY + 4, high_y, low_y)).astype(f32)
    lane_tile = lane((TILE, NZ))

    def up_y(v):
        return pltpu.roll(v, PY - 1, 0)

    def down_y(v):
        return pltpu.roll(v, 1, 0)

    def up_z(v):
        return pltpu.roll(v, NZ - 1, 1)

    def down_z(v):
        return pltpu.roll(v, 1, 1)

    def fold(v):
        return (v[0:8] + v[8:16]) + (v[16:24] + v[24:32])

    def surface(acc, plane, x):
        for t in range(NY // TILE):
            part = plane[TILE * t : TILE * (t + 1)]
            acc = jnp.where(
                lane_tile == x * 4 + t, jnp.broadcast_to(part[:, 0:1], (TILE, NZ)), acc
            )
        return acc

    def faces(q, nxt, ex_before, fx_before, plane_in):
        c0 = cp[q]
        t0 = tp[q]
        e_x = c0 + cp[nxt]
        f_x = e_x * (tp[nxt] - t0)
        e_y = c0 + up_y(c0)
        f_y = e_y * (up_y(t0) - t0)
        e_z = (c0 + up_z(c0)) * inner_z
        f_z = e_z * (up_z(t0) - t0)
        c_b = c0 * edge_z
        diag = (capp[q] + c_b) + (
            (e_x + ex_before) + ((e_y + down_y(e_y)) + (e_z + down_z(e_z)))
        )
        inverse = (rows_in * plane_in) / diag
        resid = (chp[q] - c_b * t0) + (
            (f_x - fx_before) + ((f_y - down_y(f_y)) + (f_z - down_z(f_z)))
        )
        first = resid * inverse
        ex[q] = e_x
        ey[q] = e_y
        ez[q] = e_z
        dinv[q] = inverse
        w0_ref[q] = first
        return e_x, f_x, resid, first

    e_first = cp[36] + cp[37]
    carry = (e_first, e_first * (tp[37] - tp[36]))
    for q, nxt in ((37, 38), (38, 0)):
        carry = faces(q, nxt, carry[0], carry[1], low_x)[:2]

    def faces_own(q, state):
        e_b, f_b, m0, s_t, s_0 = state
        e_x, f_x, resid, first = faces(q, q + 1, e_b, f_b, one)
        m0 = m0 + fold(resid[:NY] * first[:NY])
        return e_x, f_x, m0, surface(s_t, tp[q, :NY, :], q), surface(s_0, first, q)

    e_b, f_b, m0, surf_t, surf_0 = lax.fori_loop(
        0, NX, faces_own, (carry[0], carry[1], zero_tile, zero_tile, zero_tile), unroll=8
    )
    carry = (e_b, f_b)
    for q in (32, 33, 34):
        carry = faces(q, q + 1, carry[0], carry[1], high_x)[:2]

    def neighbours(src, q, nxt, g_before):
        v = src[q]
        e_x = ex[q]
        e_y = ey[q]
        e_z = ez[q]
        total = (e_x * src[nxt] + g_before) + (
            (e_y * up_y(v) + down_y(e_y * v)) + (e_z * up_z(v) + down_z(e_z * v))
        )
        return total, v, e_x * v

    def advance(src, dst, before, prologue, epilogue):
        carry = ex[before] * src[before]
        for q, nxt in prologue:
            total, _, carry = neighbours(src, q, nxt, carry)
            dst[q] = dinv[q] * total

        def step(q, state):
            g, ma, mb, surf = state
            total, v, g = neighbours(src, q, q + 1, g)
            new = dinv[q] * total
            dst[q] = new
            ma = ma + fold(total[:NY] * v[:NY])
            mb = mb + fold(total[:NY] * new[:NY])
            return g, ma, mb, surface(surf, new, q)

        carry, ma, mb, surf = lax.fori_loop(
            0, NX, step, (carry, zero_tile, zero_tile, zero_tile), unroll=8
        )
        for q, nxt in epilogue:
            total, _, carry = neighbours(src, q, nxt, carry)
            dst[q] = dinv[q] * total
        return ma, mb, surf

    m1, m2, surf_1 = advance(w0_ref, w1_ref, 37, ((38, 0),), ((32, 33), (33, 34)))
    m3, m4, surf_2 = advance(w1_ref, w2_ref, 38, (), ((32, 33),))

    def last(q, acc):
        v = w2_ref[q]
        half = ex[q] * w2_ref[q + 1] + (ey[q] * up_y(v) + ez[q] * up_z(v))
        return acc + fold(half[:NY] * v[:NY])

    m5 = lax.fori_loop(0, NX, last, zero_tile, unroll=8)
    m5 = m5 + m5

    moments = zero_tile
    for k, m in enumerate((m0, m1, m2, m3, m4, m5)):
        moments = jnp.where(sub == k, jnp.sum(m, axis=0, keepdims=True), moments)
    for k in range(send_ref.shape[0]):
        for j, tile in enumerate((surf_t, surf_0, surf_1, surf_2, moments)):
            send_ref[k, TILE * j : TILE * (j + 1), :] = tile


def lookup_kernel(site_hbm, table_ref, out_ref, parts, site_ref, sem):
    copy = pltpu.make_async_copy(site_hbm.at[:, pl.ds(0, TILE)], site_ref, sem)
    copy.start()
    blocks = table_ref.shape[0]
    targets = site_ref.shape[0]
    iy = lax.axis_index("gy")
    width = NY * lax.axis_size("gy")
    sub = sublane((TILE, NZ))
    subs = sublane((NZ, NZ))
    zero = jnp.zeros((TILE, NZ), f32)
    fields = FIELDS - 1
    for f in range(fields):
        rest = jnp.concatenate(
            [table_ref[a, TILE * (f + 1) : TILE * (f + 2), :] for a in range(blocks)], axis=0
        ).T
        for k in range(2):
            part = rest.astype(bf16)
            parts[NZ * f : NZ * (f + 1), NZ * k : NZ * (k + 1)] = part
            rest = rest - part.astype(f32)

    total = table_ref[0, TILE * FIELDS :, :]
    for a in range(1, blocks):
        total = total + table_ref[a, TILE * FIELDS :, :]
    copy.wait()

    def one(b, _):
        site = site_ref[b]
        row = site // width
        col = site - row * width
        here = (col // NY) == iy
        y = col % NY
        row_of = jnp.where(here, (row // NX) * TILE + y % TILE, -1)
        lane_of = (row % NX) * (NY // TILE) + y // TILE
        hot = jnp.concatenate(
            [
                jnp.where(
                    subs == jnp.broadcast_to(row_of[s : s + 1], (NZ, NZ)), 1.0, 0.0
                ).astype(bf16)
                for s in range(TILE)
            ],
            axis=1,
        )
        hot = jnp.concatenate([hot, hot], axis=0)
        found = [zero] * FIELDS
        lines = [
            jnp.dot(parts[NZ * f : NZ * (f + 1)], hot, preferred_element_type=f32)
            for f in range(fields)
        ]
        for s in range(TILE):
            lanes = jnp.broadcast_to(lane_of[s : s + 1], (TILE, NZ))
            rows = jnp.broadcast_to(row_of[s : s + 1], (TILE, NZ)) - sub
            acc = [zero] * FIELDS
            for a in range(blocks):
                got = jnp.take_along_axis(table_ref[a, 0:TILE, :], lanes, axis=1)
                acc[0] = jnp.where(rows == a * TILE, got, acc[0])
            lanes = lanes - sub
            for t in range(NZ // TILE):
                hit = lanes == t * TILE
                for f in range(fields):
                    acc[f + 1] = jnp.where(
                        hit,
                        lines[f][TILE * t : TILE * (t + 1), NZ * s : NZ * (s + 1)],
                        acc[f + 1],
                    )
            for f in range(FIELDS):
                found[f] = jnp.where(sub == s, jnp.sum(acc[f], axis=0, keepdims=True), found[f])
        for f in range(FIELDS):
            out_ref[b, TILE * f : TILE * (f + 1), :] = found[f]
        out_ref[b, TILE * FIELDS :, :] = total
        return 0

    lax.fori_loop(0, targets, one, 0, unroll=2)


def cg_coefficients(m):
    a = [m[j] - m[j + 1] for j in range(5)]

    def quadratic(v, h):
        total = None
        for i in range(3):
            for j in range(3):
                if v[i] is None or v[j] is None:
                    continue
                term = v[i] * v[j] * h[i + j]
                total = term if total is None else total + term
        return total

    def add(u, v):
        return v if u is None else u if v is None else u + v

    def scale(s, v):
        return [None if e is None else s * e for e in v]

    one = jnp.ones_like(m[0])
    z = [one, None, None]
    p = [one, None, None]
    rz = m[0]
    x = [None, None, None]
    for step in range(3):
        alpha = rz / quadratic(p, a)
        x = [add(e, g) for e, g in zip(x, scale(alpha, p))]
        if step < 2:
            ap = scale(alpha, p)
            moved = [None] + ap[:2]
            z = [
                add(add(z[i], None if ap[i] is None else -ap[i]), moved[i]) for i in range(3)
            ]
            new = quadratic(z, m)
            p = [add(z[i], e) for i, e in enumerate(scale(new / rz, p))]
            rz = new
    return x


def final_kernel(
    got_ref, pressure_hbm, t_ref, w0_ref, w1_ref, w2_ref, temp_ref, growth_ref, pressure_ref, sem
):
    copy = pltpu.make_async_copy(pressure_hbm, pressure_ref, sem)
    copy.start()
    total = got_ref[0]
    for b in range(1, got_ref.shape[0]):
        total = total + got_ref[b]
    sums = jnp.sum(total[TILE * FIELDS :], axis=1, keepdims=True)
    m = [sums[k : k + 1] for k in range(6)]
    c = cg_coefficients(m)
    c_tile = [jnp.broadcast_to(e, (TILE, NZ)) for e in c]
    c_plane = [jnp.broadcast_to(e, (NY, NZ)) for e in c]
    flank = total[0:TILE]
    for k in range(3):
        flank = flank + c_tile[k] * total[TILE * (k + 1) : TILE * (k + 2)]
    soft = jnp.maximum(flank, 0.0) + jnp.log1p(jnp.exp(-jnp.abs(flank)))
    copy.wait()
    growth_ref[...] = usui_rate * pressure_ref[...] * jnp.exp(-usui_energy / (1.0 + soft))

    def plane(q, _):
        temp_ref[q] = (
            t_ref[q, :NY, :]
            + c_plane[0] * w0_ref[q, :NY, :]
            + c_plane[1] * w1_ref[q, :NY, :]
            + c_plane[2] * w2_ref[q, :NY, :]
        )
        return 0

    lax.fori_loop(0, NX, plane, 0, unroll=2)


def local(
    prior_kelvin_state,
    substance_identifier,
    chip_touch_indicator,
    substance_reference_diffusivity,
    substance_diffusivity_gradient,
    substance_storage_coefficient,
    clearance_point_indices,
    clearance_face_pressure,
):
    size_x = lax.axis_size("gx")
    size_y = lax.axis_size("gy")
    temp, ident, chip = prior_kelvin_state, substance_identifier, chip_touch_indicator
    vmem = pl.BlockSpec(memory_space=pltpu.VMEM)
    smem = pl.BlockSpec(memory_space=pltpu.SMEM)

    def params(mib):
        return pltpu.CompilerParams(vmem_limit_bytes=mib * MIB)


    sites = jnp.pad(clearance_point_indices.reshape(TILE, NZ), ((0, NZ - TILE), (0, 0)))
    sites = lax.all_gather(sites, "gy")

    anywhere = pl.BlockSpec(memory_space=pltpu.HBM)

    def arr(*shape, dtype=f32):
        return jax.ShapeDtypeStruct(shape, dtype)

    def buf(*shape, dtype=f32):
        return pltpu.VMEM(shape, dtype)

    def in_hbm(*arrays):
        return [pltpu.with_memory_space_constraint(a, pltpu.HBM) for a in arrays]

    i32 = jnp.int32
    packed = pl.pallas_call(
        pack_kernel,
        name="pack",
        in_specs=[anywhere] * 3,
        out_specs=[vmem] * 8,
        out_shape=[
            arr(11, NY, NZ),
            arr(8, NY, NZ),
            arr(NX + PAIRS, TILE, NZ),
            arr(NX, TILE, NZ),
            arr(7, TILE, NZ),
            arr(4, TILE, NZ),
            arr(5, TILE, NZ),
            arr(3, TILE, NZ),
        ],
        scratch_shapes=[
            buf(NX, TILE, NZ),
            buf(NX, TILE, NZ),
            buf(NX, TILE, NZ, dtype=i32),
            buf(NX, TILE, NZ, dtype=i32),
            buf(NX, TILE, NZ, dtype=i32),
            buf(NX, TILE, NZ, dtype=i32),
            buf(HIGH, NY, NZ),
            buf(HIGH, NY, NZ),
            buf(HIGH, NY, NZ, dtype=i32),
            buf(HIGH, NY, NZ, dtype=i32),
            buf(HIGH, NY, NZ, dtype=i32),
            buf(HIGH, NY, NZ, dtype=i32),
            pltpu.SemaphoreType.DMA((12,)),
        ],
        compiler_params=params(10),
    )(*in_hbm(temp, ident, chip))

    def shift(block, dx, dy):
        pairs = [
            (i * size_y + j, (i + dx) * size_y + j + dy)
            for i in range(size_x)
            for j in range(size_y)
            if 0 <= i + dx < size_x and 0 <= j + dy < size_y
        ]
        return lax.ppermute(block, ("gx", "gy"), pairs)

    moves = ((-1, 0), (1, 0), (0, -1), (0, 1), (-1, -1), (-1, 1), (1, -1), (1, 1))
    halos = [shift(block, dx, dy) for block, (dx, dy) in zip(packed, moves)]

    tables = (
        substance_reference_diffusivity,
        substance_diffusivity_gradient,
        substance_storage_coefficient,
    )
    padded = arr(PX, PY, NZ)
    own = pl.pallas_call(
        own_kernel,
        name="own_cells",
        in_specs=[smem] * 3 + [vmem] * 3,
        out_specs=[vmem] * 4,
        out_shape=[padded] * 4,
        compiler_params=params(12),
    )(*tables, temp, ident, chip)

    payload = TILE * (FIELDS + 1)
    start, _, _, _, w0, w1, w2, send = pl.pallas_call(
        krylov_kernel,
        name="krylov",
        in_specs=[smem] * 3 + [vmem] * 12,
        out_specs=[vmem] * 8,
        out_shape=[padded] * 7 + [arr(size_x, payload, NZ)],
        input_output_aliases={3: 0, 4: 1, 5: 2, 6: 3},
        scratch_shapes=[buf(PX, PY, NZ)] * 4,
        compiler_params=params(24),
    )(*tables, *own, *halos)
    table = lax.all_to_all(send, "gx", 0, 0)
    found = pl.pallas_call(
        lookup_kernel,
        name="lookup",
        in_specs=[anywhere, vmem],
        out_specs=vmem,
        out_shape=arr(size_y, payload, NZ),
        scratch_shapes=[
            buf(NZ * (FIELDS - 1), 2 * NZ, dtype=bf16),
            buf(size_y, TILE, NZ, dtype=i32),
            pltpu.SemaphoreType.DMA(()),
        ],
        compiler_params=params(20),
    )(*in_hbm(sites), table)
    got = lax.all_to_all(found, "gy", 0, 0)
    temperature, growth = pl.pallas_call(
        final_kernel,
        name="finish",
        in_specs=[vmem, anywhere, vmem, vmem, vmem, vmem],
        out_specs=[vmem] * 2,
        out_shape=[arr(NX, NY, NZ), arr(TILE, NZ)],
        scratch_shapes=[buf(TILE, NZ), pltpu.SemaphoreType.DMA(())],
        compiler_params=params(12),
    )(got, *in_hbm(clearance_face_pressure.reshape(TILE, NZ)), start, w0, w1, w2)
    return temperature, growth.reshape(-1)


def solution(mesh):
    in_specs = (
        P("gx", "gy", None),
        P("gx", "gy", None),
        P("gx", "gy", None),
        P(),
        P(),
        P(),
        P(("gx", "gy")),
        P(("gx", "gy")),
    )
    out_specs = (P("gx", "gy", None), P(("gx", "gy")))
    return jax.shard_map(local, mesh=mesh, in_specs=in_specs, out_specs=out_specs, check_vma=False)
```

```python
import jax
import jax.numpy as jnp
from jax import lax
from jax.experimental import pallas as pl
from jax.experimental.pallas import tpu as pltpu
from jax.sharding import PartitionSpec as P

clock_advance = 2.0
interface_warming_rate = 3.0
usui_rate = 3.0
usui_energy = 4.0
kelvin_shift_amount = 2.0

LOW = 3
HIGH = 4
NX = 32
NY = 32
NZ = 128
PX = NX + HIGH + LOW
PY = NY + 8
FIELDS = 4
TILE = 8
PAIRS = 20
MIB = 1024 * 1024
f32 = jnp.float32
bf16 = jnp.bfloat16


def shift_pairs(count):
    up = [(i, i + 1) for i in range(count - 1)]
    return up, [(target, source) for source, target in up]


def sublane(shape):
    return lax.broadcasted_iota(jnp.int32, shape, len(shape) - 2)


def lane(shape):
    return lax.broadcasted_iota(jnp.int32, shape, len(shape) - 1)


def first_tile(sub, temp, ident):
    return jnp.where(sub < 4, temp, pltpu.roll(ident, 4, 0))


def last_tile(sub, temp, ident, chip):
    return jnp.where(
        sub >= 5, temp, jnp.where(sub >= 2, pltpu.roll(ident, 5, 0), pltpu.roll(chip, 2, 0))
    )


def pack_kernel(
    t_hbm,
    id_hbm,
    chip_hbm,
    site_hbm,
    x_low,
    x_high,
    y_low,
    y_high,
    sites,
    t_a,
    t_b,
    i_a,
    i_b,
    c_a,
    c_b,
    t_p,
    t_m,
    i_p,
    i_m,
    c_p,
    c_m,
    site_ref,
    sems,
):
    copies = []
    for k, (src, dst) in enumerate(
        (
            (t_hbm.at[pl.ds(0, HIGH)], t_p),
            (id_hbm.at[pl.ds(0, HIGH)], i_p),
            (chip_hbm.at[pl.ds(0, HIGH)], c_p),
            (t_hbm.at[pl.ds(NX - HIGH, HIGH)], t_m),
            (id_hbm.at[pl.ds(NX - HIGH, HIGH)], i_m),
            (chip_hbm.at[pl.ds(NX - HIGH, HIGH)], c_m),
            (t_hbm.at[:, pl.ds(0, TILE)], t_a),
            (id_hbm.at[:, pl.ds(0, TILE)], i_a),
            (chip_hbm.at[:, pl.ds(0, TILE)], c_a),
            (t_hbm.at[:, pl.ds(NY - TILE, TILE)], t_b),
            (id_hbm.at[:, pl.ds(NY - TILE, TILE)], i_b),
            (chip_hbm.at[:, pl.ds(NY - TILE, TILE)], c_b),
            (site_hbm, site_ref),
        )
    ):
        copies.append(pltpu.make_async_copy(src, dst, sems.at[k]))
        copies[-1].start()
    for copy in copies:
        copy.wait()

    sub = sublane((TILE, NZ))
    for k in range(HIGH):
        x_low[k] = t_p[k]
        x_low[4 + k] = i_p[k].astype(f32)
        if k < 3:
            x_low[8 + k] = c_p[k].astype(f32)
            x_high[k] = t_m[1 + k]
            x_high[3 + k] = i_m[1 + k].astype(f32)
        if k < 2:
            x_high[6 + k] = c_m[2 + k].astype(f32)

    def own(q, _):
        y_low[q] = first_tile(sub, t_a[q], i_a[q].astype(f32))
        y_high[q] = last_tile(sub, t_b[q], i_b[q].astype(f32), c_b[q].astype(f32))
        return 0

    lax.fori_loop(0, NX, own, 0, unroll=8)
    for j in range(PAIRS):
        tile = c_a[j].astype(f32)
        if j + PAIRS < NX:
            tile = jnp.where(sub < 4, tile, pltpu.roll(c_a[j + PAIRS].astype(f32), 4, 0))
        y_low[PX + j] = tile
    for k in range(sites.shape[0]):
        sites[k] = site_ref[...]


def corner_kernel(low_in, high_in, xp_ref, xm_ref, sites_in, y_low, y_high, sites_out):
    del low_in, high_in, sites_in, sites_out
    sub = sublane((TILE, NZ))
    zero = jnp.zeros((TILE, NZ), f32)
    last = pl.ds(NY - TILE, TILE)
    first = pl.ds(0, TILE)
    for k in range(HIGH + LOW):
        q = NX + k
        if k < HIGH:
            temp, ident, chip = xp_ref.at[k], xp_ref.at[4 + k], xp_ref.at[8 + k] if k < 3 else None
        else:
            j = k - HIGH
            temp, ident, chip = xm_ref.at[j], xm_ref.at[3 + j], xm_ref.at[5 + j] if j else None
        y_low[q] = first_tile(sub, temp[first, :], ident[first, :])
        y_high[q] = last_tile(
            sub, temp[last, :], ident[last, :], zero if chip is None else chip[last, :]
        )
        if chip is not None:
            tile = y_low[PX + q - PAIRS]
            y_low[PX + q - PAIRS] = jnp.where(sub < 4, tile, pltpu.roll(chip[first, :], 4, 0))


def pick(ident, table):
    low = jnp.where(ident == 1, table[1], table[0])
    high = jnp.where(ident == 3, table[3], table[2])
    return jnp.where(ident >= 2, high, low)


def element(temp, ident, ref_ref, grad_ref, store_ref):
    conduct = pick(ident, ref_ref) * (
        1.0 + pick(ident, grad_ref) * jnp.tanh(temp - kelvin_shift_amount)
    )
    return conduct, pick(ident, store_ref)


def own_kernel(
    ref_ref, grad_ref, store_ref, t_ref, id_ref, chip_ref, sites_in, tp, cp, capp, chp, sites_out
):
    del sites_in, sites_out

    def own_plane(q, _):
        temp = t_ref[q]
        conduct, store = element(temp, id_ref[q], ref_ref, grad_ref, store_ref)
        tp[q, :NY, :] = temp
        cp[q, :NY, :] = conduct
        capp[q, :NY, :] = store
        chp[q, :NY, :] = clock_advance * interface_warming_rate * chip_ref[q].astype(f32)
        return 0

    lax.fori_loop(0, NX, own_plane, 0, unroll=4)


def krylov_kernel(
    ref_ref,
    grad_ref,
    store_ref,
    tp_in,
    cp_in,
    capp_in,
    chp_in,
    xp_ref,
    xm_ref,
    yp_ref,
    ym_ref,
    tp,
    cp,
    capp,
    chp,
    w0_ref,
    w1_ref,
    w2_ref,
    send_ref,
    ex,
    ey,
    ez,
    dinv,
):
    del tp_in, cp_in, capp_in, chp_in
    ix = lax.axis_index("gx")
    iy = lax.axis_index("gy")
    last_x = lax.axis_size("gx") - 1
    last_y = lax.axis_size("gy") - 1
    sub = sublane((TILE, NZ))
    one = jnp.ones((), f32)
    low_x = jnp.where(ix > 0, 1.0, 0.0).astype(f32)
    high_x = jnp.where(ix < last_x, 1.0, 0.0).astype(f32)
    low_y = jnp.where(iy > 0, 1.0, 0.0).astype(f32)
    high_y = jnp.where(iy < last_y, 1.0, 0.0).astype(f32)
    rows_halo = jnp.where(sub < 4, high_y, low_y)
    rate = clock_advance * interface_warming_rate

    def put_halo(q, chip_high, plane_in):
        high = yp_ref[q]
        low = ym_ref[q]
        temp = jnp.where(sub < 4, high, low)
        ident = jnp.where(sub < 4, pltpu.roll(high, 4, 0), pltpu.roll(low, 3, 0))
        chip = jnp.where(sub < 4, chip_high, pltpu.roll(low, 6, 0))
        conduct, store = element(temp, ident, ref_ref, grad_ref, store_ref)
        tp[q, NY:, :] = temp
        cp[q, NY:, :] = conduct * (rows_halo * plane_in)
        capp[q, NY:, :] = store
        chp[q, NY:, :] = rate * chip

    def own_halo_first(q, _):
        put_halo(q, yp_ref[PX + q], one)
        return 0

    def own_halo_second(q, _):
        put_halo(q, pltpu.roll(yp_ref[PX + q - PAIRS], 4, 0), one)
        return 0

    lax.fori_loop(0, PAIRS, own_halo_first, 0, unroll=5)
    lax.fori_loop(PAIRS, NX, own_halo_second, 0, unroll=6)

    zero_plane = jnp.zeros((NY, NZ), f32)
    zero_tile = jnp.zeros((TILE, NZ), f32)

    def side_plane(q, temp, ident, chip, plane_in):
        conduct, store = element(temp, ident, ref_ref, grad_ref, store_ref)
        tp[q, :NY, :] = temp
        cp[q, :NY, :] = conduct * plane_in
        capp[q, :NY, :] = store
        chp[q, :NY, :] = rate * chip
        put_halo(q, pltpu.roll(yp_ref[PX + q - PAIRS], 4, 0), plane_in)

    for k in range(HIGH):
        side_plane(
            NX + k, xp_ref[k], xp_ref[4 + k], xp_ref[8 + k] if k < 3 else zero_plane, high_x
        )
    for k in range(LOW):
        side_plane(
            NX + HIGH + k,
            xm_ref[k],
            xm_ref[3 + k],
            xm_ref[5 + k] if k > 0 else zero_plane,
            low_x,
        )

    lanes = lane((PY, NZ))
    subs = sublane((PY, NZ))
    inner_z = jnp.where(lanes < NZ - 1, 1.0, 0.0).astype(f32)
    edge_z = jnp.where((lanes == 0) | (lanes == NZ - 1), 1.0, 0.0).astype(f32)
    rows_in = jnp.where(subs < NY, 1.0, jnp.where(subs < NY + 4, high_y, low_y)).astype(f32)
    lane_tile = lane((TILE, NZ))

    def up_y(v):
        return pltpu.roll(v, PY - 1, 0)

    def down_y(v):
        return pltpu.roll(v, 1, 0)

    def up_z(v):
        return pltpu.roll(v, NZ - 1, 1)

    def down_z(v):
        return pltpu.roll(v, 1, 1)

    def fold(v):
        return (v[0:8] + v[8:16]) + (v[16:24] + v[24:32])

    def surface(acc, plane, x):
        for t in range(NY // TILE):
            part = plane[TILE * t : TILE * (t + 1)]
            acc = jnp.where(
                lane_tile == x * 4 + t, jnp.broadcast_to(part[:, 0:1], (TILE, NZ)), acc
            )
        return acc

    def faces(q, nxt, ex_before, fx_before, plane_in):
        c0 = cp[q]
        t0 = tp[q]
        e_x = c0 + cp[nxt]
        f_x = e_x * (tp[nxt] - t0)
        e_y = c0 + up_y(c0)
        f_y = e_y * (up_y(t0) - t0)
        e_z = (c0 + up_z(c0)) * inner_z
        f_z = e_z * (up_z(t0) - t0)
        c_b = c0 * edge_z
        diag = (capp[q] + c_b) + (
            (e_x + ex_before) + ((e_y + down_y(e_y)) + (e_z + down_z(e_z)))
        )
        inverse = (rows_in * plane_in) / diag
        resid = (chp[q] - c_b * t0) + (
            (f_x - fx_before) + ((f_y - down_y(f_y)) + (f_z - down_z(f_z)))
        )
        first = resid * inverse
        ex[q] = e_x
        ey[q] = e_y
        ez[q] = e_z
        dinv[q] = inverse
        w0_ref[q] = first
        return e_x, f_x, resid, first

    e_first = cp[36] + cp[37]
    carry = (e_first, e_first * (tp[37] - tp[36]))
    for q, nxt in ((37, 38), (38, 0)):
        carry = faces(q, nxt, carry[0], carry[1], low_x)[:2]

    def faces_own(q, state):
        e_b, f_b, m0, s_t, s_0 = state
        e_x, f_x, resid, first = faces(q, q + 1, e_b, f_b, one)
        m0 = m0 + fold(resid[:NY] * first[:NY])
        return e_x, f_x, m0, surface(s_t, tp[q, :NY, :], q), surface(s_0, first, q)

    e_b, f_b, m0, surf_t, surf_0 = lax.fori_loop(
        0, NX, faces_own, (carry[0], carry[1], zero_tile, zero_tile, zero_tile), unroll=8
    )
    carry = (e_b, f_b)
    for q in (32, 33, 34):
        carry = faces(q, q + 1, carry[0], carry[1], high_x)[:2]

    def neighbours(src, q, nxt, g_before):
        v = src[q]
        e_x = ex[q]
        e_y = ey[q]
        e_z = ez[q]
        total = (e_x * src[nxt] + g_before) + (
            (e_y * up_y(v) + down_y(e_y * v)) + (e_z * up_z(v) + down_z(e_z * v))
        )
        return total, v, e_x * v

    def advance(src, dst, before, prologue, epilogue):
        carry = ex[before] * src[before]
        for q, nxt in prologue:
            total, _, carry = neighbours(src, q, nxt, carry)
            dst[q] = dinv[q] * total

        def step(q, state):
            g, ma, mb, surf = state
            total, v, g = neighbours(src, q, q + 1, g)
            new = dinv[q] * total
            dst[q] = new
            ma = ma + fold(total[:NY] * v[:NY])
            mb = mb + fold(total[:NY] * new[:NY])
            return g, ma, mb, surface(surf, new, q)

        carry, ma, mb, surf = lax.fori_loop(
            0, NX, step, (carry, zero_tile, zero_tile, zero_tile), unroll=8
        )
        for q, nxt in epilogue:
            total, _, carry = neighbours(src, q, nxt, carry)
            dst[q] = dinv[q] * total
        return ma, mb, surf

    m1, m2, surf_1 = advance(w0_ref, w1_ref, 37, ((38, 0),), ((32, 33), (33, 34)))
    m3, m4, surf_2 = advance(w1_ref, w2_ref, 38, (), ((32, 33),))

    def last(q, acc):
        v = w2_ref[q]
        half = ex[q] * w2_ref[q + 1] + (ey[q] * up_y(v) + ez[q] * up_z(v))
        return acc + fold(half[:NY] * v[:NY])

    m5 = lax.fori_loop(0, NX, last, zero_tile, unroll=8)
    m5 = m5 + m5

    moments = zero_tile
    for k, m in enumerate((m0, m1, m2, m3, m4, m5)):
        moments = jnp.where(sub == k, jnp.sum(m, axis=0, keepdims=True), moments)
    for k in range(send_ref.shape[0]):
        for j, tile in enumerate((surf_t, surf_0, surf_1, surf_2, moments)):
            send_ref[k, TILE * j : TILE * (j + 1), :] = tile


def lookup_kernel(site_ref, table_ref, out_ref, parts):
    blocks = table_ref.shape[0]
    targets = site_ref.shape[0]
    iy = lax.axis_index("gy")
    width = NY * lax.axis_size("gy")
    sub = sublane((TILE, NZ))
    subs = sublane((NZ, NZ))
    zero = jnp.zeros((TILE, NZ), f32)
    fields = FIELDS - 1
    for f in range(fields):
        rest = jnp.concatenate(
            [table_ref[a, TILE * (f + 1) : TILE * (f + 2), :] for a in range(blocks)], axis=0
        ).T
        for k in range(2):
            part = rest.astype(bf16)
            parts[NZ * f : NZ * (f + 1), NZ * k : NZ * (k + 1)] = part
            rest = rest - part.astype(f32)

    total = table_ref[0, TILE * FIELDS :, :]
    for a in range(1, blocks):
        total = total + table_ref[a, TILE * FIELDS :, :]

    def one(b, _):
        site = site_ref[b]
        row = site // width
        col = site - row * width
        here = (col // NY) == iy
        y = col % NY
        row_of = jnp.where(here, (row // NX) * TILE + y % TILE, -1)
        lane_of = (row % NX) * (NY // TILE) + y // TILE
        hot = jnp.concatenate(
            [
                jnp.where(
                    subs == jnp.broadcast_to(row_of[s : s + 1], (NZ, NZ)), 1.0, 0.0
                ).astype(bf16)
                for s in range(TILE)
            ],
            axis=1,
        )
        hot = jnp.concatenate([hot, hot], axis=0)
        found = [zero] * FIELDS
        lines = [
            jnp.dot(parts[NZ * f : NZ * (f + 1)], hot, preferred_element_type=f32)
            for f in range(fields)
        ]
        for s in range(TILE):
            lanes = jnp.broadcast_to(lane_of[s : s + 1], (TILE, NZ))
            rows = jnp.broadcast_to(row_of[s : s + 1], (TILE, NZ)) - sub
            acc = [zero] * FIELDS
            for a in range(blocks):
                got = jnp.take_along_axis(table_ref[a, 0:TILE, :], lanes, axis=1)
                acc[0] = jnp.where(rows == a * TILE, got, acc[0])
            lanes = lanes - sub
            for t in range(NZ // TILE):
                hit = lanes == t * TILE
                for f in range(fields):
                    acc[f + 1] = jnp.where(
                        hit,
                        lines[f][TILE * t : TILE * (t + 1), NZ * s : NZ * (s + 1)],
                        acc[f + 1],
                    )
            for f in range(FIELDS):
                found[f] = jnp.where(sub == s, jnp.sum(acc[f], axis=0, keepdims=True), found[f])
        for f in range(FIELDS):
            out_ref[b, TILE * f : TILE * (f + 1), :] = found[f]
        out_ref[b, TILE * FIELDS :, :] = total
        return 0

    lax.fori_loop(0, targets, one, 0, unroll=2)


def cg_coefficients(m):
    a = [m[j] - m[j + 1] for j in range(5)]

    def quadratic(v, h):
        total = None
        for i in range(3):
            for j in range(3):
                if v[i] is None or v[j] is None:
                    continue
                term = v[i] * v[j] * h[i + j]
                total = term if total is None else total + term
        return total

    def add(u, v):
        return v if u is None else u if v is None else u + v

    def scale(s, v):
        return [None if e is None else s * e for e in v]

    one = jnp.ones_like(m[0])
    z = [one, None, None]
    p = [one, None, None]
    rz = m[0]
    x = [None, None, None]
    for step in range(3):
        alpha = rz / quadratic(p, a)
        x = [add(e, g) for e, g in zip(x, scale(alpha, p))]
        if step < 2:
            ap = scale(alpha, p)
            moved = [None] + ap[:2]
            z = [
                add(add(z[i], None if ap[i] is None else -ap[i]), moved[i]) for i in range(3)
            ]
            new = quadratic(z, m)
            p = [add(z[i], e) for i, e in enumerate(scale(new / rz, p))]
            rz = new
    return x


def final_kernel(
    got_ref, pressure_hbm, t_ref, w0_ref, w1_ref, w2_ref, temp_ref, growth_ref, pressure_ref, sem
):
    copy = pltpu.make_async_copy(pressure_hbm, pressure_ref, sem)
    copy.start()
    total = got_ref[0]
    for b in range(1, got_ref.shape[0]):
        total = total + got_ref[b]
    sums = jnp.sum(total[TILE * FIELDS :], axis=1, keepdims=True)
    m = [sums[k : k + 1] for k in range(6)]
    c = cg_coefficients(m)
    c_tile = [jnp.broadcast_to(e, (TILE, NZ)) for e in c]
    c_plane = [jnp.broadcast_to(e, (NY, NZ)) for e in c]
    flank = total[0:TILE]
    for k in range(3):
        flank = flank + c_tile[k] * total[TILE * (k + 1) : TILE * (k + 2)]
    soft = jnp.maximum(flank, 0.0) + jnp.log1p(jnp.exp(-jnp.abs(flank)))
    copy.wait()
    growth_ref[...] = usui_rate * pressure_ref[...] * jnp.exp(-usui_energy / (1.0 + soft))

    def plane(q, _):
        temp_ref[q] = (
            t_ref[q, :NY, :]
            + c_plane[0] * w0_ref[q, :NY, :]
            + c_plane[1] * w1_ref[q, :NY, :]
            + c_plane[2] * w2_ref[q, :NY, :]
        )
        return 0

    lax.fori_loop(0, NX, plane, 0, unroll=2)


def local(
    prior_kelvin_state,
    substance_identifier,
    chip_touch_indicator,
    substance_reference_diffusivity,
    substance_diffusivity_gradient,
    substance_storage_coefficient,
    clearance_point_indices,
    clearance_face_pressure,
):
    size_x = lax.axis_size("gx")
    size_y = lax.axis_size("gy")
    temp, ident, chip = prior_kelvin_state, substance_identifier, chip_touch_indicator
    vmem = pl.BlockSpec(memory_space=pltpu.VMEM)
    smem = pl.BlockSpec(memory_space=pltpu.SMEM)

    def params(mib):
        return pltpu.CompilerParams(vmem_limit_bytes=mib * MIB)


    anywhere = pl.BlockSpec(memory_space=pltpu.HBM)

    def arr(*shape, dtype=f32):
        return jax.ShapeDtypeStruct(shape, dtype)

    def buf(*shape, dtype=f32):
        return pltpu.VMEM(shape, dtype)

    def in_hbm(*arrays):
        return [pltpu.with_memory_space_constraint(a, pltpu.HBM) for a in arrays]

    i32 = jnp.int32
    x_low, x_high, y_low, y_high, sites = pl.pallas_call(
        pack_kernel,
        name="pack",
        in_specs=[anywhere] * 4,
        out_specs=[vmem] * 5,
        out_shape=[
            arr(11, NY, NZ),
            arr(8, NY, NZ),
            arr(PX + PAIRS, TILE, NZ),
            arr(PX, TILE, NZ),
            arr(size_y, TILE, NZ, dtype=i32),
        ],
        scratch_shapes=[
            buf(NX, TILE, NZ),
            buf(NX, TILE, NZ),
            buf(NX, TILE, NZ, dtype=i32),
            buf(NX, TILE, NZ, dtype=i32),
            buf(NX, TILE, NZ, dtype=i32),
            buf(NX, TILE, NZ, dtype=i32),
            buf(HIGH, NY, NZ),
            buf(HIGH, NY, NZ),
            buf(HIGH, NY, NZ, dtype=i32),
            buf(HIGH, NY, NZ, dtype=i32),
            buf(HIGH, NY, NZ, dtype=i32),
            buf(HIGH, NY, NZ, dtype=i32),
            buf(TILE, NZ, dtype=i32),
            pltpu.SemaphoreType.DMA((13,)),
        ],
        compiler_params=params(10),
    )(*in_hbm(temp, ident, chip, clearance_point_indices.reshape(TILE, NZ)))
    sites = lax.all_to_all(sites, "gy", 0, 0)

    up, down = shift_pairs(size_x)
    xp = lax.ppermute(x_low, "gx", down)
    xm = lax.ppermute(x_high, "gx", up)
    y_low, y_high, sites = pl.pallas_call(
        corner_kernel,
        name="corners",
        in_specs=[vmem] * 5,
        out_specs=[vmem] * 3,
        out_shape=[
            arr(PX + PAIRS, TILE, NZ),
            arr(PX, TILE, NZ),
            arr(size_y, TILE, NZ, dtype=i32),
        ],
        input_output_aliases={0: 0, 1: 1, 4: 2},
        compiler_params=params(8),
    )(y_low, y_high, xp, xm, sites)
    up, down = shift_pairs(size_y)
    yp = lax.ppermute(y_low, "gy", down)
    ym = lax.ppermute(y_high, "gy", up)

    tables = (
        substance_reference_diffusivity,
        substance_diffusivity_gradient,
        substance_storage_coefficient,
    )
    padded = arr(PX, PY, NZ)
    *own, sites = pl.pallas_call(
        own_kernel,
        name="own_cells",
        in_specs=[smem] * 3 + [vmem] * 4,
        out_specs=[vmem] * 5,
        out_shape=[padded] * 4 + [arr(size_y, TILE, NZ, dtype=i32)],
        input_output_aliases={6: 4},
        compiler_params=params(12),
    )(*tables, temp, ident, chip, sites)

    payload = TILE * (FIELDS + 1)
    start, _, _, _, w0, w1, w2, send = pl.pallas_call(
        krylov_kernel,
        name="krylov",
        in_specs=[smem] * 3 + [vmem] * 8,
        out_specs=[vmem] * 8,
        out_shape=[padded] * 7 + [arr(size_x, payload, NZ)],
        input_output_aliases={3: 0, 4: 1, 5: 2, 6: 3},
        scratch_shapes=[buf(PX, PY, NZ)] * 4,
        compiler_params=params(24),
    )(*tables, *own, xp, xm, yp, ym)
    table = lax.all_to_all(send, "gx", 0, 0)
    found = pl.pallas_call(
        lookup_kernel,
        name="lookup",
        in_specs=[vmem] * 2,
        out_specs=vmem,
        out_shape=arr(size_y, payload, NZ),
        scratch_shapes=[buf(NZ * (FIELDS - 1), 2 * NZ, dtype=bf16)],
        compiler_params=params(20),
    )(sites, table)
    got = lax.all_to_all(found, "gy", 0, 0)
    temperature, growth = pl.pallas_call(
        final_kernel,
        name="finish",
        in_specs=[vmem, anywhere, vmem, vmem, vmem, vmem],
        out_specs=[vmem] * 2,
        out_shape=[arr(NX, NY, NZ), arr(TILE, NZ)],
        scratch_shapes=[buf(TILE, NZ), pltpu.SemaphoreType.DMA(())],
        compiler_params=params(12),
    )(got, *in_hbm(clearance_face_pressure.reshape(TILE, NZ)), start, w0, w1, w2)
    return temperature, growth.reshape(-1)


def solution(mesh):
    in_specs = (
        P("gx", "gy", None),
        P("gx", "gy", None),
        P("gx", "gy", None),
        P(),
        P(),
        P(),
        P(("gx", "gy")),
        P(("gx", "gy")),
    )
    out_specs = (P("gx", "gy", None), P(("gx", "gy")))
    return jax.shard_map(local, mesh=mesh, in_specs=in_specs, out_specs=out_specs, check_vma=False)
```

```python
import jax
import jax.numpy as jnp
from jax import lax
from jax.experimental import pallas as pl
from jax.experimental.pallas import tpu as pltpu
from jax.sharding import PartitionSpec as P

clock_advance = 2.0
interface_warming_rate = 3.0
usui_rate = 3.0
usui_energy = 4.0
kelvin_shift_amount = 2.0

LOW = 3
HIGH = 4
NX = 32
NY = 32
NZ = 128
PX = NX + HIGH + LOW
PY = NY + 8
FIELDS = 4
TILE = 8
PAIRS = 20
MIB = 1024 * 1024
f32 = jnp.float32
bf16 = jnp.bfloat16


def swaps(count, first):
    low = range(first, count - 1, 2)
    return [(i, i + 1) for i in low] + [(i + 1, i) for i in low]


def sublane(shape):
    return lax.broadcasted_iota(jnp.int32, shape, len(shape) - 2)


def lane(shape):
    return lax.broadcasted_iota(jnp.int32, shape, len(shape) - 1)


def first_tile(sub, temp, ident):
    return jnp.where(sub < 4, temp, pltpu.roll(ident, 4, 0))


def last_tile(sub, temp, ident, chip):
    return jnp.where(
        sub >= 5, temp, jnp.where(sub >= 2, pltpu.roll(ident, 5, 0), pltpu.roll(chip, 2, 0))
    )


def pack_kernel(
    t_hbm,
    id_hbm,
    chip_hbm,
    site_hbm,
    xa,
    xb,
    ya,
    yb,
    sites,
    t_a,
    t_b,
    i_a,
    i_b,
    c_a,
    c_b,
    t_p,
    t_m,
    i_p,
    i_m,
    c_p,
    c_m,
    site_ref,
    sems,
):
    copies = []
    for k, (src, dst) in enumerate(
        (
            (t_hbm.at[pl.ds(0, HIGH)], t_p),
            (id_hbm.at[pl.ds(0, HIGH)], i_p),
            (chip_hbm.at[pl.ds(0, HIGH)], c_p),
            (t_hbm.at[pl.ds(NX - HIGH, HIGH)], t_m),
            (id_hbm.at[pl.ds(NX - HIGH, HIGH)], i_m),
            (chip_hbm.at[pl.ds(NX - HIGH, HIGH)], c_m),
            (t_hbm.at[:, pl.ds(0, TILE)], t_a),
            (id_hbm.at[:, pl.ds(0, TILE)], i_a),
            (chip_hbm.at[:, pl.ds(0, TILE)], c_a),
            (t_hbm.at[:, pl.ds(NY - TILE, TILE)], t_b),
            (id_hbm.at[:, pl.ds(NY - TILE, TILE)], i_b),
            (chip_hbm.at[:, pl.ds(NY - TILE, TILE)], c_b),
            (site_hbm, site_ref),
        )
    ):
        copies.append(pltpu.make_async_copy(src, dst, sems.at[k]))
        copies[-1].start()
    for copy in copies:
        copy.wait()

    def x_sides(low, high):
        for k in range(HIGH):
            low[k] = t_p[k]
            low[4 + k] = i_p[k].astype(f32)
            if k < 3:
                low[8 + k] = c_p[k].astype(f32)
                high[k] = t_m[1 + k]
                high[3 + k] = i_m[1 + k].astype(f32)
            if k < 2:
                high[6 + k] = c_m[2 + k].astype(f32)

    even_x = lax.rem(lax.axis_index("gx"), 2) == 0
    even_y = lax.rem(lax.axis_index("gy"), 2) == 0

    @pl.when(even_x)
    def _():
        x_sides(xa, xb)

    @pl.when(jnp.logical_not(even_x))
    def _():
        x_sides(xb, xa)

    sub = sublane((TILE, NZ))

    def own(q, _):
        low = first_tile(sub, t_a[q], i_a[q].astype(f32))
        high = last_tile(sub, t_b[q], i_b[q].astype(f32), c_b[q].astype(f32))
        ya[q] = jnp.where(even_y, low, high)
        yb[q] = jnp.where(even_y, high, low)
        return 0

    lax.fori_loop(0, NX, own, 0, unroll=8)
    for j in range(PAIRS):
        tile = c_a[j].astype(f32)
        if j + PAIRS < NX:
            tile = jnp.where(sub < 4, tile, pltpu.roll(c_a[j + PAIRS].astype(f32), 4, 0))
        ya[PX + j] = tile
        yb[PX + j] = tile
    for k in range(sites.shape[0]):
        sites[k] = site_ref[...]


def corner_kernel(ya_in, yb_in, xa_ref, xb_ref, sites_in, ya, yb, sites_out):
    del ya_in, yb_in, sites_in, sites_out
    even_x = lax.rem(lax.axis_index("gx"), 2) == 0
    even_y = lax.rem(lax.axis_index("gy"), 2) == 0
    sub = sublane((TILE, NZ))
    zero = jnp.zeros((TILE, NZ), f32)
    first = pl.ds(0, TILE)
    last = pl.ds(NY - TILE, TILE)

    def high_side(k, rows):
        return jnp.where(even_x, xb_ref[k, rows, :], xa_ref[k, rows, :])

    def low_side(k, rows):
        return jnp.where(even_x, xa_ref[k, rows, :], xb_ref[k, rows, :])

    for k in range(HIGH + LOW):
        q = NX + k
        if k < HIGH:
            side, places = high_side, (k, 4 + k, 8 + k if k < 3 else None)
        else:
            j = k - HIGH
            side, places = low_side, (j, 3 + j, 5 + j if j else None)
        temp, ident, chip = places
        low = first_tile(sub, side(temp, first), side(ident, first))
        high = last_tile(
            sub, side(temp, last), side(ident, last), zero if chip is None else side(chip, last)
        )
        ya[q] = jnp.where(even_y, low, high)
        yb[q] = jnp.where(even_y, high, low)
        if chip is not None:
            place = PX + q - PAIRS
            tile = jnp.where(sub < 4, ya[place], pltpu.roll(side(chip, first), 4, 0))
            ya[place] = tile
            yb[place] = tile


def pick(ident, table):
    low = jnp.where(ident == 1, table[1], table[0])
    high = jnp.where(ident == 3, table[3], table[2])
    return jnp.where(ident >= 2, high, low)


def element(temp, ident, ref_ref, grad_ref, store_ref):
    conduct = pick(ident, ref_ref) * (
        1.0 + pick(ident, grad_ref) * jnp.tanh(temp - kelvin_shift_amount)
    )
    return conduct, pick(ident, store_ref)


def own_kernel(
    ref_ref, grad_ref, store_ref, t_ref, id_ref, chip_ref, sites_in, tp, cp, capp, chp, sites_out
):
    del sites_in, sites_out

    def own_plane(q, _):
        temp = t_ref[q]
        conduct, store = element(temp, id_ref[q], ref_ref, grad_ref, store_ref)
        tp[q, :NY, :] = temp
        cp[q, :NY, :] = conduct
        capp[q, :NY, :] = store
        chp[q, :NY, :] = clock_advance * interface_warming_rate * chip_ref[q].astype(f32)
        return 0

    lax.fori_loop(0, NX, own_plane, 0, unroll=4)


def krylov_kernel(
    ref_ref,
    grad_ref,
    store_ref,
    tp_in,
    cp_in,
    capp_in,
    chp_in,
    xa_ref,
    xb_ref,
    ya_ref,
    yb_ref,
    tp,
    cp,
    capp,
    chp,
    w0_ref,
    w1_ref,
    w2_ref,
    send_ref,
    ex,
    ey,
    ez,
    dinv,
):
    del tp_in, cp_in, capp_in, chp_in
    ix = lax.axis_index("gx")
    iy = lax.axis_index("gy")
    last_x = lax.axis_size("gx") - 1
    last_y = lax.axis_size("gy") - 1
    sub = sublane((TILE, NZ))
    one = jnp.ones((), f32)
    low_x = jnp.where(ix > 0, 1.0, 0.0).astype(f32)
    high_x = jnp.where(ix < last_x, 1.0, 0.0).astype(f32)
    low_y = jnp.where(iy > 0, 1.0, 0.0).astype(f32)
    high_y = jnp.where(iy < last_y, 1.0, 0.0).astype(f32)
    rows_halo = jnp.where(sub < 4, high_y, low_y)
    rate = clock_advance * interface_warming_rate

    even_x = lax.rem(ix, 2) == 0
    even_y = lax.rem(iy, 2) == 0

    def high_row(q):
        return jnp.where(even_y, yb_ref[q], ya_ref[q])

    def low_row(q):
        return jnp.where(even_y, ya_ref[q], yb_ref[q])

    def high_plane(k):
        return jnp.where(even_x, xb_ref[k], xa_ref[k])

    def low_plane(k):
        return jnp.where(even_x, xa_ref[k], xb_ref[k])

    def put_halo(q, chip_high, plane_in):
        high = high_row(q)
        low = low_row(q)
        temp = jnp.where(sub < 4, high, low)
        ident = jnp.where(sub < 4, pltpu.roll(high, 4, 0), pltpu.roll(low, 3, 0))
        chip = jnp.where(sub < 4, chip_high, pltpu.roll(low, 6, 0))
        conduct, store = element(temp, ident, ref_ref, grad_ref, store_ref)
        tp[q, NY:, :] = temp
        cp[q, NY:, :] = conduct * (rows_halo * plane_in)
        capp[q, NY:, :] = store
        chp[q, NY:, :] = rate * chip

    def own_halo_first(q, _):
        put_halo(q, high_row(PX + q), one)
        return 0

    def own_halo_second(q, _):
        put_halo(q, pltpu.roll(high_row(PX + q - PAIRS), 4, 0), one)
        return 0

    lax.fori_loop(0, PAIRS, own_halo_first, 0, unroll=5)
    lax.fori_loop(PAIRS, NX, own_halo_second, 0, unroll=6)

    zero_plane = jnp.zeros((NY, NZ), f32)
    zero_tile = jnp.zeros((TILE, NZ), f32)

    def side_plane(q, temp, ident, chip, plane_in):
        conduct, store = element(temp, ident, ref_ref, grad_ref, store_ref)
        tp[q, :NY, :] = temp
        cp[q, :NY, :] = conduct * plane_in
        capp[q, :NY, :] = store
        chp[q, :NY, :] = rate * chip
        put_halo(q, pltpu.roll(high_row(PX + q - PAIRS), 4, 0), plane_in)

    for k in range(HIGH):
        side_plane(
            NX + k,
            high_plane(k),
            high_plane(4 + k),
            high_plane(8 + k) if k < 3 else zero_plane,
            high_x,
        )
    for k in range(LOW):
        side_plane(
            NX + HIGH + k,
            low_plane(k),
            low_plane(3 + k),
            low_plane(5 + k) if k > 0 else zero_plane,
            low_x,
        )

    lanes = lane((PY, NZ))
    subs = sublane((PY, NZ))
    inner_z = jnp.where(lanes < NZ - 1, 1.0, 0.0).astype(f32)
    edge_z = jnp.where((lanes == 0) | (lanes == NZ - 1), 1.0, 0.0).astype(f32)
    rows_in = jnp.where(subs < NY, 1.0, jnp.where(subs < NY + 4, high_y, low_y)).astype(f32)
    lane_tile = lane((TILE, NZ))

    def up_y(v):
        return pltpu.roll(v, PY - 1, 0)

    def down_y(v):
        return pltpu.roll(v, 1, 0)

    def up_z(v):
        return pltpu.roll(v, NZ - 1, 1)

    def down_z(v):
        return pltpu.roll(v, 1, 1)

    def fold(v):
        return (v[0:8] + v[8:16]) + (v[16:24] + v[24:32])

    def surface(acc, plane, x):
        for t in range(NY // TILE):
            part = plane[TILE * t : TILE * (t + 1)]
            acc = jnp.where(
                lane_tile == x * 4 + t, jnp.broadcast_to(part[:, 0:1], (TILE, NZ)), acc
            )
        return acc

    def faces(q, nxt, ex_before, fx_before, plane_in):
        c0 = cp[q]
        t0 = tp[q]
        e_x = c0 + cp[nxt]
        f_x = e_x * (tp[nxt] - t0)
        e_y = c0 + up_y(c0)
        f_y = e_y * (up_y(t0) - t0)
        e_z = (c0 + up_z(c0)) * inner_z
        f_z = e_z * (up_z(t0) - t0)
        c_b = c0 * edge_z
        diag = (capp[q] + c_b) + (
            (e_x + ex_before) + ((e_y + down_y(e_y)) + (e_z + down_z(e_z)))
        )
        inverse = (rows_in * plane_in) / diag
        resid = (chp[q] - c_b * t0) + (
            (f_x - fx_before) + ((f_y - down_y(f_y)) + (f_z - down_z(f_z)))
        )
        first = resid * inverse
        ex[q] = e_x
        ey[q] = e_y
        ez[q] = e_z
        dinv[q] = inverse
        w0_ref[q] = first
        return e_x, f_x, resid, first

    e_first = cp[36] + cp[37]
    carry = (e_first, e_first * (tp[37] - tp[36]))
    for q, nxt in ((37, 38), (38, 0)):
        carry = faces(q, nxt, carry[0], carry[1], low_x)[:2]

    def faces_own(q, state):
        e_b, f_b, m0, s_t, s_0 = state
        e_x, f_x, resid, first = faces(q, q + 1, e_b, f_b, one)
        m0 = m0 + fold(resid[:NY] * first[:NY])
        return e_x, f_x, m0, surface(s_t, tp[q, :NY, :], q), surface(s_0, first, q)

    e_b, f_b, m0, surf_t, surf_0 = lax.fori_loop(
        0, NX, faces_own, (carry[0], carry[1], zero_tile, zero_tile, zero_tile), unroll=8
    )
    carry = (e_b, f_b)
    for q in (32, 33, 34):
        carry = faces(q, q + 1, carry[0], carry[1], high_x)[:2]

    def neighbours(src, q, nxt, g_before):
        v = src[q]
        e_x = ex[q]
        e_y = ey[q]
        e_z = ez[q]
        total = (e_x * src[nxt] + g_before) + (
            (e_y * up_y(v) + down_y(e_y * v)) + (e_z * up_z(v) + down_z(e_z * v))
        )
        return total, v, e_x * v

    def advance(src, dst, before, prologue, epilogue):
        carry = ex[before] * src[before]
        for q, nxt in prologue:
            total, _, carry = neighbours(src, q, nxt, carry)
            dst[q] = dinv[q] * total

        def step(q, state):
            g, ma, mb, surf = state
            total, v, g = neighbours(src, q, q + 1, g)
            new = dinv[q] * total
            dst[q] = new
            ma = ma + fold(total[:NY] * v[:NY])
            mb = mb + fold(total[:NY] * new[:NY])
            return g, ma, mb, surface(surf, new, q)

        carry, ma, mb, surf = lax.fori_loop(
            0, NX, step, (carry, zero_tile, zero_tile, zero_tile), unroll=8
        )
        for q, nxt in epilogue:
            total, _, carry = neighbours(src, q, nxt, carry)
            dst[q] = dinv[q] * total
        return ma, mb, surf

    m1, m2, surf_1 = advance(w0_ref, w1_ref, 37, ((38, 0),), ((32, 33), (33, 34)))
    m3, m4, surf_2 = advance(w1_ref, w2_ref, 38, (), ((32, 33),))

    def last(q, acc):
        v = w2_ref[q]
        half = ex[q] * w2_ref[q + 1] + (ey[q] * up_y(v) + ez[q] * up_z(v))
        return acc + fold(half[:NY] * v[:NY])

    m5 = lax.fori_loop(0, NX, last, zero_tile, unroll=8)
    m5 = m5 + m5

    moments = zero_tile
    for k, m in enumerate((m0, m1, m2, m3, m4, m5)):
        moments = jnp.where(sub == k, jnp.sum(m, axis=0, keepdims=True), moments)
    for k in range(send_ref.shape[0]):
        for j, tile in enumerate((surf_t, surf_0, surf_1, surf_2, moments)):
            send_ref[k, TILE * j : TILE * (j + 1), :] = tile


def lookup_kernel(site_ref, table_ref, out_ref, parts):
    blocks = table_ref.shape[0]
    targets = site_ref.shape[0]
    iy = lax.axis_index("gy")
    width = NY * lax.axis_size("gy")
    sub = sublane((TILE, NZ))
    subs = sublane((NZ, NZ))
    zero = jnp.zeros((TILE, NZ), f32)
    fields = FIELDS - 1
    for f in range(fields):
        rest = jnp.concatenate(
            [table_ref[a, TILE * (f + 1) : TILE * (f + 2), :] for a in range(blocks)], axis=0
        ).T
        for k in range(2):
            part = rest.astype(bf16)
            parts[NZ * f : NZ * (f + 1), NZ * k : NZ * (k + 1)] = part
            rest = rest - part.astype(f32)

    total = table_ref[0, TILE * FIELDS :, :]
    for a in range(1, blocks):
        total = total + table_ref[a, TILE * FIELDS :, :]

    def one(b, _):
        site = site_ref[b]
        row = site // width
        col = site - row * width
        here = (col // NY) == iy
        y = col % NY
        row_of = jnp.where(here, (row // NX) * TILE + y % TILE, -1)
        lane_of = (row % NX) * (NY // TILE) + y // TILE
        hot = jnp.concatenate(
            [
                jnp.where(
                    subs == jnp.broadcast_to(row_of[s : s + 1], (NZ, NZ)), 1.0, 0.0
                ).astype(bf16)
                for s in range(TILE)
            ],
            axis=1,
        )
        hot = jnp.concatenate([hot, hot], axis=0)
        found = [zero] * FIELDS
        lines = [
            jnp.dot(parts[NZ * f : NZ * (f + 1)], hot, preferred_element_type=f32)
            for f in range(fields)
        ]
        for s in range(TILE):
            lanes = jnp.broadcast_to(lane_of[s : s + 1], (TILE, NZ))
            rows = jnp.broadcast_to(row_of[s : s + 1], (TILE, NZ)) - sub
            acc = [zero] * FIELDS
            for a in range(blocks):
                got = jnp.take_along_axis(table_ref[a, 0:TILE, :], lanes, axis=1)
                acc[0] = jnp.where(rows == a * TILE, got, acc[0])
            lanes = lanes - sub
            for t in range(NZ // TILE):
                hit = lanes == t * TILE
                for f in range(fields):
                    acc[f + 1] = jnp.where(
                        hit,
                        lines[f][TILE * t : TILE * (t + 1), NZ * s : NZ * (s + 1)],
                        acc[f + 1],
                    )
            for f in range(FIELDS):
                found[f] = jnp.where(sub == s, jnp.sum(acc[f], axis=0, keepdims=True), found[f])
        for f in range(FIELDS):
            out_ref[b, TILE * f : TILE * (f + 1), :] = found[f]
        out_ref[b, TILE * FIELDS :, :] = total
        return 0

    lax.fori_loop(0, targets, one, 0, unroll=2)


def cg_coefficients(m):
    a = [m[j] - m[j + 1] for j in range(5)]

    def quadratic(v, h):
        total = None
        for i in range(3):
            for j in range(3):
                if v[i] is None or v[j] is None:
                    continue
                term = v[i] * v[j] * h[i + j]
                total = term if total is None else total + term
        return total

    def add(u, v):
        return v if u is None else u if v is None else u + v

    def scale(s, v):
        return [None if e is None else s * e for e in v]

    one = jnp.ones_like(m[0])
    z = [one, None, None]
    p = [one, None, None]
    rz = m[0]
    x = [None, None, None]
    for step in range(3):
        alpha = rz / quadratic(p, a)
        x = [add(e, g) for e, g in zip(x, scale(alpha, p))]
        if step < 2:
            ap = scale(alpha, p)
            moved = [None] + ap[:2]
            z = [
                add(add(z[i], None if ap[i] is None else -ap[i]), moved[i]) for i in range(3)
            ]
            new = quadratic(z, m)
            p = [add(z[i], e) for i, e in enumerate(scale(new / rz, p))]
            rz = new
    return x


def final_kernel(
    got_ref,
    pressure_hbm,
    t_ref,
    w0_ref,
    w1_ref,
    w2_ref,
    temp_hbm,
    growth_ref,
    pressure_ref,
    temp_ref,
    sem,
    out_sems,
):
    copy = pltpu.make_async_copy(pressure_hbm, pressure_ref, sem)
    copy.start()
    total = got_ref[0]
    for b in range(1, got_ref.shape[0]):
        total = total + got_ref[b]
    sums = jnp.sum(total[TILE * FIELDS :], axis=1, keepdims=True)
    m = [sums[k : k + 1] for k in range(6)]
    c = cg_coefficients(m)
    c_tile = [jnp.broadcast_to(e, (TILE, NZ)) for e in c]
    c_plane = [jnp.broadcast_to(e, (NY, NZ)) for e in c]

    def plane(q, _):
        temp_ref[q] = (
            t_ref[q, :NY, :]
            + c_plane[0] * w0_ref[q, :NY, :]
            + c_plane[1] * w1_ref[q, :NY, :]
            + c_plane[2] * w2_ref[q, :NY, :]
        )
        return 0

    outs = []
    step = NX // 4
    for k in range(4):
        lax.fori_loop(step * k, step * (k + 1), plane, 0, unroll=4)
        part = pl.ds(step * k, step)
        outs.append(pltpu.make_async_copy(temp_ref.at[part], temp_hbm.at[part], out_sems.at[k]))
        outs[-1].start()

    flank = total[0:TILE]
    for k in range(3):
        flank = flank + c_tile[k] * total[TILE * (k + 1) : TILE * (k + 2)]
    soft = jnp.maximum(flank, 0.0) + jnp.log1p(jnp.exp(-jnp.abs(flank)))
    copy.wait()
    growth_ref[...] = usui_rate * pressure_ref[...] * jnp.exp(-usui_energy / (1.0 + soft))
    for out in outs:
        out.wait()


def local(
    prior_kelvin_state,
    substance_identifier,
    chip_touch_indicator,
    substance_reference_diffusivity,
    substance_diffusivity_gradient,
    substance_storage_coefficient,
    clearance_point_indices,
    clearance_face_pressure,
):
    size_x = lax.axis_size("gx")
    size_y = lax.axis_size("gy")
    temp, ident, chip = prior_kelvin_state, substance_identifier, chip_touch_indicator
    vmem = pl.BlockSpec(memory_space=pltpu.VMEM)
    smem = pl.BlockSpec(memory_space=pltpu.SMEM)

    def params(mib):
        return pltpu.CompilerParams(vmem_limit_bytes=mib * MIB)


    anywhere = pl.BlockSpec(memory_space=pltpu.HBM)

    def arr(*shape, dtype=f32):
        return jax.ShapeDtypeStruct(shape, dtype)

    def buf(*shape, dtype=f32):
        return pltpu.VMEM(shape, dtype)

    def in_hbm(*arrays):
        return [pltpu.with_memory_space_constraint(a, pltpu.HBM) for a in arrays]

    i32 = jnp.int32
    xa, xb, ya, yb, sites = pl.pallas_call(
        pack_kernel,
        name="pack",
        in_specs=[anywhere] * 4,
        out_specs=[vmem] * 5,
        out_shape=[
            arr(11, NY, NZ),
            arr(11, NY, NZ),
            arr(PX + PAIRS, TILE, NZ),
            arr(PX + PAIRS, TILE, NZ),
            arr(size_y, TILE, NZ, dtype=i32),
        ],
        scratch_shapes=[
            buf(NX, TILE, NZ),
            buf(NX, TILE, NZ),
            buf(NX, TILE, NZ, dtype=i32),
            buf(NX, TILE, NZ, dtype=i32),
            buf(NX, TILE, NZ, dtype=i32),
            buf(NX, TILE, NZ, dtype=i32),
            buf(HIGH, NY, NZ),
            buf(HIGH, NY, NZ),
            buf(HIGH, NY, NZ, dtype=i32),
            buf(HIGH, NY, NZ, dtype=i32),
            buf(HIGH, NY, NZ, dtype=i32),
            buf(HIGH, NY, NZ, dtype=i32),
            buf(TILE, NZ, dtype=i32),
            pltpu.SemaphoreType.DMA((13,)),
        ],
        compiler_params=params(10),
    )(*in_hbm(temp, ident, chip, clearance_point_indices.reshape(TILE, NZ)))
    sites = lax.all_to_all(sites, "gy", 0, 0)

    xa = lax.ppermute(xa, "gx", swaps(size_x, 1))
    xb = lax.ppermute(xb, "gx", swaps(size_x, 0))
    ya, yb, sites = pl.pallas_call(
        corner_kernel,
        name="corners",
        in_specs=[vmem] * 5,
        out_specs=[vmem] * 3,
        out_shape=[
            arr(PX + PAIRS, TILE, NZ),
            arr(PX + PAIRS, TILE, NZ),
            arr(size_y, TILE, NZ, dtype=i32),
        ],
        input_output_aliases={0: 0, 1: 1, 4: 2},
        compiler_params=params(8),
    )(ya, yb, xa, xb, sites)
    ya = lax.ppermute(ya, "gy", swaps(size_y, 1))
    yb = lax.ppermute(yb, "gy", swaps(size_y, 0))

    tables = (
        substance_reference_diffusivity,
        substance_diffusivity_gradient,
        substance_storage_coefficient,
    )
    padded = arr(PX, PY, NZ)
    *own, sites = pl.pallas_call(
        own_kernel,
        name="own_cells",
        in_specs=[smem] * 3 + [vmem] * 4,
        out_specs=[vmem] * 5,
        out_shape=[padded] * 4 + [arr(size_y, TILE, NZ, dtype=i32)],
        input_output_aliases={6: 4},
        compiler_params=params(12),
    )(*tables, temp, ident, chip, sites)

    payload = TILE * (FIELDS + 1)
    start, _, _, _, w0, w1, w2, send = pl.pallas_call(
        krylov_kernel,
        name="krylov",
        in_specs=[smem] * 3 + [vmem] * 8,
        out_specs=[vmem] * 8,
        out_shape=[padded] * 7 + [arr(size_x, payload, NZ)],
        input_output_aliases={3: 0, 4: 1, 5: 2, 6: 3},
        scratch_shapes=[buf(PX, PY, NZ)] * 4,
        compiler_params=params(24),
    )(*tables, *own, xa, xb, ya, yb)
    table = lax.all_to_all(send, "gx", 0, 0)
    found = pl.pallas_call(
        lookup_kernel,
        name="lookup",
        in_specs=[vmem] * 2,
        out_specs=vmem,
        out_shape=arr(size_y, payload, NZ),
        scratch_shapes=[buf(NZ * (FIELDS - 1), 2 * NZ, dtype=bf16)],
        compiler_params=params(20),
    )(sites, table)
    got = lax.all_to_all(found, "gy", 0, 0)
    temperature, growth = pl.pallas_call(
        final_kernel,
        name="finish",
        in_specs=[vmem, anywhere, vmem, vmem, vmem, vmem],
        out_specs=[anywhere, vmem],
        out_shape=[arr(NX, NY, NZ), arr(TILE, NZ)],
        scratch_shapes=[
            buf(TILE, NZ),
            buf(NX, NY, NZ),
            pltpu.SemaphoreType.DMA(()),
            pltpu.SemaphoreType.DMA((4,)),
        ],
        compiler_params=params(12),
    )(got, *in_hbm(clearance_face_pressure.reshape(TILE, NZ)), start, w0, w1, w2)
    return temperature, growth.reshape(-1)


def solution(mesh):
    in_specs = (
        P("gx", "gy", None),
        P("gx", "gy", None),
        P("gx", "gy", None),
        P(),
        P(),
        P(),
        P(("gx", "gy")),
        P(("gx", "gy")),
    )
    out_specs = (P("gx", "gy", None), P(("gx", "gy")))
    return jax.shard_map(local, mesh=mesh, in_specs=in_specs, out_specs=out_specs, check_vma=False)
```

```python
import jax
import jax.numpy as jnp
from jax import lax
from jax.experimental import pallas as pl
from jax.experimental.pallas import tpu as pltpu
from jax.sharding import PartitionSpec as P

clock_advance = 2.0
interface_warming_rate = 3.0
usui_rate = 3.0
usui_energy = 4.0
kelvin_shift_amount = 2.0

LOW = 3
HIGH = 4
NX = 32
NY = 32
NZ = 128
PX = NX + HIGH + LOW
PY = NY + 8
FIELDS = 4
TILE = 8
PAIRS = 20
MIB = 1024 * 1024
f32 = jnp.float32
bf16 = jnp.bfloat16


def swaps(count, first):
    low = range(first, count - 1, 2)
    return [(i, i + 1) for i in low] + [(i + 1, i) for i in low]


def sublane(shape):
    return lax.broadcasted_iota(jnp.int32, shape, len(shape) - 2)


def lane(shape):
    return lax.broadcasted_iota(jnp.int32, shape, len(shape) - 1)


def first_tile(sub, temp, ident):
    return jnp.where(sub < 4, temp, pltpu.roll(ident, 4, 0))


def last_tile(sub, temp, ident, chip):
    return jnp.where(
        sub >= 5, temp, jnp.where(sub >= 2, pltpu.roll(ident, 5, 0), pltpu.roll(chip, 2, 0))
    )


def pack_kernel(
    t_hbm,
    id_hbm,
    chip_hbm,
    site_hbm,
    xa,
    xb,
    ya,
    yb,
    sites,
    t_a,
    t_b,
    i_a,
    i_b,
    c_a,
    c_b,
    t_p,
    t_m,
    i_p,
    i_m,
    c_p,
    c_m,
    site_ref,
    sems,
):
    copies = []
    for k, (src, dst) in enumerate(
        (
            (t_hbm.at[pl.ds(0, HIGH)], t_p),
            (id_hbm.at[pl.ds(0, HIGH)], i_p),
            (chip_hbm.at[pl.ds(0, HIGH)], c_p),
            (t_hbm.at[pl.ds(NX - HIGH, HIGH)], t_m),
            (id_hbm.at[pl.ds(NX - HIGH, HIGH)], i_m),
            (chip_hbm.at[pl.ds(NX - HIGH, HIGH)], c_m),
            (t_hbm.at[:, pl.ds(0, TILE)], t_a),
            (id_hbm.at[:, pl.ds(0, TILE)], i_a),
            (chip_hbm.at[:, pl.ds(0, TILE)], c_a),
            (t_hbm.at[:, pl.ds(NY - TILE, TILE)], t_b),
            (id_hbm.at[:, pl.ds(NY - TILE, TILE)], i_b),
            (chip_hbm.at[:, pl.ds(NY - TILE, TILE)], c_b),
            (site_hbm, site_ref),
        )
    ):
        copies.append(pltpu.make_async_copy(src, dst, sems.at[k]))
        copies[-1].start()
    for copy in copies:
        copy.wait()

    def x_sides(low, high):
        for k in range(HIGH):
            low[k] = t_p[k]
            low[4 + k] = i_p[k].astype(f32)
            if k < 3:
                low[8 + k] = c_p[k].astype(f32)
                high[k] = t_m[1 + k]
                high[3 + k] = i_m[1 + k].astype(f32)
            if k < 2:
                high[6 + k] = c_m[2 + k].astype(f32)

    even_x = lax.rem(lax.axis_index("gx"), 2) == 0
    even_y = lax.rem(lax.axis_index("gy"), 2) == 0

    @pl.when(even_x)
    def _():
        x_sides(xa, xb)

    @pl.when(jnp.logical_not(even_x))
    def _():
        x_sides(xb, xa)

    sub = sublane((TILE, NZ))

    def own(q, _):
        low = first_tile(sub, t_a[q], i_a[q].astype(f32))
        high = last_tile(sub, t_b[q], i_b[q].astype(f32), c_b[q].astype(f32))
        ya[q] = jnp.where(even_y, low, high)
        yb[q] = jnp.where(even_y, high, low)
        return 0

    lax.fori_loop(0, NX, own, 0, unroll=8)
    for j in range(PAIRS):
        tile = c_a[j].astype(f32)
        if j + PAIRS < NX:
            tile = jnp.where(sub < 4, tile, pltpu.roll(c_a[j + PAIRS].astype(f32), 4, 0))
        ya[PX + j] = tile
        yb[PX + j] = tile
    for k in range(sites.shape[0]):
        sites[k] = site_ref[...]


def corner_kernel(ya_in, yb_in, xa_ref, xb_ref, sites_in, ya, yb, sites_out):
    del ya_in, yb_in, sites_in, sites_out
    even_x = lax.rem(lax.axis_index("gx"), 2) == 0
    even_y = lax.rem(lax.axis_index("gy"), 2) == 0
    sub = sublane((TILE, NZ))
    zero = jnp.zeros((TILE, NZ), f32)
    first = pl.ds(0, TILE)
    last = pl.ds(NY - TILE, TILE)

    def high_side(k, rows):
        return jnp.where(even_x, xb_ref[k, rows, :], xa_ref[k, rows, :])

    def low_side(k, rows):
        return jnp.where(even_x, xa_ref[k, rows, :], xb_ref[k, rows, :])

    for k in range(HIGH + LOW):
        q = NX + k
        if k < HIGH:
            side, places = high_side, (k, 4 + k, 8 + k if k < 3 else None)
        else:
            j = k - HIGH
            side, places = low_side, (j, 3 + j, 5 + j if j else None)
        temp, ident, chip = places
        low = first_tile(sub, side(temp, first), side(ident, first))
        high = last_tile(
            sub, side(temp, last), side(ident, last), zero if chip is None else side(chip, last)
        )
        ya[q] = jnp.where(even_y, low, high)
        yb[q] = jnp.where(even_y, high, low)
        if chip is not None:
            place = PX + q - PAIRS
            tile = jnp.where(sub < 4, ya[place], pltpu.roll(side(chip, first), 4, 0))
            ya[place] = tile
            yb[place] = tile


def pick(ident, table):
    low = jnp.where(ident == 1, table[1], table[0])
    high = jnp.where(ident == 3, table[3], table[2])
    return jnp.where(ident >= 2, high, low)


def up_z(v):
    return pltpu.roll(v, NZ - 1, 1)


def down_z(v):
    return pltpu.roll(v, 1, 1)


def cells(temp, ident, chip, tables, inside=None):
    ref_ref, grad_ref, store_ref = tables
    conduct = pick(ident, ref_ref) * (
        1.0 + pick(ident, grad_ref) * jnp.tanh(temp - kelvin_shift_amount)
    )
    if inside is not None:
        conduct = conduct * inside
    lanes = lane(temp.shape)
    inner_z = jnp.where(lanes < NZ - 1, 1.0, 0.0).astype(f32)
    edge_z = jnp.where((lanes == 0) | (lanes == NZ - 1), 1.0, 0.0).astype(f32)
    e_z = (conduct + up_z(conduct)) * inner_z
    f_z = e_z * (up_z(temp) - temp)
    c_b = conduct * edge_z
    diag = (pick(ident, store_ref) + c_b) + (e_z + down_z(e_z))
    resid = (clock_advance * interface_warming_rate * chip - c_b * temp) + (f_z - down_z(f_z))
    return conduct, diag, resid, e_z


def surface(read, terms):
    rows = sublane((TILE, NZ))
    lanes = lane((TILE, NZ))
    total = jnp.zeros((TILE, NZ), f32)
    for s in range(TILE):
        one_hot = jnp.where((rows == s) & (lanes == 0), 1.0, 0.0).astype(bf16)
        rest = read(s)
        for _ in range(terms):
            part = rest.astype(bf16)
            total = total + lax.dot_general(
                one_hot, part, (((1,), (1,)), ((), ())), preferred_element_type=f32
            )
            rest = rest - part.astype(f32)
    return total


def own_rows(ref):
    per = NX // TILE
    return lambda s: jnp.concatenate([ref[per * s + i, :NY, :] for i in range(per)], axis=0)


def own_kernel(
    ref_ref,
    grad_ref,
    store_ref,
    t_ref,
    id_ref,
    chip_ref,
    sites_in,
    tp,
    cp,
    dp,
    rp,
    ez,
    surf_ref,
    sites_out,
):
    del sites_in, sites_out
    tables = (ref_ref, grad_ref, store_ref)

    def own_plane(q, _):
        temp = t_ref[q]
        conduct, diag, resid, e_z = cells(temp, id_ref[q], chip_ref[q].astype(f32), tables)
        tp[q, :NY, :] = temp
        cp[q, :NY, :] = conduct
        dp[q, :NY, :] = diag
        rp[q, :NY, :] = resid
        ez[q, :NY, :] = e_z
        return 0

    lax.fori_loop(0, NX, own_plane, 0, unroll=4)
    surf_ref[...] = surface(own_rows(t_ref), 3)


def krylov_kernel(
    ref_ref,
    grad_ref,
    store_ref,
    tp_in,
    cp_in,
    dp_in,
    rp_in,
    ez_in,
    surf_ref,
    xa_ref,
    xb_ref,
    ya_ref,
    yb_ref,
    tp,
    cp,
    dp,
    rp,
    ez,
    w0_ref,
    w1_ref,
    w2_ref,
    send_ref,
    ex,
    ey,
    dinv,
):
    del tp_in, cp_in, dp_in, rp_in, ez_in
    tables = (ref_ref, grad_ref, store_ref)
    ix = lax.axis_index("gx")
    iy = lax.axis_index("gy")
    last_x = lax.axis_size("gx") - 1
    last_y = lax.axis_size("gy") - 1
    sub = sublane((TILE, NZ))
    one = jnp.ones((), f32)
    low_x = jnp.where(ix > 0, 1.0, 0.0).astype(f32)
    high_x = jnp.where(ix < last_x, 1.0, 0.0).astype(f32)
    low_y = jnp.where(iy > 0, 1.0, 0.0).astype(f32)
    high_y = jnp.where(iy < last_y, 1.0, 0.0).astype(f32)
    rows_halo = jnp.where(sub < 4, high_y, low_y)

    even_x = lax.rem(ix, 2) == 0
    even_y = lax.rem(iy, 2) == 0

    def high_row(q):
        return jnp.where(even_y, yb_ref[q], ya_ref[q])

    def low_row(q):
        return jnp.where(even_y, ya_ref[q], yb_ref[q])

    def high_plane(k):
        return jnp.where(even_x, xb_ref[k], xa_ref[k])

    def low_plane(k):
        return jnp.where(even_x, xa_ref[k], xb_ref[k])

    def put_halo(q, chip_high, plane_in):
        high = high_row(q)
        low = low_row(q)
        temp = jnp.where(sub < 4, high, low)
        ident = jnp.where(sub < 4, pltpu.roll(high, 4, 0), pltpu.roll(low, 3, 0))
        chip = jnp.where(sub < 4, chip_high, pltpu.roll(low, 6, 0))
        conduct, diag, resid, e_z = cells(temp, ident, chip, tables, rows_halo * plane_in)
        tp[q, NY:, :] = temp
        cp[q, NY:, :] = conduct
        dp[q, NY:, :] = diag
        rp[q, NY:, :] = resid
        ez[q, NY:, :] = e_z

    def own_halo_first(q, _):
        put_halo(q, high_row(PX + q), one)
        return 0

    def own_halo_second(q, _):
        put_halo(q, pltpu.roll(high_row(PX + q - PAIRS), 4, 0), one)
        return 0

    lax.fori_loop(0, PAIRS, own_halo_first, 0, unroll=5)
    lax.fori_loop(PAIRS, NX, own_halo_second, 0, unroll=6)

    zero_plane = jnp.zeros((NY, NZ), f32)
    zero_tile = jnp.zeros((TILE, NZ), f32)

    def side_plane(q, temp, ident, chip, plane_in):
        conduct, diag, resid, e_z = cells(temp, ident, chip, tables, plane_in)
        tp[q, :NY, :] = temp
        cp[q, :NY, :] = conduct
        dp[q, :NY, :] = diag
        rp[q, :NY, :] = resid
        ez[q, :NY, :] = e_z
        put_halo(q, pltpu.roll(high_row(PX + q - PAIRS), 4, 0), plane_in)

    for k in range(HIGH):
        side_plane(
            NX + k,
            high_plane(k),
            high_plane(4 + k),
            high_plane(8 + k) if k < 3 else zero_plane,
            high_x,
        )
    for k in range(LOW):
        side_plane(
            NX + HIGH + k,
            low_plane(k),
            low_plane(3 + k),
            low_plane(5 + k) if k > 0 else zero_plane,
            low_x,
        )

    subs = sublane((PY, NZ))
    rows_in = jnp.where(subs < NY, 1.0, jnp.where(subs < NY + 4, high_y, low_y)).astype(f32)

    def up_y(v):
        return pltpu.roll(v, PY - 1, 0)

    def down_y(v):
        return pltpu.roll(v, 1, 0)

    def fold(v):
        return (v[0:8] + v[8:16]) + (v[16:24] + v[24:32])

    def faces(q, nxt, ex_before, fx_before, plane_in):
        c0 = cp[q]
        t0 = tp[q]
        e_x = c0 + cp[nxt]
        f_x = e_x * (tp[nxt] - t0)
        e_y = c0 + up_y(c0)
        f_y = e_y * (up_y(t0) - t0)
        diag = dp[q] + ((e_x + ex_before) + (e_y + down_y(e_y)))
        inverse = (rows_in * plane_in) / diag
        resid = rp[q] + ((f_x - fx_before) + (f_y - down_y(f_y)))
        first = resid * inverse
        ex[q] = e_x
        ey[q] = e_y
        dinv[q] = inverse
        w0_ref[q] = first
        return e_x, f_x, resid, first

    e_first = cp[36] + cp[37]
    carry = (e_first, e_first * (tp[37] - tp[36]))
    for q, nxt in ((37, 38), (38, 0)):
        carry = faces(q, nxt, carry[0], carry[1], low_x)[:2]

    def faces_own(q, state):
        e_b, f_b, m0 = state
        e_x, f_x, resid, first = faces(q, q + 1, e_b, f_b, one)
        return e_x, f_x, m0 + fold(resid[:NY] * first[:NY])

    e_b, f_b, m0 = lax.fori_loop(0, NX, faces_own, (carry[0], carry[1], zero_tile), unroll=8)
    carry = (e_b, f_b)
    for q in (32, 33, 34):
        carry = faces(q, q + 1, carry[0], carry[1], high_x)[:2]

    def neighbours(src, q, nxt, g_before):
        v = src[q]
        e_x = ex[q]
        e_y = ey[q]
        e_z = ez[q]
        total = (e_x * src[nxt] + g_before) + (
            (e_y * up_y(v) + down_y(e_y * v)) + (e_z * up_z(v) + down_z(e_z * v))
        )
        return total, v, e_x * v

    def advance(src, dst, before, prologue, epilogue):
        carry = ex[before] * src[before]
        for q, nxt in prologue:
            total, _, carry = neighbours(src, q, nxt, carry)
            dst[q] = dinv[q] * total

        def step(q, state):
            g, ma, mb = state
            total, v, g = neighbours(src, q, q + 1, g)
            new = dinv[q] * total
            dst[q] = new
            ma = ma + fold(total[:NY] * v[:NY])
            mb = mb + fold(total[:NY] * new[:NY])
            return g, ma, mb

        carry, ma, mb = lax.fori_loop(0, NX, step, (carry, zero_tile, zero_tile), unroll=8)
        for q, nxt in epilogue:
            total, _, carry = neighbours(src, q, nxt, carry)
            dst[q] = dinv[q] * total
        return ma, mb

    m1, m2 = advance(w0_ref, w1_ref, 37, ((38, 0),), ((32, 33), (33, 34)))
    m3, m4 = advance(w1_ref, w2_ref, 38, (), ((32, 33),))

    def last(q, acc):
        v = w2_ref[q]
        half = ex[q] * w2_ref[q + 1] + (ey[q] * up_y(v) + ez[q] * up_z(v))
        return acc + fold(half[:NY] * v[:NY])

    m5 = lax.fori_loop(0, NX, last, zero_tile, unroll=8)
    m5 = m5 + m5

    moments = zero_tile
    for k, m in enumerate((m0, m1, m2, m3, m4, m5)):
        moments = jnp.where(sub == k, jnp.sum(m, axis=0, keepdims=True), moments)
    fields = [surf_ref[...]] + [surface(own_rows(w), 2) for w in (w0_ref, w1_ref, w2_ref)]
    for k in range(send_ref.shape[0]):
        for j, tile in enumerate((*fields, moments)):
            send_ref[k, TILE * j : TILE * (j + 1), :] = tile


def lookup_kernel(site_ref, table_ref, out_ref, parts):
    blocks = table_ref.shape[0]
    targets = site_ref.shape[0]
    iy = lax.axis_index("gy")
    width = NY * lax.axis_size("gy")
    sub = sublane((TILE, NZ))
    subs = sublane((NZ, NZ))
    zero = jnp.zeros((TILE, NZ), f32)
    fields = FIELDS - 1
    for f in range(fields):
        rest = jnp.concatenate(
            [table_ref[a, TILE * (f + 1) : TILE * (f + 2), :] for a in range(blocks)], axis=0
        ).T
        for k in range(2):
            part = rest.astype(bf16)
            parts[NZ * f : NZ * (f + 1), NZ * k : NZ * (k + 1)] = part
            rest = rest - part.astype(f32)

    total = table_ref[0, TILE * FIELDS :, :]
    for a in range(1, blocks):
        total = total + table_ref[a, TILE * FIELDS :, :]

    def one(b, _):
        site = site_ref[b]
        row = site // width
        col = site - row * width
        here = (col // NY) == iy
        cell = (row % NX) * NY + col % NY
        row_of = jnp.where(here, (row // NX) * TILE + cell // NZ, -1)
        lane_of = cell % NZ
        found = [zero] * FIELDS
        for pair in range(0, TILE, 2):
            hot = jnp.concatenate(
                [
                    jnp.where(
                        subs == jnp.broadcast_to(row_of[s : s + 1], (NZ, NZ)), 1.0, 0.0
                    ).astype(bf16)
                    for s in (pair, pair + 1)
                ],
                axis=1,
            )
            hot = jnp.concatenate([hot, hot], axis=0)
            lanes = [jnp.broadcast_to(lane_of[pair + i : pair + i + 1], (TILE, NZ)) for i in (0, 1)]
            offset = [e - sub for e in lanes]
            for i in (0, 1):
                rows = jnp.broadcast_to(row_of[pair + i : pair + i + 1], (TILE, NZ)) - sub
                acc = zero
                for a in range(blocks):
                    got = jnp.take_along_axis(table_ref[a, 0:TILE, :], lanes[i], axis=1)
                    acc = jnp.where(rows == a * TILE, got, acc)
                found[0] = jnp.where(
                    sub == pair + i, jnp.sum(acc, axis=0, keepdims=True), found[0]
                )
            for f in range(fields):
                line = jnp.dot(parts[NZ * f : NZ * (f + 1)], hot, preferred_element_type=f32)
                for i in (0, 1):
                    acc = zero
                    for t in range(NZ // TILE):
                        acc = jnp.where(
                            offset[i] == t * TILE,
                            line[TILE * t : TILE * (t + 1), NZ * i : NZ * (i + 1)],
                            acc,
                        )
                    found[f + 1] = jnp.where(
                        sub == pair + i, jnp.sum(acc, axis=0, keepdims=True), found[f + 1]
                    )
        for f in range(FIELDS):
            out_ref[b, TILE * f : TILE * (f + 1), :] = found[f]
        out_ref[b, TILE * FIELDS :, :] = total
        return 0

    lax.fori_loop(0, targets, one, 0, unroll=2)


def cg_coefficients(m):
    a = [m[j] - m[j + 1] for j in range(5)]

    def quadratic(v, h):
        total = None
        for i in range(3):
            for j in range(3):
                if v[i] is None or v[j] is None:
                    continue
                term = v[i] * v[j] * h[i + j]
                total = term if total is None else total + term
        return total

    def add(u, v):
        return v if u is None else u if v is None else u + v

    def scale(s, v):
        return [None if e is None else s * e for e in v]

    one = jnp.ones_like(m[0])
    z = [one, None, None]
    p = [one, None, None]
    rz = m[0]
    x = [None, None, None]
    for step in range(3):
        alpha = rz / quadratic(p, a)
        x = [add(e, g) for e, g in zip(x, scale(alpha, p))]
        if step < 2:
            ap = scale(alpha, p)
            moved = [None] + ap[:2]
            z = [
                add(add(z[i], None if ap[i] is None else -ap[i]), moved[i]) for i in range(3)
            ]
            new = quadratic(z, m)
            p = [add(z[i], e) for i, e in enumerate(scale(new / rz, p))]
            rz = new
    return x


def final_kernel(
    got_ref,
    pressure_hbm,
    t_ref,
    w0_ref,
    w1_ref,
    w2_ref,
    temp_hbm,
    growth_ref,
    pressure_ref,
    temp_ref,
    sem,
    out_sems,
):
    copy = pltpu.make_async_copy(pressure_hbm, pressure_ref, sem)
    copy.start()
    total = got_ref[0]
    for b in range(1, got_ref.shape[0]):
        total = total + got_ref[b]
    sums = jnp.sum(total[TILE * FIELDS :], axis=1, keepdims=True)
    m = [sums[k : k + 1] for k in range(6)]
    c = cg_coefficients(m)
    c_tile = [jnp.broadcast_to(e, (TILE, NZ)) for e in c]
    c_plane = [jnp.broadcast_to(e, (NY, NZ)) for e in c]

    def plane(q, _):
        temp_ref[q] = (
            t_ref[q, :NY, :]
            + c_plane[0] * w0_ref[q, :NY, :]
            + c_plane[1] * w1_ref[q, :NY, :]
            + c_plane[2] * w2_ref[q, :NY, :]
        )
        return 0

    outs = []
    step = NX // 4
    for k in range(4):
        lax.fori_loop(step * k, step * (k + 1), plane, 0, unroll=4)
        part = pl.ds(step * k, step)
        outs.append(pltpu.make_async_copy(temp_ref.at[part], temp_hbm.at[part], out_sems.at[k]))
        outs[-1].start()

    flank = total[0:TILE]
    for k in range(3):
        flank = flank + c_tile[k] * total[TILE * (k + 1) : TILE * (k + 2)]
    soft = jnp.maximum(flank, 0.0) + jnp.log1p(jnp.exp(-jnp.abs(flank)))
    copy.wait()
    growth_ref[...] = usui_rate * pressure_ref[...] * jnp.exp(-usui_energy / (1.0 + soft))
    for out in outs:
        out.wait()


def local(
    prior_kelvin_state,
    substance_identifier,
    chip_touch_indicator,
    substance_reference_diffusivity,
    substance_diffusivity_gradient,
    substance_storage_coefficient,
    clearance_point_indices,
    clearance_face_pressure,
):
    size_x = lax.axis_size("gx")
    size_y = lax.axis_size("gy")
    temp, ident, chip = prior_kelvin_state, substance_identifier, chip_touch_indicator
    vmem = pl.BlockSpec(memory_space=pltpu.VMEM)
    smem = pl.BlockSpec(memory_space=pltpu.SMEM)

    def params(mib):
        return pltpu.CompilerParams(vmem_limit_bytes=mib * MIB)


    anywhere = pl.BlockSpec(memory_space=pltpu.HBM)

    def arr(*shape, dtype=f32):
        return jax.ShapeDtypeStruct(shape, dtype)

    def buf(*shape, dtype=f32):
        return pltpu.VMEM(shape, dtype)

    def in_hbm(*arrays):
        return [pltpu.with_memory_space_constraint(a, pltpu.HBM) for a in arrays]

    i32 = jnp.int32
    xa, xb, ya, yb, sites = pl.pallas_call(
        pack_kernel,
        name="pack",
        in_specs=[anywhere] * 4,
        out_specs=[vmem] * 5,
        out_shape=[
            arr(11, NY, NZ),
            arr(11, NY, NZ),
            arr(PX + PAIRS, TILE, NZ),
            arr(PX + PAIRS, TILE, NZ),
            arr(size_y, TILE, NZ, dtype=i32),
        ],
        scratch_shapes=[
            buf(NX, TILE, NZ),
            buf(NX, TILE, NZ),
            buf(NX, TILE, NZ, dtype=i32),
            buf(NX, TILE, NZ, dtype=i32),
            buf(NX, TILE, NZ, dtype=i32),
            buf(NX, TILE, NZ, dtype=i32),
            buf(HIGH, NY, NZ),
            buf(HIGH, NY, NZ),
            buf(HIGH, NY, NZ, dtype=i32),
            buf(HIGH, NY, NZ, dtype=i32),
            buf(HIGH, NY, NZ, dtype=i32),
            buf(HIGH, NY, NZ, dtype=i32),
            buf(TILE, NZ, dtype=i32),
            pltpu.SemaphoreType.DMA((13,)),
        ],
        compiler_params=params(10),
    )(*in_hbm(temp, ident, chip, clearance_point_indices.reshape(TILE, NZ)))
    sites = lax.all_to_all(sites, "gy", 0, 0)

    xa = lax.ppermute(xa, "gx", swaps(size_x, 1))
    xb = lax.ppermute(xb, "gx", swaps(size_x, 0))
    ya, yb, sites = pl.pallas_call(
        corner_kernel,
        name="corners",
        in_specs=[vmem] * 5,
        out_specs=[vmem] * 3,
        out_shape=[
            arr(PX + PAIRS, TILE, NZ),
            arr(PX + PAIRS, TILE, NZ),
            arr(size_y, TILE, NZ, dtype=i32),
        ],
        input_output_aliases={0: 0, 1: 1, 4: 2},
        compiler_params=params(8),
    )(ya, yb, xa, xb, sites)
    ya = lax.ppermute(ya, "gy", swaps(size_y, 1))
    yb = lax.ppermute(yb, "gy", swaps(size_y, 0))

    tables = (
        substance_reference_diffusivity,
        substance_diffusivity_gradient,
        substance_storage_coefficient,
    )
    padded = arr(PX, PY, NZ)
    *own, sites = pl.pallas_call(
        own_kernel,
        name="own_cells",
        in_specs=[smem] * 3 + [vmem] * 4,
        out_specs=[vmem] * 7,
        out_shape=[padded] * 5 + [arr(TILE, NZ), arr(size_y, TILE, NZ, dtype=i32)],
        input_output_aliases={6: 6},
        compiler_params=params(12),
    )(*tables, temp, ident, chip, sites)

    payload = TILE * (FIELDS + 1)
    start, _, _, _, _, w0, w1, w2, send = pl.pallas_call(
        krylov_kernel,
        name="krylov",
        in_specs=[smem] * 3 + [vmem] * 10,
        out_specs=[vmem] * 9,
        out_shape=[padded] * 8 + [arr(size_x, payload, NZ)],
        input_output_aliases={3: 0, 4: 1, 5: 2, 6: 3, 7: 4},
        scratch_shapes=[buf(PX, PY, NZ)] * 3,
        compiler_params=params(24),
    )(*tables, *own, xa, xb, ya, yb)
    table = lax.all_to_all(send, "gx", 0, 0)
    found = pl.pallas_call(
        lookup_kernel,
        name="lookup",
        in_specs=[vmem] * 2,
        out_specs=vmem,
        out_shape=arr(size_y, payload, NZ),
        scratch_shapes=[buf(NZ * (FIELDS - 1), 2 * NZ, dtype=bf16)],
        compiler_params=params(20),
    )(sites, table)
    got = lax.all_to_all(found, "gy", 0, 0)
    temperature, growth = pl.pallas_call(
        final_kernel,
        name="finish",
        in_specs=[vmem, anywhere, vmem, vmem, vmem, vmem],
        out_specs=[anywhere, vmem],
        out_shape=[arr(NX, NY, NZ), arr(TILE, NZ)],
        scratch_shapes=[
            buf(TILE, NZ),
            buf(NX, NY, NZ),
            pltpu.SemaphoreType.DMA(()),
            pltpu.SemaphoreType.DMA((4,)),
        ],
        compiler_params=params(12),
    )(got, *in_hbm(clearance_face_pressure.reshape(TILE, NZ)), start, w0, w1, w2)
    return temperature, growth.reshape(-1)


def solution(mesh):
    in_specs = (
        P("gx", "gy", None),
        P("gx", "gy", None),
        P("gx", "gy", None),
        P(),
        P(),
        P(),
        P(("gx", "gy")),
        P(("gx", "gy")),
    )
    out_specs = (P("gx", "gy", None), P(("gx", "gy")))
    return jax.shard_map(local, mesh=mesh, in_specs=in_specs, out_specs=out_specs, check_vma=False)
```

```python
import jax
import jax.numpy as jnp
from jax import lax
from jax.experimental import pallas as pl
from jax.experimental.pallas import tpu as pltpu
from jax.sharding import PartitionSpec as P

clock_advance = 2.0
interface_warming_rate = 3.0
usui_rate = 3.0
usui_energy = 4.0
kelvin_shift_amount = 2.0

LOW = 3
HIGH = 4
NX = 32
NY = 32
NZ = 128
PX = NX + HIGH + LOW
PY = NY + 8
FIELDS = 4
TILE = 8
PAIRS = 20
MIB = 1024 * 1024
f32 = jnp.float32
bf16 = jnp.bfloat16


def swaps(count, first):
    low = range(first, count - 1, 2)
    return [(i, i + 1) for i in low] + [(i + 1, i) for i in low]


def sublane(shape):
    return lax.broadcasted_iota(jnp.int32, shape, len(shape) - 2)


def lane(shape):
    return lax.broadcasted_iota(jnp.int32, shape, len(shape) - 1)


def first_tile(sub, temp, ident):
    return jnp.where(sub < 4, temp, pltpu.roll(ident, 4, 0))


def last_tile(sub, temp, ident, chip):
    return jnp.where(
        sub >= 5, temp, jnp.where(sub >= 2, pltpu.roll(ident, 5, 0), pltpu.roll(chip, 2, 0))
    )


def pack_kernel(
    t_hbm,
    id_hbm,
    chip_hbm,
    site_hbm,
    xa,
    xb,
    ya,
    yb,
    sites,
    t_a,
    t_b,
    i_a,
    i_b,
    c_a,
    c_b,
    t_p,
    t_m,
    i_p,
    i_m,
    c_p,
    c_m,
    site_ref,
    sems,
):
    copies = []
    for k, (src, dst) in enumerate(
        (
            (t_hbm.at[pl.ds(0, HIGH)], t_p),
            (id_hbm.at[pl.ds(0, HIGH)], i_p),
            (chip_hbm.at[pl.ds(0, HIGH)], c_p),
            (t_hbm.at[pl.ds(NX - HIGH, HIGH)], t_m),
            (id_hbm.at[pl.ds(NX - HIGH, HIGH)], i_m),
            (chip_hbm.at[pl.ds(NX - HIGH, HIGH)], c_m),
            (t_hbm.at[:, pl.ds(0, TILE)], t_a),
            (id_hbm.at[:, pl.ds(0, TILE)], i_a),
            (chip_hbm.at[:, pl.ds(0, TILE)], c_a),
            (t_hbm.at[:, pl.ds(NY - TILE, TILE)], t_b),
            (id_hbm.at[:, pl.ds(NY - TILE, TILE)], i_b),
            (chip_hbm.at[:, pl.ds(NY - TILE, TILE)], c_b),
            (site_hbm, site_ref),
        )
    ):
        copies.append(pltpu.make_async_copy(src, dst, sems.at[k]))
        copies[-1].start()
    for copy in copies:
        copy.wait()

    def x_sides(low, high):
        for k in range(HIGH):
            low[k] = t_p[k]
            low[4 + k] = i_p[k].astype(f32)
            if k < 3:
                low[8 + k] = c_p[k].astype(f32)
                high[k] = t_m[1 + k]
                high[3 + k] = i_m[1 + k].astype(f32)
            if k < 2:
                high[6 + k] = c_m[2 + k].astype(f32)

    even_x = lax.rem(lax.axis_index("gx"), 2) == 0
    even_y = lax.rem(lax.axis_index("gy"), 2) == 0

    @pl.when(even_x)
    def _():
        x_sides(xa, xb)

    @pl.when(jnp.logical_not(even_x))
    def _():
        x_sides(xb, xa)

    sub = sublane((TILE, NZ))

    def own(q, _):
        low = first_tile(sub, t_a[q], i_a[q].astype(f32))
        high = last_tile(sub, t_b[q], i_b[q].astype(f32), c_b[q].astype(f32))
        ya[q] = jnp.where(even_y, low, high)
        yb[q] = jnp.where(even_y, high, low)
        return 0

    lax.fori_loop(0, NX, own, 0, unroll=8)
    for j in range(PAIRS):
        tile = c_a[j].astype(f32)
        if j + PAIRS < NX:
            tile = jnp.where(sub < 4, tile, pltpu.roll(c_a[j + PAIRS].astype(f32), 4, 0))
        ya[PX + j] = tile
        yb[PX + j] = tile
    for k in range(sites.shape[0]):
        sites[k] = site_ref[...]


def corner_kernel(ya_in, yb_in, xa_ref, xb_ref, sites_in, ya, yb, sites_out):
    del ya_in, yb_in, sites_in, sites_out
    even_x = lax.rem(lax.axis_index("gx"), 2) == 0
    even_y = lax.rem(lax.axis_index("gy"), 2) == 0
    sub = sublane((TILE, NZ))
    zero = jnp.zeros((TILE, NZ), f32)
    first = pl.ds(0, TILE)
    last = pl.ds(NY - TILE, TILE)

    def high_side(k, rows):
        return jnp.where(even_x, xb_ref[k, rows, :], xa_ref[k, rows, :])

    def low_side(k, rows):
        return jnp.where(even_x, xa_ref[k, rows, :], xb_ref[k, rows, :])

    for k in range(HIGH + LOW):
        q = NX + k
        if k < HIGH:
            side, places = high_side, (k, 4 + k, 8 + k if k < 3 else None)
        else:
            j = k - HIGH
            side, places = low_side, (j, 3 + j, 5 + j if j else None)
        temp, ident, chip = places
        low = first_tile(sub, side(temp, first), side(ident, first))
        high = last_tile(
            sub, side(temp, last), side(ident, last), zero if chip is None else side(chip, last)
        )
        ya[q] = jnp.where(even_y, low, high)
        yb[q] = jnp.where(even_y, high, low)
        if chip is not None:
            place = PX + q - PAIRS
            tile = jnp.where(sub < 4, ya[place], pltpu.roll(side(chip, first), 4, 0))
            ya[place] = tile
            yb[place] = tile


def pick(ident, table):
    low = jnp.where(ident == 1, table[1], table[0])
    high = jnp.where(ident == 3, table[3], table[2])
    return jnp.where(ident >= 2, high, low)


def up_z(v):
    return pltpu.roll(v, NZ - 1, 1)


def down_z(v):
    return pltpu.roll(v, 1, 1)


def cells(temp, ident, chip, tables, inside=None):
    ref_ref, grad_ref, store_ref = tables
    conduct = pick(ident, ref_ref) * (
        1.0 + pick(ident, grad_ref) * jnp.tanh(temp - kelvin_shift_amount)
    )
    if inside is not None:
        conduct = conduct * inside
    lanes = lane(temp.shape)
    inner_z = jnp.where(lanes < NZ - 1, 1.0, 0.0).astype(f32)
    edge_z = jnp.where((lanes == 0) | (lanes == NZ - 1), 1.0, 0.0).astype(f32)
    e_z = (conduct + up_z(conduct)) * inner_z
    f_z = e_z * (up_z(temp) - temp)
    c_b = conduct * edge_z
    diag = (pick(ident, store_ref) + c_b) + (e_z + down_z(e_z))
    resid = (clock_advance * interface_warming_rate * chip - c_b * temp) + (f_z - down_z(f_z))
    return conduct, diag, resid, e_z


def surface(read, terms):
    rows = sublane((TILE, NZ))
    diagonal = sublane((NZ, NZ)) == lane((NZ, NZ))
    first = jnp.where(sublane((NZ, NZ)) == 0, 1.0, 0.0).astype(bf16)
    total = jnp.zeros((TILE, NZ), f32)
    for s in range(TILE):
        rest = read(s)
        line = jnp.zeros((NZ, NZ), f32)
        for _ in range(terms):
            part = rest.astype(bf16)
            line = line + jnp.dot(part, first, preferred_element_type=f32)
            rest = rest - part.astype(f32)
        line = jnp.sum(jnp.where(diagonal, line, 0.0), axis=0, keepdims=True)
        total = jnp.where(rows == s, line, total)
    return total


def own_rows(ref):
    per = NX // TILE
    return lambda s: jnp.concatenate([ref[per * s + i, :NY, :] for i in range(per)], axis=0)


def own_kernel(
    ref_ref,
    grad_ref,
    store_ref,
    t_hbm,
    id_hbm,
    chip_hbm,
    xa_ref,
    xb_ref,
    site_ref,
    tp,
    cp,
    dp,
    rp,
    ez,
    surf_ref,
    hot_ref,
    row_ref,
    lane_ref,
    t_ref,
    id_ref,
    chip_ref,
    sems,
):
    tables = (ref_ref, grad_ref, store_ref)
    ix = lax.axis_index("gx")
    iy = lax.axis_index("gy")

    copies = [
        pltpu.make_async_copy(src, dst, sems.at[k])
        for k, (src, dst) in enumerate(((t_hbm, t_ref), (id_hbm, id_ref), (chip_hbm, chip_ref)))
    ]
    for copy in copies:
        copy.start()

    width = NY * lax.axis_size("gy")
    subs = sublane((NZ, NZ))

    def places(b, _):
        site = site_ref[b]
        row = site // width
        col = site - row * width
        here = (col // NY) == iy
        cell = (row % NX) * NY + col % NY
        row_of = jnp.where(here, (row // NX) * TILE + cell // NZ, -1)
        row_ref[b] = row_of
        lane_ref[b] = cell % NZ
        for s in range(TILE):
            hit = subs == jnp.broadcast_to(row_of[s : s + 1], (NZ, NZ))
            hot_ref[b, :, NZ * s : NZ * (s + 1)] = jnp.where(hit, 1.0, 0.0).astype(bf16)
        return 0

    lax.fori_loop(0, site_ref.shape[0], places, 0, unroll=2)
    for copy in copies:
        copy.wait()

    def put(q, temp, ident, chip, inside=None):
        conduct, diag, resid, e_z = cells(temp, ident, chip, tables, inside)
        tp[q, :NY, :] = temp
        cp[q, :NY, :] = conduct
        dp[q, :NY, :] = diag
        rp[q, :NY, :] = resid
        ez[q, :NY, :] = e_z

    def own_plane(q, _):
        put(q, t_ref[q], id_ref[q], chip_ref[q].astype(f32))
        return 0

    lax.fori_loop(0, NX, own_plane, 0, unroll=4)

    even_x = lax.rem(ix, 2) == 0
    low_x = jnp.where(ix > 0, 1.0, 0.0).astype(f32)
    high_x = jnp.where(ix < lax.axis_size("gx") - 1, 1.0, 0.0).astype(f32)
    zero_plane = jnp.zeros((NY, NZ), f32)

    def high_plane(k):
        return jnp.where(even_x, xb_ref[k], xa_ref[k])

    def low_plane(k):
        return jnp.where(even_x, xa_ref[k], xb_ref[k])

    for k in range(HIGH):
        chip = high_plane(8 + k) if k < 3 else zero_plane
        put(NX + k, high_plane(k), high_plane(4 + k), chip, high_x)
    for k in range(LOW):
        chip = low_plane(5 + k) if k > 0 else zero_plane
        put(NX + HIGH + k, low_plane(k), low_plane(3 + k), chip, low_x)

    surf_ref[...] = surface(own_rows(t_ref), 3)


def krylov_kernel(
    ref_ref,
    grad_ref,
    store_ref,
    tp_in,
    cp_in,
    dp_in,
    rp_in,
    ez_in,
    surf_ref,
    ya_ref,
    yb_ref,
    tp,
    cp,
    dp,
    rp,
    ez,
    w0_ref,
    w1_ref,
    w2_ref,
    send_ref,
    ex,
    ey,
    dinv,
):
    del tp_in, cp_in, dp_in, rp_in, ez_in
    tables = (ref_ref, grad_ref, store_ref)
    ix = lax.axis_index("gx")
    iy = lax.axis_index("gy")
    last_x = lax.axis_size("gx") - 1
    last_y = lax.axis_size("gy") - 1
    sub = sublane((TILE, NZ))
    one = jnp.ones((), f32)
    low_x = jnp.where(ix > 0, 1.0, 0.0).astype(f32)
    high_x = jnp.where(ix < last_x, 1.0, 0.0).astype(f32)
    low_y = jnp.where(iy > 0, 1.0, 0.0).astype(f32)
    high_y = jnp.where(iy < last_y, 1.0, 0.0).astype(f32)
    rows_halo = jnp.where(sub < 4, high_y, low_y)

    even_y = lax.rem(iy, 2) == 0

    def high_row(q):
        return jnp.where(even_y, yb_ref[q], ya_ref[q])

    def low_row(q):
        return jnp.where(even_y, ya_ref[q], yb_ref[q])

    def put_halo(q, chip_high, plane_in):
        high = high_row(q)
        low = low_row(q)
        temp = jnp.where(sub < 4, high, low)
        ident = jnp.where(sub < 4, pltpu.roll(high, 4, 0), pltpu.roll(low, 3, 0))
        chip = jnp.where(sub < 4, chip_high, pltpu.roll(low, 6, 0))
        conduct, diag, resid, e_z = cells(temp, ident, chip, tables, rows_halo * plane_in)
        tp[q, NY:, :] = temp
        cp[q, NY:, :] = conduct
        dp[q, NY:, :] = diag
        rp[q, NY:, :] = resid
        ez[q, NY:, :] = e_z

    def own_halo_first(q, _):
        put_halo(q, high_row(PX + q), one)
        return 0

    def own_halo_second(q, _):
        put_halo(q, pltpu.roll(high_row(PX + q - PAIRS), 4, 0), one)
        return 0

    lax.fori_loop(0, PAIRS, own_halo_first, 0, unroll=20)
    lax.fori_loop(PAIRS, NX, own_halo_second, 0, unroll=12)

    zero_tile = jnp.zeros((TILE, NZ), f32)
    for q in range(NX, PX):
        put_halo(q, pltpu.roll(high_row(PX + q - PAIRS), 4, 0), high_x if q < NX + HIGH else low_x)

    subs = sublane((PY, NZ))
    rows_in = jnp.where(subs < NY, 1.0, jnp.where(subs < NY + 4, high_y, low_y)).astype(f32)

    def up_y(v):
        return pltpu.roll(v, PY - 1, 0)

    def down_y(v):
        return pltpu.roll(v, 1, 0)

    def fold(v):
        return (v[0:8] + v[8:16]) + (v[16:24] + v[24:32])

    def faces(q, nxt, ex_before, fx_before, plane_in):
        c0 = cp[q]
        t0 = tp[q]
        e_x = c0 + cp[nxt]
        f_x = e_x * (tp[nxt] - t0)
        e_y = c0 + up_y(c0)
        f_y = e_y * (up_y(t0) - t0)
        diag = dp[q] + ((e_x + ex_before) + (e_y + down_y(e_y)))
        inverse = (rows_in * plane_in) / diag
        resid = rp[q] + ((f_x - fx_before) + (f_y - down_y(f_y)))
        first = resid * inverse
        ex[q] = e_x
        ey[q] = e_y
        dinv[q] = inverse
        w0_ref[q] = first
        return e_x, f_x, resid, first

    e_first = cp[36] + cp[37]
    carry = (e_first, e_first * (tp[37] - tp[36]))
    for q, nxt in ((37, 38), (38, 0)):
        carry = faces(q, nxt, carry[0], carry[1], low_x)[:2]

    def faces_own(q, state):
        e_b, f_b, m0 = state
        e_x, f_x, resid, first = faces(q, q + 1, e_b, f_b, one)
        return e_x, f_x, m0 + fold(resid[:NY] * first[:NY])

    e_b, f_b, m0 = lax.fori_loop(0, NX, faces_own, (carry[0], carry[1], zero_tile), unroll=16)
    carry = (e_b, f_b)
    for q in (32, 33, 34):
        carry = faces(q, q + 1, carry[0], carry[1], high_x)[:2]

    def neighbours(src, q, nxt, g_before):
        v = src[q]
        e_x = ex[q]
        e_y = ey[q]
        e_z = ez[q]
        total = (e_x * src[nxt] + g_before) + (
            (e_y * up_y(v) + down_y(e_y * v)) + (e_z * up_z(v) + down_z(e_z * v))
        )
        return total, v, e_x * v

    def advance(src, dst, before, prologue, epilogue):
        carry = ex[before] * src[before]
        for q, nxt in prologue:
            total, _, carry = neighbours(src, q, nxt, carry)
            dst[q] = dinv[q] * total

        def step(q, state):
            g, ma, mb = state
            total, v, g = neighbours(src, q, q + 1, g)
            new = dinv[q] * total
            dst[q] = new
            ma = ma + fold(total[:NY] * v[:NY])
            mb = mb + fold(total[:NY] * new[:NY])
            return g, ma, mb

        carry, ma, mb = lax.fori_loop(0, NX, step, (carry, zero_tile, zero_tile), unroll=8)
        for q, nxt in epilogue:
            total, _, carry = neighbours(src, q, nxt, carry)
            dst[q] = dinv[q] * total
        return ma, mb

    m1, m2 = advance(w0_ref, w1_ref, 37, ((38, 0),), ((32, 33), (33, 34)))

    def crossing(q, v, after):
        half = ex[q] * after + (ey[q] * up_y(v) + ez[q] * up_z(v))
        return fold(half[:NY] * v[:NY])

    def second(q, g):
        total, v, g = neighbours(w1_ref, q, q + 1, g)
        new = dinv[q] * total
        w2_ref[q] = new
        return g, new, fold(total[:NY] * v[:NY]), fold(total[:NY] * new[:NY])

    g, before, m3, m4 = second(0, ex[38] * w1_ref[38])

    def step_2(q, state):
        g, before, ma, mb, mc = state
        g, new, a, b = second(q, g)
        return g, new, ma + a, mb + b, mc + crossing(q - 1, before, new)

    g, before, m3, m4, m5 = lax.fori_loop(
        1, NX, step_2, (g, before, m3, m4, zero_tile), unroll=31
    )
    total, _, _ = neighbours(w1_ref, NX, NX + 1, g)
    m5 = m5 + crossing(NX - 1, before, dinv[NX] * total)
    m5 = m5 + m5

    moments = zero_tile
    for k, m in enumerate((m0, m1, m2, m3, m4, m5)):
        moments = jnp.where(sub == k, jnp.sum(m, axis=0, keepdims=True), moments)
    fields = [surf_ref[...]] + [surface(own_rows(w), 2) for w in (w0_ref, w1_ref, w2_ref)]
    for k in range(send_ref.shape[0]):
        for j, tile in enumerate((*fields, moments)):
            send_ref[k, TILE * j : TILE * (j + 1), :] = tile


def lookup_kernel(hot_ref, row_ref, lane_ref, table_ref, out_ref, parts):
    blocks = table_ref.shape[0]
    targets = hot_ref.shape[0]
    sub = sublane((TILE, NZ))
    zero = jnp.zeros((TILE, NZ), f32)
    fields = FIELDS - 1
    for f in range(fields):
        rest = jnp.concatenate(
            [table_ref[a, TILE * (f + 1) : TILE * (f + 2), :] for a in range(blocks)], axis=0
        ).T
        for k in range(2):
            part = rest.astype(bf16)
            parts[NZ * f : NZ * (f + 1), NZ * k : NZ * (k + 1)] = part
            rest = rest - part.astype(f32)

    total = table_ref[0, TILE * FIELDS :, :]
    for a in range(1, blocks):
        total = total + table_ref[a, TILE * FIELDS :, :]

    def one(b, _):
        row_of = row_ref[b]
        lane_of = lane_ref[b]
        found = [zero] * FIELDS
        for pair in range(0, TILE, 2):
            hot = hot_ref[b, :, NZ * pair : NZ * (pair + 2)]
            hot = jnp.concatenate([hot, hot], axis=0)
            lanes = [jnp.broadcast_to(lane_of[pair + i : pair + i + 1], (TILE, NZ)) for i in (0, 1)]
            offset = [e - sub for e in lanes]
            for i in (0, 1):
                rows = jnp.broadcast_to(row_of[pair + i : pair + i + 1], (TILE, NZ)) - sub
                acc = zero
                for a in range(blocks):
                    got = jnp.take_along_axis(table_ref[a, 0:TILE, :], lanes[i], axis=1)
                    acc = jnp.where(rows == a * TILE, got, acc)
                found[0] = jnp.where(
                    sub == pair + i, jnp.sum(acc, axis=0, keepdims=True), found[0]
                )
            for f in range(fields):
                line = jnp.dot(parts[NZ * f : NZ * (f + 1)], hot, preferred_element_type=f32)
                for i in (0, 1):
                    acc = zero
                    for t in range(NZ // TILE):
                        acc = jnp.where(
                            offset[i] == t * TILE,
                            line[TILE * t : TILE * (t + 1), NZ * i : NZ * (i + 1)],
                            acc,
                        )
                    found[f + 1] = jnp.where(
                        sub == pair + i, jnp.sum(acc, axis=0, keepdims=True), found[f + 1]
                    )
        for f in range(FIELDS):
            out_ref[b, TILE * f : TILE * (f + 1), :] = found[f]
        out_ref[b, TILE * FIELDS :, :] = total
        return 0

    lax.fori_loop(0, targets, one, 0, unroll=2)


def cg_coefficients(m):
    a = [m[j] - m[j + 1] for j in range(5)]

    def quadratic(v, h):
        total = None
        for i in range(3):
            for j in range(3):
                if v[i] is None or v[j] is None:
                    continue
                term = v[i] * v[j] * h[i + j]
                total = term if total is None else total + term
        return total

    def add(u, v):
        return v if u is None else u if v is None else u + v

    def scale(s, v):
        return [None if e is None else s * e for e in v]

    one = jnp.ones_like(m[0])
    z = [one, None, None]
    p = [one, None, None]
    rz = m[0]
    x = [None, None, None]
    for step in range(3):
        alpha = rz / quadratic(p, a)
        x = [add(e, g) for e, g in zip(x, scale(alpha, p))]
        if step < 2:
            ap = scale(alpha, p)
            moved = [None] + ap[:2]
            z = [
                add(add(z[i], None if ap[i] is None else -ap[i]), moved[i]) for i in range(3)
            ]
            new = quadratic(z, m)
            p = [add(z[i], e) for i, e in enumerate(scale(new / rz, p))]
            rz = new
    return x


def final_kernel(
    got_ref,
    pressure_hbm,
    t_ref,
    w0_ref,
    w1_ref,
    w2_ref,
    temp_hbm,
    growth_ref,
    pressure_ref,
    temp_ref,
    sem,
    out_sems,
):
    copy = pltpu.make_async_copy(pressure_hbm, pressure_ref, sem)
    copy.start()
    total = got_ref[0]
    for b in range(1, got_ref.shape[0]):
        total = total + got_ref[b]
    sums = jnp.sum(total[TILE * FIELDS :], axis=1, keepdims=True)
    m = [sums[k : k + 1] for k in range(6)]
    c = cg_coefficients(m)
    c_tile = [jnp.broadcast_to(e, (TILE, NZ)) for e in c]
    c_plane = [jnp.broadcast_to(e, (NY, NZ)) for e in c]

    def plane(q, _):
        temp_ref[q] = (
            t_ref[q, :NY, :]
            + c_plane[0] * w0_ref[q, :NY, :]
            + c_plane[1] * w1_ref[q, :NY, :]
            + c_plane[2] * w2_ref[q, :NY, :]
        )
        return 0

    outs = []
    step = NX // 4
    for k in range(4):
        lax.fori_loop(step * k, step * (k + 1), plane, 0, unroll=4)
        part = pl.ds(step * k, step)
        outs.append(pltpu.make_async_copy(temp_ref.at[part], temp_hbm.at[part], out_sems.at[k]))
        outs[-1].start()

    flank = total[0:TILE]
    for k in range(3):
        flank = flank + c_tile[k] * total[TILE * (k + 1) : TILE * (k + 2)]
    soft = jnp.maximum(flank, 0.0) + jnp.log1p(jnp.exp(-jnp.abs(flank)))
    copy.wait()
    growth_ref[...] = usui_rate * pressure_ref[...] * jnp.exp(-usui_energy / (1.0 + soft))
    for out in outs:
        out.wait()


def local(
    prior_kelvin_state,
    substance_identifier,
    chip_touch_indicator,
    substance_reference_diffusivity,
    substance_diffusivity_gradient,
    substance_storage_coefficient,
    clearance_point_indices,
    clearance_face_pressure,
):
    size_x = lax.axis_size("gx")
    size_y = lax.axis_size("gy")
    temp, ident, chip = prior_kelvin_state, substance_identifier, chip_touch_indicator
    vmem = pl.BlockSpec(memory_space=pltpu.VMEM)
    smem = pl.BlockSpec(memory_space=pltpu.SMEM)

    def params(mib):
        return pltpu.CompilerParams(vmem_limit_bytes=mib * MIB)


    anywhere = pl.BlockSpec(memory_space=pltpu.HBM)

    def arr(*shape, dtype=f32):
        return jax.ShapeDtypeStruct(shape, dtype)

    def buf(*shape, dtype=f32):
        return pltpu.VMEM(shape, dtype)

    def in_hbm(*arrays):
        return [pltpu.with_memory_space_constraint(a, pltpu.HBM) for a in arrays]

    i32 = jnp.int32
    xa, xb, ya, yb, sites = pl.pallas_call(
        pack_kernel,
        name="pack",
        in_specs=[anywhere] * 4,
        out_specs=[vmem] * 5,
        out_shape=[
            arr(11, NY, NZ),
            arr(11, NY, NZ),
            arr(PX + PAIRS, TILE, NZ),
            arr(PX + PAIRS, TILE, NZ),
            arr(size_y, TILE, NZ, dtype=i32),
        ],
        scratch_shapes=[
            buf(NX, TILE, NZ),
            buf(NX, TILE, NZ),
            buf(NX, TILE, NZ, dtype=i32),
            buf(NX, TILE, NZ, dtype=i32),
            buf(NX, TILE, NZ, dtype=i32),
            buf(NX, TILE, NZ, dtype=i32),
            buf(HIGH, NY, NZ),
            buf(HIGH, NY, NZ),
            buf(HIGH, NY, NZ, dtype=i32),
            buf(HIGH, NY, NZ, dtype=i32),
            buf(HIGH, NY, NZ, dtype=i32),
            buf(HIGH, NY, NZ, dtype=i32),
            buf(TILE, NZ, dtype=i32),
            pltpu.SemaphoreType.DMA((13,)),
        ],
        compiler_params=params(10),
    )(*in_hbm(temp, ident, chip, clearance_point_indices.reshape(TILE, NZ)))
    sites = lax.all_to_all(sites, "gy", 0, 0)

    xa = lax.ppermute(xa, "gx", swaps(size_x, 1))
    xb = lax.ppermute(xb, "gx", swaps(size_x, 0))
    ya, yb, sites = pl.pallas_call(
        corner_kernel,
        name="corners",
        in_specs=[vmem] * 5,
        out_specs=[vmem] * 3,
        out_shape=[
            arr(PX + PAIRS, TILE, NZ),
            arr(PX + PAIRS, TILE, NZ),
            arr(size_y, TILE, NZ, dtype=i32),
        ],
        input_output_aliases={0: 0, 1: 1, 4: 2},
        compiler_params=params(8),
    )(ya, yb, xa, xb, sites)
    ya = lax.ppermute(ya, "gy", swaps(size_y, 1))
    yb = lax.ppermute(yb, "gy", swaps(size_y, 0))

    tables = (
        substance_reference_diffusivity,
        substance_diffusivity_gradient,
        substance_storage_coefficient,
    )
    padded = arr(PX, PY, NZ)
    *own, hot, row, place = pl.pallas_call(
        own_kernel,
        name="own_cells",
        in_specs=[smem] * 3 + [anywhere] * 3 + [vmem] * 3,
        out_specs=[vmem] * 9,
        out_shape=[padded] * 5
        + [
            arr(TILE, NZ),
            arr(size_y, NZ, TILE * NZ, dtype=bf16),
            arr(size_y, TILE, NZ, dtype=i32),
            arr(size_y, TILE, NZ, dtype=i32),
        ],
        scratch_shapes=[
            buf(NX, NY, NZ),
            buf(NX, NY, NZ, dtype=i32),
            buf(NX, NY, NZ, dtype=i32),
            pltpu.SemaphoreType.DMA((3,)),
        ],
        compiler_params=params(14),
    )(*tables, *in_hbm(temp, ident, chip), xa, xb, sites)

    payload = TILE * (FIELDS + 1)
    start, _, _, _, _, w0, w1, w2, send = pl.pallas_call(
        krylov_kernel,
        name="krylov",
        in_specs=[smem] * 3 + [vmem] * 8,
        out_specs=[vmem] * 9,
        out_shape=[padded] * 8 + [arr(size_x, payload, NZ)],
        input_output_aliases={3: 0, 4: 1, 5: 2, 6: 3, 7: 4},
        scratch_shapes=[buf(PX, PY, NZ)] * 3,
        compiler_params=params(24),
    )(*tables, *own, ya, yb)
    table = lax.all_to_all(send, "gx", 0, 0)
    found = pl.pallas_call(
        lookup_kernel,
        name="lookup",
        in_specs=[vmem] * 4,
        out_specs=vmem,
        out_shape=arr(size_y, payload, NZ),
        scratch_shapes=[buf(NZ * (FIELDS - 1), 2 * NZ, dtype=bf16)],
        compiler_params=params(20),
    )(hot, row, place, table)
    got = lax.all_to_all(found, "gy", 0, 0)
    temperature, growth = pl.pallas_call(
        final_kernel,
        name="finish",
        in_specs=[vmem, anywhere, vmem, vmem, vmem, vmem],
        out_specs=[anywhere, vmem],
        out_shape=[arr(NX, NY, NZ), arr(TILE, NZ)],
        scratch_shapes=[
            buf(TILE, NZ),
            buf(NX, NY, NZ),
            pltpu.SemaphoreType.DMA(()),
            pltpu.SemaphoreType.DMA((4,)),
        ],
        compiler_params=params(12),
    )(got, *in_hbm(clearance_face_pressure.reshape(TILE, NZ)), start, w0, w1, w2)
    return temperature, growth.reshape(-1)


def solution(mesh):
    in_specs = (
        P("gx", "gy", None),
        P("gx", "gy", None),
        P("gx", "gy", None),
        P(),
        P(),
        P(),
        P(("gx", "gy")),
        P(("gx", "gy")),
    )
    out_specs = (P("gx", "gy", None), P(("gx", "gy")))
    return jax.shard_map(local, mesh=mesh, in_specs=in_specs, out_specs=out_specs, check_vma=False)
```

```python
import jax
import jax.numpy as jnp
from jax import lax
from jax.experimental import pallas as pl
from jax.experimental.pallas import tpu as pltpu
from jax.sharding import PartitionSpec as P

clock_advance = 2.0
interface_warming_rate = 3.0
usui_rate = 3.0
usui_energy = 4.0
kelvin_shift_amount = 2.0

LOW = 3
HIGH = 4
NX = 32
NY = 32
NZ = 128
PX = NX + HIGH + LOW
PY = NY + 8
FIELDS = 4
TILE = 8
PAIRS = 20
MIB = 1024 * 1024
f32 = jnp.float32
bf16 = jnp.bfloat16


def swaps(count, first):
    low = range(first, count - 1, 2)
    return [(i, i + 1) for i in low] + [(i + 1, i) for i in low]


def sublane(shape):
    return lax.broadcasted_iota(jnp.int32, shape, len(shape) - 2)


def lane(shape):
    return lax.broadcasted_iota(jnp.int32, shape, len(shape) - 1)


def first_tile(sub, temp, ident):
    return jnp.where(sub < 4, temp, pltpu.roll(ident, 4, 0))


def last_tile(sub, temp, ident, chip):
    return jnp.where(
        sub >= 5, temp, jnp.where(sub >= 2, pltpu.roll(ident, 5, 0), pltpu.roll(chip, 2, 0))
    )


def pack_kernel(
    t_hbm,
    id_hbm,
    chip_hbm,
    site_hbm,
    xa,
    xb,
    ya,
    yb,
    sites,
    t_a,
    t_b,
    i_a,
    i_b,
    c_a,
    c_b,
    t_p,
    t_m,
    i_p,
    i_m,
    c_p,
    c_m,
    site_ref,
    sems,
):
    copies = []
    for k, (src, dst) in enumerate(
        (
            (t_hbm.at[pl.ds(0, HIGH)], t_p),
            (id_hbm.at[pl.ds(0, HIGH)], i_p),
            (chip_hbm.at[pl.ds(0, HIGH)], c_p),
            (t_hbm.at[pl.ds(NX - HIGH, HIGH)], t_m),
            (id_hbm.at[pl.ds(NX - HIGH, HIGH)], i_m),
            (chip_hbm.at[pl.ds(NX - HIGH, HIGH)], c_m),
            (t_hbm.at[:, pl.ds(0, TILE)], t_a),
            (id_hbm.at[:, pl.ds(0, TILE)], i_a),
            (chip_hbm.at[:, pl.ds(0, TILE)], c_a),
            (t_hbm.at[:, pl.ds(NY - TILE, TILE)], t_b),
            (id_hbm.at[:, pl.ds(NY - TILE, TILE)], i_b),
            (chip_hbm.at[:, pl.ds(NY - TILE, TILE)], c_b),
            (site_hbm, site_ref),
        )
    ):
        copies.append(pltpu.make_async_copy(src, dst, sems.at[k]))
        copies[-1].start()
    for copy in copies:
        copy.wait()

    def x_sides(low, high):
        for k in range(HIGH):
            low[k] = t_p[k]
            low[4 + k] = i_p[k].astype(f32)
            if k < 3:
                low[8 + k] = c_p[k].astype(f32)
                high[k] = t_m[1 + k]
                high[3 + k] = i_m[1 + k].astype(f32)
            if k < 2:
                high[6 + k] = c_m[2 + k].astype(f32)

    even_x = lax.rem(lax.axis_index("gx"), 2) == 0
    even_y = lax.rem(lax.axis_index("gy"), 2) == 0

    @pl.when(even_x)
    def _():
        x_sides(xa, xb)

    @pl.when(jnp.logical_not(even_x))
    def _():
        x_sides(xb, xa)

    sub = sublane((TILE, NZ))

    def own(q, _):
        low = first_tile(sub, t_a[q], i_a[q].astype(f32))
        high = last_tile(sub, t_b[q], i_b[q].astype(f32), c_b[q].astype(f32))
        ya[q] = jnp.where(even_y, low, high)
        yb[q] = jnp.where(even_y, high, low)
        return 0

    lax.fori_loop(0, NX, own, 0, unroll=8)
    for j in range(PAIRS):
        tile = c_a[j].astype(f32)
        if j + PAIRS < NX:
            tile = jnp.where(sub < 4, tile, pltpu.roll(c_a[j + PAIRS].astype(f32), 4, 0))
        ya[PX + j] = tile
        yb[PX + j] = tile
    for k in range(sites.shape[0]):
        sites[k] = site_ref[...]


def corner_kernel(ya_in, yb_in, xa_ref, xb_ref, sites_in, ya, yb, sites_out):
    del ya_in, yb_in, sites_in, sites_out
    even_x = lax.rem(lax.axis_index("gx"), 2) == 0
    even_y = lax.rem(lax.axis_index("gy"), 2) == 0
    sub = sublane((TILE, NZ))
    zero = jnp.zeros((TILE, NZ), f32)
    first = pl.ds(0, TILE)
    last = pl.ds(NY - TILE, TILE)

    def high_side(k, rows):
        return jnp.where(even_x, xb_ref[k, rows, :], xa_ref[k, rows, :])

    def low_side(k, rows):
        return jnp.where(even_x, xa_ref[k, rows, :], xb_ref[k, rows, :])

    for k in range(HIGH + LOW):
        q = NX + k
        if k < HIGH:
            side, places = high_side, (k, 4 + k, 8 + k if k < 3 else None)
        else:
            j = k - HIGH
            side, places = low_side, (j, 3 + j, 5 + j if j else None)
        temp, ident, chip = places
        low = first_tile(sub, side(temp, first), side(ident, first))
        high = last_tile(
            sub, side(temp, last), side(ident, last), zero if chip is None else side(chip, last)
        )
        ya[q] = jnp.where(even_y, low, high)
        yb[q] = jnp.where(even_y, high, low)
        if chip is not None:
            place = PX + q - PAIRS
            tile = jnp.where(sub < 4, ya[place], pltpu.roll(side(chip, first), 4, 0))
            ya[place] = tile
            yb[place] = tile


def pick(ident, table):
    low = jnp.where(ident == 1, table(1), table(0))
    high = jnp.where(ident == 3, table(3), table(2))
    return jnp.where(ident >= 2, high, low)


def up_z(v):
    return pltpu.roll(v, NZ - 1, 1)


def down_z(v):
    return pltpu.roll(v, 1, 1)


def cells(temp, ident, chip, tables, inside=None):
    ref_ref, grad_ref, store_ref = tables
    conduct = pick(ident, ref_ref) * (
        1.0 + pick(ident, grad_ref) * jnp.tanh(temp - kelvin_shift_amount)
    )
    if inside is not None:
        conduct = conduct * inside
    lanes = lane(temp.shape)
    inner_z = jnp.where(lanes < NZ - 1, 1.0, 0.0).astype(f32)
    edge_z = jnp.where((lanes == 0) | (lanes == NZ - 1), 1.0, 0.0).astype(f32)
    e_z = (conduct + up_z(conduct)) * inner_z
    f_z = e_z * (up_z(temp) - temp)
    c_b = conduct * edge_z
    diag = (pick(ident, store_ref) + c_b) + (e_z + down_z(e_z))
    resid = (clock_advance * interface_warming_rate * chip - c_b * temp) + (f_z - down_z(f_z))
    return conduct, diag, resid, e_z


def surface(read, terms):
    rows = sublane((TILE, NZ))
    diagonal = sublane((NZ, NZ)) == lane((NZ, NZ))
    first = jnp.where(sublane((NZ, NZ)) == 0, 1.0, 0.0).astype(bf16)
    total = jnp.zeros((TILE, NZ), f32)
    for s in range(TILE):
        rest = read(s)
        line = jnp.zeros((NZ, NZ), f32)
        for _ in range(terms):
            part = rest.astype(bf16)
            line = line + jnp.dot(part, first, preferred_element_type=f32)
            rest = rest - part.astype(f32)
        line = jnp.sum(jnp.where(diagonal, line, 0.0), axis=0, keepdims=True)
        total = jnp.where(rows == s, line, total)
    return total


def own_rows(ref):
    per = NX // TILE
    return lambda s: jnp.concatenate([ref[per * s + i, :NY, :] for i in range(per)], axis=0)


def own_kernel(
    ref_hbm,
    grad_hbm,
    store_hbm,
    t_hbm,
    id_hbm,
    chip_hbm,
    xa_ref,
    xb_ref,
    site_ref,
    tp,
    cp,
    dp,
    rp,
    ez,
    surf_ref,
    hot_ref,
    row_ref,
    lane_ref,
    table_ref,
    t_ref,
    id_ref,
    chip_ref,
    ref_ref,
    grad_ref,
    store_ref,
    sems,
):
    ix = lax.axis_index("gx")
    iy = lax.axis_index("gy")

    copies = [
        pltpu.make_async_copy(src, dst, sems.at[k])
        for k, (src, dst) in enumerate(
            (
                (ref_hbm, ref_ref),
                (grad_hbm, grad_ref),
                (store_hbm, store_ref),
                (t_hbm, t_ref),
                (id_hbm, id_ref),
                (chip_hbm, chip_ref),
            )
        )
    ]
    for copy in copies:
        copy.start()

    width = NY * lax.axis_size("gy")
    subs = sublane((NZ, NZ))

    def places(b, _):
        site = site_ref[b]
        row = site // width
        col = site - row * width
        here = (col // NY) == iy
        cell = (row % NX) * NY + col % NY
        row_of = jnp.where(here, (row // NX) * TILE + cell // NZ, -1)
        row_ref[b] = row_of
        lane_ref[b] = cell % NZ
        for s in range(TILE):
            hit = subs == jnp.broadcast_to(row_of[s : s + 1], (NZ, NZ))
            hot_ref[b, :, NZ * s : NZ * (s + 1)] = jnp.where(hit, 1.0, 0.0).astype(bf16)
        return 0

    lax.fori_loop(0, site_ref.shape[0], places, 0, unroll=2)
    for copy in copies:
        copy.wait()

    tables = [lambda k, ref=ref: ref[k] for ref in (ref_ref, grad_ref, store_ref)]
    for j, table in enumerate(tables):
        for k in range(4):
            table_ref[4 * j + k] = jnp.full((TILE, NZ), table(k), f32)

    def put(q, temp, ident, chip, inside=None):
        conduct, diag, resid, e_z = cells(temp, ident, chip, tables, inside)
        tp[q, :NY, :] = temp
        cp[q, :NY, :] = conduct
        dp[q, :NY, :] = diag
        rp[q, :NY, :] = resid
        ez[q, :NY, :] = e_z

    def own_plane(q, _):
        put(q, t_ref[q], id_ref[q], chip_ref[q].astype(f32))
        return 0

    lax.fori_loop(0, NX, own_plane, 0, unroll=4)

    even_x = lax.rem(ix, 2) == 0
    low_x = jnp.where(ix > 0, 1.0, 0.0).astype(f32)
    high_x = jnp.where(ix < lax.axis_size("gx") - 1, 1.0, 0.0).astype(f32)
    zero_plane = jnp.zeros((NY, NZ), f32)

    def high_plane(k):
        return jnp.where(even_x, xb_ref[k], xa_ref[k])

    def low_plane(k):
        return jnp.where(even_x, xa_ref[k], xb_ref[k])

    for k in range(HIGH):
        chip = high_plane(8 + k) if k < 3 else zero_plane
        put(NX + k, high_plane(k), high_plane(4 + k), chip, high_x)
    for k in range(LOW):
        chip = low_plane(5 + k) if k > 0 else zero_plane
        put(NX + HIGH + k, low_plane(k), low_plane(3 + k), chip, low_x)

    surf_ref[...] = surface(own_rows(t_ref), 3)


def krylov_kernel(
    table_ref,
    tp_in,
    cp_in,
    dp_in,
    rp_in,
    ez_in,
    surf_ref,
    ya_ref,
    yb_ref,
    tp,
    cp,
    dp,
    rp,
    ez,
    w0_ref,
    w1_ref,
    w2_ref,
    send_ref,
    ex,
    ey,
    dinv,
):
    del tp_in, cp_in, dp_in, rp_in, ez_in
    tables = [lambda k, j=j: table_ref[4 * j + k] for j in range(3)]
    ix = lax.axis_index("gx")
    iy = lax.axis_index("gy")
    last_x = lax.axis_size("gx") - 1
    last_y = lax.axis_size("gy") - 1
    sub = sublane((TILE, NZ))
    one = jnp.ones((), f32)
    low_x = jnp.where(ix > 0, 1.0, 0.0).astype(f32)
    high_x = jnp.where(ix < last_x, 1.0, 0.0).astype(f32)
    low_y = jnp.where(iy > 0, 1.0, 0.0).astype(f32)
    high_y = jnp.where(iy < last_y, 1.0, 0.0).astype(f32)
    rows_halo = jnp.where(sub < 4, high_y, low_y)

    even_y = lax.rem(iy, 2) == 0

    def high_row(q):
        return jnp.where(even_y, yb_ref[q], ya_ref[q])

    def low_row(q):
        return jnp.where(even_y, ya_ref[q], yb_ref[q])

    def put_halo(q, chip_high, plane_in):
        high = high_row(q)
        low = low_row(q)
        temp = jnp.where(sub < 4, high, low)
        ident = jnp.where(sub < 4, pltpu.roll(high, 4, 0), pltpu.roll(low, 3, 0))
        chip = jnp.where(sub < 4, chip_high, pltpu.roll(low, 6, 0))
        conduct, diag, resid, e_z = cells(temp, ident, chip, tables, rows_halo * plane_in)
        tp[q, NY:, :] = temp
        cp[q, NY:, :] = conduct
        dp[q, NY:, :] = diag
        rp[q, NY:, :] = resid
        ez[q, NY:, :] = e_z

    def own_halo_first(q, _):
        put_halo(q, high_row(PX + q), one)
        return 0

    def own_halo_second(q, _):
        put_halo(q, pltpu.roll(high_row(PX + q - PAIRS), 4, 0), one)
        return 0

    lax.fori_loop(0, PAIRS, own_halo_first, 0, unroll=20)
    lax.fori_loop(PAIRS, NX, own_halo_second, 0, unroll=12)

    zero_tile = jnp.zeros((TILE, NZ), f32)
    for q in range(NX, PX):
        put_halo(q, pltpu.roll(high_row(PX + q - PAIRS), 4, 0), high_x if q < NX + HIGH else low_x)

    subs = sublane((PY, NZ))
    rows_in = jnp.where(subs < NY, 1.0, jnp.where(subs < NY + 4, high_y, low_y)).astype(f32)

    def up_y(v):
        return pltpu.roll(v, PY - 1, 0)

    def down_y(v):
        return pltpu.roll(v, 1, 0)

    def fold(v):
        return (v[0:8] + v[8:16]) + (v[16:24] + v[24:32])

    def faces(q, nxt, ex_before, fx_before, plane_in):
        c0 = cp[q]
        t0 = tp[q]
        e_x = c0 + cp[nxt]
        f_x = e_x * (tp[nxt] - t0)
        e_y = c0 + up_y(c0)
        f_y = e_y * (up_y(t0) - t0)
        diag = dp[q] + ((e_x + ex_before) + (e_y + down_y(e_y)))
        inverse = (rows_in * plane_in) / diag
        resid = rp[q] + ((f_x - fx_before) + (f_y - down_y(f_y)))
        first = resid * inverse
        ex[q] = e_x
        ey[q] = e_y
        dinv[q] = inverse
        w0_ref[q] = first
        return e_x, f_x, resid, first

    e_first = cp[36] + cp[37]
    carry = (e_first, e_first * (tp[37] - tp[36]))
    for q, nxt in ((37, 38), (38, 0)):
        carry = faces(q, nxt, carry[0], carry[1], low_x)[:2]

    def faces_own(q, state):
        e_b, f_b, m0 = state
        e_x, f_x, resid, first = faces(q, q + 1, e_b, f_b, one)
        return e_x, f_x, m0 + fold(resid[:NY] * first[:NY])

    e_b, f_b, m0 = lax.fori_loop(0, NX, faces_own, (carry[0], carry[1], zero_tile), unroll=16)
    carry = (e_b, f_b)
    for q in (32, 33, 34):
        carry = faces(q, q + 1, carry[0], carry[1], high_x)[:2]

    def neighbours(src, q, nxt, g_before):
        v = src[q]
        e_x = ex[q]
        e_y = ey[q]
        e_z = ez[q]
        total = (e_x * src[nxt] + g_before) + (
            (e_y * up_y(v) + down_y(e_y * v)) + (e_z * up_z(v) + down_z(e_z * v))
        )
        return total, v, e_x * v

    def advance(src, dst, before, prologue, epilogue):
        carry = ex[before] * src[before]
        for q, nxt in prologue:
            total, _, carry = neighbours(src, q, nxt, carry)
            dst[q] = dinv[q] * total

        def step(q, state):
            g, ma, mb = state
            total, v, g = neighbours(src, q, q + 1, g)
            new = dinv[q] * total
            dst[q] = new
            ma = ma + fold(total[:NY] * v[:NY])
            mb = mb + fold(total[:NY] * new[:NY])
            return g, ma, mb

        carry, ma, mb = lax.fori_loop(0, NX, step, (carry, zero_tile, zero_tile), unroll=8)
        for q, nxt in epilogue:
            total, _, carry = neighbours(src, q, nxt, carry)
            dst[q] = dinv[q] * total
        return ma, mb

    m1, m2 = advance(w0_ref, w1_ref, 37, ((38, 0),), ((32, 33), (33, 34)))

    def crossing(q, v, after):
        half = ex[q] * after + (ey[q] * up_y(v) + ez[q] * up_z(v))
        return fold(half[:NY] * v[:NY])

    def second(q, g):
        total, v, g = neighbours(w1_ref, q, q + 1, g)
        new = dinv[q] * total
        w2_ref[q] = new
        return g, new, fold(total[:NY] * v[:NY]), fold(total[:NY] * new[:NY])

    g, before, m3, m4 = second(0, ex[38] * w1_ref[38])

    def step_2(q, state):
        g, before, ma, mb, mc = state
        g, new, a, b = second(q, g)
        return g, new, ma + a, mb + b, mc + crossing(q - 1, before, new)

    g, before, m3, m4, m5 = lax.fori_loop(
        1, NX, step_2, (g, before, m3, m4, zero_tile), unroll=31
    )
    total, _, _ = neighbours(w1_ref, NX, NX + 1, g)
    m5 = m5 + crossing(NX - 1, before, dinv[NX] * total)
    m5 = m5 + m5

    moments = zero_tile
    for k, m in enumerate((m0, m1, m2, m3, m4, m5)):
        moments = jnp.where(sub == k, jnp.sum(m, axis=0, keepdims=True), moments)
    fields = [surf_ref[...]] + [surface(own_rows(w), 2) for w in (w0_ref, w1_ref, w2_ref)]
    for k in range(send_ref.shape[0]):
        for j, tile in enumerate((*fields, moments)):
            send_ref[k, TILE * j : TILE * (j + 1), :] = tile


def lookup_kernel(hot_ref, row_ref, lane_ref, table_ref, out_ref, parts):
    blocks = table_ref.shape[0]
    targets = hot_ref.shape[0]
    sub = sublane((TILE, NZ))
    zero = jnp.zeros((TILE, NZ), f32)
    fields = FIELDS - 1
    for f in range(fields):
        rest = jnp.concatenate(
            [table_ref[a, TILE * (f + 1) : TILE * (f + 2), :] for a in range(blocks)], axis=0
        ).T
        for k in range(2):
            part = rest.astype(bf16)
            parts[NZ * f : NZ * (f + 1), NZ * k : NZ * (k + 1)] = part
            rest = rest - part.astype(f32)

    total = table_ref[0, TILE * FIELDS :, :]
    for a in range(1, blocks):
        total = total + table_ref[a, TILE * FIELDS :, :]

    def one(b, _):
        row_of = row_ref[b]
        lane_of = lane_ref[b]
        found = [zero] * FIELDS
        for pair in range(0, TILE, 2):
            hot = hot_ref[b, :, NZ * pair : NZ * (pair + 2)]
            hot = jnp.concatenate([hot, hot], axis=0)
            lanes = [jnp.broadcast_to(lane_of[pair + i : pair + i + 1], (TILE, NZ)) for i in (0, 1)]
            offset = [e - sub for e in lanes]
            for i in (0, 1):
                rows = jnp.broadcast_to(row_of[pair + i : pair + i + 1], (TILE, NZ)) - sub
                acc = zero
                for a in range(blocks):
                    got = jnp.take_along_axis(table_ref[a, 0:TILE, :], lanes[i], axis=1)
                    acc = jnp.where(rows == a * TILE, got, acc)
                found[0] = jnp.where(
                    sub == pair + i, jnp.sum(acc, axis=0, keepdims=True), found[0]
                )
            for f in range(fields):
                line = jnp.dot(parts[NZ * f : NZ * (f + 1)], hot, preferred_element_type=f32)
                for i in (0, 1):
                    acc = zero
                    for t in range(NZ // TILE):
                        acc = jnp.where(
                            offset[i] == t * TILE,
                            line[TILE * t : TILE * (t + 1), NZ * i : NZ * (i + 1)],
                            acc,
                        )
                    found[f + 1] = jnp.where(
                        sub == pair + i, jnp.sum(acc, axis=0, keepdims=True), found[f + 1]
                    )
        for f in range(FIELDS):
            out_ref[b, TILE * f : TILE * (f + 1), :] = found[f]
        out_ref[b, TILE * FIELDS :, :] = total
        return 0

    lax.fori_loop(0, targets, one, 0, unroll=2)


def cg_coefficients(m):
    a = [m[j] - m[j + 1] for j in range(5)]

    def quadratic(v, h):
        total = None
        for i in range(3):
            for j in range(3):
                if v[i] is None or v[j] is None:
                    continue
                term = v[i] * v[j] * h[i + j]
                total = term if total is None else total + term
        return total

    def add(u, v):
        return v if u is None else u if v is None else u + v

    def scale(s, v):
        return [None if e is None else s * e for e in v]

    one = jnp.ones_like(m[0])
    z = [one, None, None]
    p = [one, None, None]
    rz = m[0]
    x = [None, None, None]
    for step in range(3):
        alpha = rz / quadratic(p, a)
        x = [add(e, g) for e, g in zip(x, scale(alpha, p))]
        if step < 2:
            ap = scale(alpha, p)
            moved = [None] + ap[:2]
            z = [
                add(add(z[i], None if ap[i] is None else -ap[i]), moved[i]) for i in range(3)
            ]
            new = quadratic(z, m)
            p = [add(z[i], e) for i, e in enumerate(scale(new / rz, p))]
            rz = new
    return x


def final_kernel(
    got_ref,
    pressure_hbm,
    t_ref,
    w0_ref,
    w1_ref,
    w2_ref,
    temp_hbm,
    growth_ref,
    pressure_ref,
    temp_ref,
    sem,
    out_sems,
):
    copy = pltpu.make_async_copy(pressure_hbm, pressure_ref, sem)
    copy.start()
    total = got_ref[0]
    for b in range(1, got_ref.shape[0]):
        total = total + got_ref[b]
    sums = jnp.sum(total[TILE * FIELDS :], axis=1, keepdims=True)
    m = [sums[k : k + 1] for k in range(6)]
    c = cg_coefficients(m)
    c_tile = [jnp.broadcast_to(e, (TILE, NZ)) for e in c]
    c_plane = [jnp.broadcast_to(e, (NY, NZ)) for e in c]

    def plane(q, _):
        temp_ref[q] = (
            t_ref[q, :NY, :]
            + c_plane[0] * w0_ref[q, :NY, :]
            + c_plane[1] * w1_ref[q, :NY, :]
            + c_plane[2] * w2_ref[q, :NY, :]
        )
        return 0

    outs = []
    step = NX // 4
    for k in range(4):
        lax.fori_loop(step * k, step * (k + 1), plane, 0, unroll=4)
        part = pl.ds(step * k, step)
        outs.append(pltpu.make_async_copy(temp_ref.at[part], temp_hbm.at[part], out_sems.at[k]))
        outs[-1].start()

    flank = total[0:TILE]
    for k in range(3):
        flank = flank + c_tile[k] * total[TILE * (k + 1) : TILE * (k + 2)]
    soft = jnp.maximum(flank, 0.0) + jnp.log1p(jnp.exp(-jnp.abs(flank)))
    copy.wait()
    growth_ref[...] = usui_rate * pressure_ref[...] * jnp.exp(-usui_energy / (1.0 + soft))
    for out in outs:
        out.wait()


def local(
    prior_kelvin_state,
    substance_identifier,
    chip_touch_indicator,
    substance_reference_diffusivity,
    substance_diffusivity_gradient,
    substance_storage_coefficient,
    clearance_point_indices,
    clearance_face_pressure,
):
    size_x = lax.axis_size("gx")
    size_y = lax.axis_size("gy")
    temp, ident, chip = prior_kelvin_state, substance_identifier, chip_touch_indicator
    vmem = pl.BlockSpec(memory_space=pltpu.VMEM)

    def params(mib):
        return pltpu.CompilerParams(vmem_limit_bytes=mib * MIB)


    anywhere = pl.BlockSpec(memory_space=pltpu.HBM)

    def arr(*shape, dtype=f32):
        return jax.ShapeDtypeStruct(shape, dtype)

    def buf(*shape, dtype=f32):
        return pltpu.VMEM(shape, dtype)

    def in_hbm(*arrays):
        return [pltpu.with_memory_space_constraint(a, pltpu.HBM) for a in arrays]

    i32 = jnp.int32
    xa, xb, ya, yb, sites = pl.pallas_call(
        pack_kernel,
        name="pack",
        in_specs=[anywhere] * 4,
        out_specs=[vmem] * 5,
        out_shape=[
            arr(11, NY, NZ),
            arr(11, NY, NZ),
            arr(PX + PAIRS, TILE, NZ),
            arr(PX + PAIRS, TILE, NZ),
            arr(size_y, TILE, NZ, dtype=i32),
        ],
        scratch_shapes=[
            buf(NX, TILE, NZ),
            buf(NX, TILE, NZ),
            buf(NX, TILE, NZ, dtype=i32),
            buf(NX, TILE, NZ, dtype=i32),
            buf(NX, TILE, NZ, dtype=i32),
            buf(NX, TILE, NZ, dtype=i32),
            buf(HIGH, NY, NZ),
            buf(HIGH, NY, NZ),
            buf(HIGH, NY, NZ, dtype=i32),
            buf(HIGH, NY, NZ, dtype=i32),
            buf(HIGH, NY, NZ, dtype=i32),
            buf(HIGH, NY, NZ, dtype=i32),
            buf(TILE, NZ, dtype=i32),
            pltpu.SemaphoreType.DMA((13,)),
        ],
        compiler_params=params(10),
    )(*in_hbm(temp, ident, chip, clearance_point_indices.reshape(TILE, NZ)))
    sites = lax.all_to_all(sites, "gy", 0, 0)

    xa = lax.ppermute(xa, "gx", swaps(size_x, 1))
    xb = lax.ppermute(xb, "gx", swaps(size_x, 0))
    ya, yb, sites = pl.pallas_call(
        corner_kernel,
        name="corners",
        in_specs=[vmem] * 5,
        out_specs=[vmem] * 3,
        out_shape=[
            arr(PX + PAIRS, TILE, NZ),
            arr(PX + PAIRS, TILE, NZ),
            arr(size_y, TILE, NZ, dtype=i32),
        ],
        input_output_aliases={0: 0, 1: 1, 4: 2},
        compiler_params=params(8),
    )(ya, yb, xa, xb, sites)
    ya = lax.ppermute(ya, "gy", swaps(size_y, 1))
    yb = lax.ppermute(yb, "gy", swaps(size_y, 0))

    tables = (
        substance_reference_diffusivity,
        substance_diffusivity_gradient,
        substance_storage_coefficient,
    )
    padded = arr(PX, PY, NZ)
    *own, hot, row, place, table_tiles = pl.pallas_call(
        own_kernel,
        name="own_cells",
        in_specs=[anywhere] * 6 + [vmem] * 3,
        out_specs=[vmem] * 10,
        out_shape=[padded] * 5
        + [
            arr(TILE, NZ),
            arr(size_y, NZ, TILE * NZ, dtype=bf16),
            arr(size_y, TILE, NZ, dtype=i32),
            arr(size_y, TILE, NZ, dtype=i32),
            arr(12, TILE, NZ),
        ],
        scratch_shapes=[
            buf(NX, NY, NZ),
            buf(NX, NY, NZ, dtype=i32),
            buf(NX, NY, NZ, dtype=i32),
            pltpu.SMEM((4,), f32),
            pltpu.SMEM((4,), f32),
            pltpu.SMEM((4,), f32),
            pltpu.SemaphoreType.DMA((6,)),
        ],
        compiler_params=params(14),
    )(*in_hbm(*tables, temp, ident, chip), xa, xb, sites)

    payload = TILE * (FIELDS + 1)
    start, _, _, _, _, w0, w1, w2, send = pl.pallas_call(
        krylov_kernel,
        name="krylov",
        in_specs=[vmem] * 9,
        out_specs=[vmem] * 9,
        out_shape=[padded] * 8 + [arr(size_x, payload, NZ)],
        input_output_aliases={1: 0, 2: 1, 3: 2, 4: 3, 5: 4},
        scratch_shapes=[buf(PX, PY, NZ)] * 3,
        compiler_params=params(24),
    )(table_tiles, *own, ya, yb)
    table = lax.all_to_all(send, "gx", 0, 0)
    found = pl.pallas_call(
        lookup_kernel,
        name="lookup",
        in_specs=[vmem] * 4,
        out_specs=vmem,
        out_shape=arr(size_y, payload, NZ),
        scratch_shapes=[buf(NZ * (FIELDS - 1), 2 * NZ, dtype=bf16)],
        compiler_params=params(20),
    )(hot, row, place, table)
    got = lax.all_to_all(found, "gy", 0, 0)
    temperature, growth = pl.pallas_call(
        final_kernel,
        name="finish",
        in_specs=[vmem, anywhere, vmem, vmem, vmem, vmem],
        out_specs=[anywhere, vmem],
        out_shape=[arr(NX, NY, NZ), arr(TILE, NZ)],
        scratch_shapes=[
            buf(TILE, NZ),
            buf(NX, NY, NZ),
            pltpu.SemaphoreType.DMA(()),
            pltpu.SemaphoreType.DMA((4,)),
        ],
        compiler_params=params(12),
    )(got, *in_hbm(clearance_face_pressure.reshape(TILE, NZ)), start, w0, w1, w2)
    return temperature, growth.reshape(-1)


def solution(mesh):
    in_specs = (
        P("gx", "gy", None),
        P("gx", "gy", None),
        P("gx", "gy", None),
        P(),
        P(),
        P(),
        P(("gx", "gy")),
        P(("gx", "gy")),
    )
    out_specs = (P("gx", "gy", None), P(("gx", "gy")))
    return jax.shard_map(local, mesh=mesh, in_specs=in_specs, out_specs=out_specs, check_vma=False)
```

```python
import jax
import jax.numpy as jnp
from jax import lax
from jax.experimental import pallas as pl
from jax.experimental.pallas import tpu as pltpu
from jax.sharding import PartitionSpec as P

clock_advance = 2.0
interface_warming_rate = 3.0
usui_rate = 3.0
usui_energy = 4.0
kelvin_shift_amount = 2.0

LOW = 3
HIGH = 4
NX = 32
NY = 32
NZ = 128
PX = NX + HIGH + LOW
PY = NY + 8
FIELDS = 4
TILE = 8
HALF = 4
BLOCK = 2 * FIELDS + 1
PAIRS = 20
MIB = 1024 * 1024
f32 = jnp.float32
bf16 = jnp.bfloat16


def swaps(count, first):
    low = range(first, count - 1, 2)
    return [(i, i + 1) for i in low] + [(i + 1, i) for i in low]


def sublane(shape):
    return lax.broadcasted_iota(jnp.int32, shape, len(shape) - 2)


def lane(shape):
    return lax.broadcasted_iota(jnp.int32, shape, len(shape) - 1)


def first_tile(sub, temp, ident):
    return jnp.where(sub < 4, temp, pltpu.roll(ident, 4, 0))


def last_tile(sub, temp, ident, chip):
    return jnp.where(
        sub >= 5, temp, jnp.where(sub >= 2, pltpu.roll(ident, 5, 0), pltpu.roll(chip, 2, 0))
    )


def pack_kernel(
    t_hbm,
    id_hbm,
    chip_hbm,
    site_hbm,
    xa,
    xb,
    ya,
    yb,
    sites,
    t_a,
    t_b,
    i_a,
    i_b,
    c_a,
    c_b,
    t_p,
    t_m,
    i_p,
    i_m,
    c_p,
    c_m,
    site_ref,
    sems,
):
    copies = []
    for k, (src, dst) in enumerate(
        (
            (t_hbm.at[pl.ds(0, HIGH)], t_p),
            (id_hbm.at[pl.ds(0, HIGH)], i_p),
            (chip_hbm.at[pl.ds(0, HIGH)], c_p),
            (t_hbm.at[pl.ds(NX - HIGH, HIGH)], t_m),
            (id_hbm.at[pl.ds(NX - HIGH, HIGH)], i_m),
            (chip_hbm.at[pl.ds(NX - HIGH, HIGH)], c_m),
            (t_hbm.at[:, pl.ds(0, TILE)], t_a),
            (id_hbm.at[:, pl.ds(0, TILE)], i_a),
            (chip_hbm.at[:, pl.ds(0, TILE)], c_a),
            (t_hbm.at[:, pl.ds(NY - TILE, TILE)], t_b),
            (id_hbm.at[:, pl.ds(NY - TILE, TILE)], i_b),
            (chip_hbm.at[:, pl.ds(NY - TILE, TILE)], c_b),
            (site_hbm, site_ref),
        )
    ):
        copies.append(pltpu.make_async_copy(src, dst, sems.at[k]))
        copies[-1].start()
    for copy in copies[:6]:
        copy.wait()

    def x_sides(low, high):
        for k in range(HIGH):
            low[k] = t_p[k]
            low[4 + k] = i_p[k].astype(f32)
            if k < 3:
                low[8 + k] = c_p[k].astype(f32)
                high[k] = t_m[1 + k]
                high[3 + k] = i_m[1 + k].astype(f32)
            if k < 2:
                high[6 + k] = c_m[2 + k].astype(f32)

    even_x = lax.rem(lax.axis_index("gx"), 2) == 0
    even_y = lax.rem(lax.axis_index("gy"), 2) == 0

    @pl.when(even_x)
    def _():
        x_sides(xa, xb)

    @pl.when(jnp.logical_not(even_x))
    def _():
        x_sides(xb, xa)

    for copy in copies[6:]:
        copy.wait()
    sub = sublane((TILE, NZ))

    def own(q, _):
        low = first_tile(sub, t_a[q], i_a[q].astype(f32))
        high = last_tile(sub, t_b[q], i_b[q].astype(f32), c_b[q].astype(f32))
        ya[q] = jnp.where(even_y, low, high)
        yb[q] = jnp.where(even_y, high, low)
        return 0

    lax.fori_loop(0, NX, own, 0, unroll=8)
    for j in range(PAIRS):
        tile = c_a[j].astype(f32)
        if j + PAIRS < NX:
            tile = jnp.where(sub < 4, tile, pltpu.roll(c_a[j + PAIRS].astype(f32), 4, 0))
        ya[PX + j] = tile
        yb[PX + j] = tile
    for k in range(sites.shape[0]):
        sites[k] = site_ref[...]


def corner_kernel(ya_in, yb_in, xa_ref, xb_ref, sites_in, ya, yb, sites_out):
    del ya_in, yb_in, sites_in, sites_out
    even_x = lax.rem(lax.axis_index("gx"), 2) == 0
    even_y = lax.rem(lax.axis_index("gy"), 2) == 0
    sub = sublane((TILE, NZ))
    zero = jnp.zeros((TILE, NZ), f32)
    first = pl.ds(0, TILE)
    last = pl.ds(NY - TILE, TILE)

    def high_side(k, rows):
        return jnp.where(even_x, xb_ref[k, rows, :], xa_ref[k, rows, :])

    def low_side(k, rows):
        return jnp.where(even_x, xa_ref[k, rows, :], xb_ref[k, rows, :])

    for k in range(HIGH + LOW):
        q = NX + k
        if k < HIGH:
            side, places = high_side, (k, 4 + k, 8 + k if k < 3 else None)
        else:
            j = k - HIGH
            side, places = low_side, (j, 3 + j, 5 + j if j else None)
        temp, ident, chip = places
        low = first_tile(sub, side(temp, first), side(ident, first))
        high = last_tile(
            sub, side(temp, last), side(ident, last), zero if chip is None else side(chip, last)
        )
        ya[q] = jnp.where(even_y, low, high)
        yb[q] = jnp.where(even_y, high, low)
        if chip is not None:
            place = PX + q - PAIRS
            tile = jnp.where(sub < 4, ya[place], pltpu.roll(side(chip, first), 4, 0))
            ya[place] = tile
            yb[place] = tile


def pick(ident, table):
    low = jnp.where(ident == 1, table(1), table(0))
    high = jnp.where(ident == 3, table(3), table(2))
    return jnp.where(ident >= 2, high, low)


def up_z(v):
    return pltpu.roll(v, NZ - 1, 1)


def down_z(v):
    return pltpu.roll(v, 1, 1)


def cells(temp, ident, chip, tables, inside=None):
    ref_ref, grad_ref, store_ref = tables
    conduct = pick(ident, ref_ref) * (
        1.0 + pick(ident, grad_ref) * jnp.tanh(temp - kelvin_shift_amount)
    )
    if inside is not None:
        conduct = conduct * inside
    lanes = lane(temp.shape)
    inner_z = jnp.where(lanes < NZ - 1, 1.0, 0.0).astype(f32)
    edge_z = jnp.where((lanes == 0) | (lanes == NZ - 1), 1.0, 0.0).astype(f32)
    e_z = (conduct + up_z(conduct)) * inner_z
    f_z = e_z * (up_z(temp) - temp)
    c_b = conduct * edge_z
    diag = (pick(ident, store_ref) + c_b) + (e_z + down_z(e_z))
    resid = (clock_advance * interface_warming_rate * chip - c_b * temp) + (f_z - down_z(f_z))
    return conduct, diag, resid, e_z


def surface(read, terms):
    rows = sublane((TILE, NZ))
    diagonal = sublane((NZ, NZ)) == lane((NZ, NZ))
    first = jnp.where(sublane((NZ, NZ)) == 0, 1.0, 0.0).astype(bf16)
    total = jnp.zeros((TILE, NZ), f32)
    for s in range(TILE):
        rest = read(s)
        line = jnp.zeros((NZ, NZ), f32)
        for _ in range(terms):
            part = rest.astype(bf16)
            line = line + jnp.dot(part, first, preferred_element_type=f32)
            rest = rest - part.astype(f32)
        line = jnp.sum(jnp.where(diagonal, line, 0.0), axis=0, keepdims=True)
        total = jnp.where(rows == s, line, total)
    return total


def own_rows(ref):
    per = NX // TILE
    return lambda s: jnp.concatenate([ref[per * s + i, :NY, :] for i in range(per)], axis=0)


def own_kernel(
    ref_hbm,
    grad_hbm,
    store_hbm,
    t_hbm,
    id_hbm,
    chip_hbm,
    xa_ref,
    xb_ref,
    site_ref,
    tp,
    cp,
    dp,
    rp,
    ez,
    surf_ref,
    hot_ref,
    row_ref,
    lane_ref,
    table_ref,
    t_ref,
    id_ref,
    chip_ref,
    ref_ref,
    grad_ref,
    store_ref,
    sems,
):
    ix = lax.axis_index("gx")
    iy = lax.axis_index("gy")

    copies = [
        pltpu.make_async_copy(src, dst, sems.at[k])
        for k, (src, dst) in enumerate(
            (
                (ref_hbm, ref_ref),
                (grad_hbm, grad_ref),
                (store_hbm, store_ref),
                (t_hbm, t_ref),
                (id_hbm, id_ref),
                (chip_hbm, chip_ref),
            )
        )
    ]
    for copy in copies:
        copy.start()

    width = NY * lax.axis_size("gy")
    subs = sublane((NZ, NZ))

    def places(b, _):
        site = site_ref[b]
        row = site // width
        col = site - row * width
        here = (col // NY) == iy
        cell = (row % NX) * NY + col % NY
        row_of = jnp.where(here, (row // NX) * TILE + cell // NZ, -1)
        row_ref[b] = row_of
        lane_ref[b] = cell % NZ
        for s in range(TILE):
            hit = subs == jnp.broadcast_to(row_of[s : s + 1], (NZ, NZ))
            hot_ref[b, :, NZ * s : NZ * (s + 1)] = jnp.where(hit, 1.0, 0.0).astype(bf16)
        return 0

    lax.fori_loop(0, site_ref.shape[0], places, 0, unroll=2)
    for copy in copies:
        copy.wait()

    tables = [lambda k, ref=ref: ref[k] for ref in (ref_ref, grad_ref, store_ref)]
    for j, table in enumerate(tables):
        for k in range(4):
            table_ref[4 * j + k] = jnp.full((TILE, NZ), table(k), f32)

    def put(q, temp, ident, chip, inside=None):
        conduct, diag, resid, e_z = cells(temp, ident, chip, tables, inside)
        tp[q, :NY, :] = temp
        cp[q, :NY, :] = conduct
        dp[q, :NY, :] = diag
        rp[q, :NY, :] = resid
        ez[q, :NY, :] = e_z

    def own_plane(q, _):
        put(q, t_ref[q], id_ref[q], chip_ref[q].astype(f32))
        return 0

    lax.fori_loop(0, NX, own_plane, 0, unroll=4)

    even_x = lax.rem(ix, 2) == 0
    low_x = jnp.where(ix > 0, 1.0, 0.0).astype(f32)
    high_x = jnp.where(ix < lax.axis_size("gx") - 1, 1.0, 0.0).astype(f32)
    zero_plane = jnp.zeros((NY, NZ), f32)

    def high_plane(k):
        return jnp.where(even_x, xb_ref[k], xa_ref[k])

    def low_plane(k):
        return jnp.where(even_x, xa_ref[k], xb_ref[k])

    for k in range(HIGH):
        chip = high_plane(8 + k) if k < 3 else zero_plane
        put(NX + k, high_plane(k), high_plane(4 + k), chip, high_x)
    for k in range(LOW):
        chip = low_plane(5 + k) if k > 0 else zero_plane
        put(NX + HIGH + k, low_plane(k), low_plane(3 + k), chip, low_x)

    surf_ref[...] = surface(own_rows(t_ref), 3)


def krylov_kernel(
    table_ref,
    tp_in,
    cp_in,
    dp_in,
    rp_in,
    ez_in,
    surf_ref,
    ya_ref,
    yb_ref,
    tp,
    cp,
    dp,
    rp,
    ez,
    w0_ref,
    w1_ref,
    w2_ref,
    send_ref,
    ex,
    ey,
    dinv,
):
    del tp_in, cp_in, dp_in, rp_in, ez_in
    tables = [lambda k, j=j: table_ref[4 * j + k] for j in range(3)]
    ix = lax.axis_index("gx")
    iy = lax.axis_index("gy")
    last_x = lax.axis_size("gx") - 1
    last_y = lax.axis_size("gy") - 1
    sub = sublane((TILE, NZ))
    one = jnp.ones((), f32)
    low_x = jnp.where(ix > 0, 1.0, 0.0).astype(f32)
    high_x = jnp.where(ix < last_x, 1.0, 0.0).astype(f32)
    low_y = jnp.where(iy > 0, 1.0, 0.0).astype(f32)
    high_y = jnp.where(iy < last_y, 1.0, 0.0).astype(f32)
    rows_halo = jnp.where(sub < 4, high_y, low_y)

    even_y = lax.rem(iy, 2) == 0

    def high_row(q):
        return jnp.where(even_y, yb_ref[q], ya_ref[q])

    def low_row(q):
        return jnp.where(even_y, ya_ref[q], yb_ref[q])

    def put_halo(q, chip_high, plane_in):
        high = high_row(q)
        low = low_row(q)
        temp = jnp.where(sub < 4, high, low)
        ident = jnp.where(sub < 4, pltpu.roll(high, 4, 0), pltpu.roll(low, 3, 0))
        chip = jnp.where(sub < 4, chip_high, pltpu.roll(low, 6, 0))
        conduct, diag, resid, e_z = cells(temp, ident, chip, tables, rows_halo * plane_in)
        tp[q, NY:, :] = temp
        cp[q, NY:, :] = conduct
        dp[q, NY:, :] = diag
        rp[q, NY:, :] = resid
        ez[q, NY:, :] = e_z

    def own_halo_first(q, _):
        put_halo(q, high_row(PX + q), one)
        return 0

    def own_halo_second(q, _):
        put_halo(q, pltpu.roll(high_row(PX + q - PAIRS), 4, 0), one)
        return 0

    lax.fori_loop(0, PAIRS, own_halo_first, 0, unroll=20)
    lax.fori_loop(PAIRS, NX, own_halo_second, 0, unroll=12)

    zero_tile = jnp.zeros((TILE, NZ), f32)
    for q in range(NX, PX):
        put_halo(q, pltpu.roll(high_row(PX + q - PAIRS), 4, 0), high_x if q < NX + HIGH else low_x)

    subs = sublane((PY, NZ))
    rows_in = jnp.where(subs < NY, 1.0, jnp.where(subs < NY + 4, high_y, low_y)).astype(f32)

    def up_y(v):
        return pltpu.roll(v, PY - 1, 0)

    def down_y(v):
        return pltpu.roll(v, 1, 0)

    def fold(v):
        return (v[0:8] + v[8:16]) + (v[16:24] + v[24:32])

    def faces(q, nxt, ex_before, fx_before, plane_in):
        c0 = cp[q]
        t0 = tp[q]
        e_x = c0 + cp[nxt]
        f_x = e_x * (tp[nxt] - t0)
        e_y = c0 + up_y(c0)
        f_y = e_y * (up_y(t0) - t0)
        diag = dp[q] + ((e_x + ex_before) + (e_y + down_y(e_y)))
        inverse = (rows_in * plane_in) / diag
        resid = rp[q] + ((f_x - fx_before) + (f_y - down_y(f_y)))
        first = resid * inverse
        ex[q] = e_x
        ey[q] = e_y
        dinv[q] = inverse
        w0_ref[q] = first
        return e_x, f_x, resid, first

    e_first = cp[36] + cp[37]
    carry = (e_first, e_first * (tp[37] - tp[36]))
    for q, nxt in ((37, 38), (38, 0)):
        carry = faces(q, nxt, carry[0], carry[1], low_x)[:2]

    def faces_own(q, state):
        e_b, f_b, m0 = state
        e_x, f_x, resid, first = faces(q, q + 1, e_b, f_b, one)
        return e_x, f_x, m0 + fold(resid[:NY] * first[:NY])

    e_b, f_b, m0 = lax.fori_loop(0, NX, faces_own, (carry[0], carry[1], zero_tile), unroll=16)
    carry = (e_b, f_b)
    for q in (32, 33, 34):
        carry = faces(q, q + 1, carry[0], carry[1], high_x)[:2]

    def neighbours(src, q, nxt, g_before):
        v = src[q]
        e_x = ex[q]
        e_y = ey[q]
        e_z = ez[q]
        total = (e_x * src[nxt] + g_before) + (
            (e_y * up_y(v) + down_y(e_y * v)) + (e_z * up_z(v) + down_z(e_z * v))
        )
        return total, v, e_x * v

    def advance(src, dst, before, prologue, epilogue):
        carry = ex[before] * src[before]
        for q, nxt in prologue:
            total, _, carry = neighbours(src, q, nxt, carry)
            dst[q] = dinv[q] * total

        def step(q, state):
            g, ma, mb = state
            total, v, g = neighbours(src, q, q + 1, g)
            new = dinv[q] * total
            dst[q] = new
            ma = ma + fold(total[:NY] * v[:NY])
            mb = mb + fold(total[:NY] * new[:NY])
            return g, ma, mb

        carry, ma, mb = lax.fori_loop(0, NX, step, (carry, zero_tile, zero_tile), unroll=8)
        for q, nxt in epilogue:
            total, _, carry = neighbours(src, q, nxt, carry)
            dst[q] = dinv[q] * total
        return ma, mb

    m1, m2 = advance(w0_ref, w1_ref, 37, ((38, 0),), ((32, 33), (33, 34)))

    def crossing(q, v, after):
        half = ex[q] * after + (ey[q] * up_y(v) + ez[q] * up_z(v))
        return fold(half[:NY] * v[:NY])

    def second(q, g):
        total, v, g = neighbours(w1_ref, q, q + 1, g)
        new = dinv[q] * total
        w2_ref[q] = new
        return g, new, fold(total[:NY] * v[:NY]), fold(total[:NY] * new[:NY])

    g, before, m3, m4 = second(0, ex[38] * w1_ref[38])

    def step_2(q, state):
        g, before, ma, mb, mc = state
        g, new, a, b = second(q, g)
        return g, new, ma + a, mb + b, mc + crossing(q - 1, before, new)

    g, before, m3, m4, m5 = lax.fori_loop(
        1, NX, step_2, (g, before, m3, m4, zero_tile), unroll=31
    )
    total, _, _ = neighbours(w1_ref, NX, NX + 1, g)
    m5 = m5 + crossing(NX - 1, before, dinv[NX] * total)
    m5 = m5 + m5

    lanes = lane((HALF, NZ))
    moments = jnp.zeros((HALF, NZ), f32)
    for k, m in enumerate((m0, m1, m2, m3, m4, m5)):
        m = jnp.sum(jnp.sum(m, axis=0, keepdims=True), axis=1, keepdims=True)
        moments = jnp.where(lanes == k, jnp.broadcast_to(m, (HALF, NZ)), moments)
    fields = [surf_ref[...]] + [surface(own_rows(w), 2) for w in (w0_ref, w1_ref, w2_ref)]
    halves = [tile[i : i + HALF] for tile in fields for i in (0, HALF)] + [moments]
    for k in range(send_ref.shape[0]):
        for j, half in enumerate(halves):
            send_ref[k, j] = half


def lookup_kernel(hot_ref, row_ref, lane_ref, table_ref, out_ref, parts, start):
    blocks = table_ref.shape[0]
    targets = hot_ref.shape[0]
    sub = sublane((TILE, NZ))
    zero = jnp.zeros((TILE, NZ), f32)
    fields = FIELDS - 1

    def tile(a, f):
        return jnp.concatenate([table_ref[a, 2 * f], table_ref[a, 2 * f + 1]], axis=0)

    for a in range(blocks):
        start[a] = tile(a, 0)
    for f in range(fields):
        rest = jnp.concatenate([tile(a, f + 1) for a in range(blocks)], axis=0).T
        for k in range(2):
            part = rest.astype(bf16)
            parts[NZ * f : NZ * (f + 1), NZ * k : NZ * (k + 1)] = part
            rest = rest - part.astype(f32)

    total = table_ref[0, 2 * FIELDS]
    for a in range(1, blocks):
        total = total + table_ref[a, 2 * FIELDS]

    def one(b, _):
        row_of = row_ref[b]
        lane_of = lane_ref[b]
        found = [zero] * FIELDS
        for pair in range(0, TILE, 2):
            hot = hot_ref[b, :, NZ * pair : NZ * (pair + 2)]
            hot = jnp.concatenate([hot, hot], axis=0)
            lanes = [jnp.broadcast_to(lane_of[pair + i : pair + i + 1], (TILE, NZ)) for i in (0, 1)]
            offset = [e - sub for e in lanes]
            for i in (0, 1):
                rows = jnp.broadcast_to(row_of[pair + i : pair + i + 1], (TILE, NZ)) - sub
                acc = zero
                for a in range(blocks):
                    got = jnp.take_along_axis(start[a], lanes[i], axis=1)
                    acc = jnp.where(rows == a * TILE, got, acc)
                found[0] = jnp.where(
                    sub == pair + i, jnp.sum(acc, axis=0, keepdims=True), found[0]
                )
            for f in range(fields):
                line = jnp.dot(parts[NZ * f : NZ * (f + 1)], hot, preferred_element_type=f32)
                for i in (0, 1):
                    acc = zero
                    for t in range(NZ // TILE):
                        acc = jnp.where(
                            offset[i] == t * TILE,
                            line[TILE * t : TILE * (t + 1), NZ * i : NZ * (i + 1)],
                            acc,
                        )
                    found[f + 1] = jnp.where(
                        sub == pair + i, jnp.sum(acc, axis=0, keepdims=True), found[f + 1]
                    )
        for f in range(FIELDS):
            out_ref[b, 2 * f] = found[f][:HALF]
            out_ref[b, 2 * f + 1] = found[f][HALF:]
        out_ref[b, 2 * FIELDS] = total
        return 0

    lax.fori_loop(0, targets, one, 0, unroll=4)


def cg_coefficients(m):
    a = [m[j] - m[j + 1] for j in range(5)]

    def quadratic(v, h):
        total = None
        for i in range(3):
            for j in range(3):
                if v[i] is None or v[j] is None:
                    continue
                term = v[i] * v[j] * h[i + j]
                total = term if total is None else total + term
        return total

    def add(u, v):
        return v if u is None else u if v is None else u + v

    def scale(s, v):
        return [None if e is None else s * e for e in v]

    one = jnp.ones_like(m[0])
    z = [one, None, None]
    p = [one, None, None]
    rz = m[0]
    x = [None, None, None]
    for step in range(3):
        alpha = rz / quadratic(p, a)
        x = [add(e, g) for e, g in zip(x, scale(alpha, p))]
        if step < 2:
            ap = scale(alpha, p)
            moved = [None] + ap[:2]
            z = [
                add(add(z[i], None if ap[i] is None else -ap[i]), moved[i]) for i in range(3)
            ]
            new = quadratic(z, m)
            p = [add(z[i], e) for i, e in enumerate(scale(new / rz, p))]
            rz = new
    return x


def final_kernel(
    got_ref,
    pressure_hbm,
    t_ref,
    w0_ref,
    w1_ref,
    w2_ref,
    temp_hbm,
    growth_ref,
    pressure_ref,
    temp_ref,
    sem,
    out_sems,
):
    copy = pltpu.make_async_copy(pressure_hbm, pressure_ref, sem)
    copy.start()
    total = got_ref[0]
    for b in range(1, got_ref.shape[0]):
        total = total + got_ref[b]
    m = [total[2 * FIELDS, 0:1, k : k + 1] for k in range(6)]
    fields = [jnp.concatenate([total[2 * f], total[2 * f + 1]], axis=0) for f in range(FIELDS)]
    c = cg_coefficients(m)
    c_tile = [jnp.broadcast_to(e, (TILE, NZ)) for e in c]
    c_plane = [jnp.broadcast_to(e, (NY, NZ)) for e in c]

    def plane(q, _):
        temp_ref[q] = (
            t_ref[q, :NY, :]
            + c_plane[0] * w0_ref[q, :NY, :]
            + c_plane[1] * w1_ref[q, :NY, :]
            + c_plane[2] * w2_ref[q, :NY, :]
        )
        return 0

    outs = []
    step = NX // 4
    for k in range(4):
        lax.fori_loop(step * k, step * (k + 1), plane, 0, unroll=4)
        part = pl.ds(step * k, step)
        outs.append(pltpu.make_async_copy(temp_ref.at[part], temp_hbm.at[part], out_sems.at[k]))
        outs[-1].start()

    flank = fields[0]
    for k in range(3):
        flank = flank + c_tile[k] * fields[k + 1]
    soft = jnp.maximum(flank, 0.0) + jnp.log1p(jnp.exp(-jnp.abs(flank)))
    copy.wait()
    growth_ref[...] = usui_rate * pressure_ref[...] * jnp.exp(-usui_energy / (1.0 + soft))
    for out in outs:
        out.wait()


def local(
    prior_kelvin_state,
    substance_identifier,
    chip_touch_indicator,
    substance_reference_diffusivity,
    substance_diffusivity_gradient,
    substance_storage_coefficient,
    clearance_point_indices,
    clearance_face_pressure,
):
    size_x = lax.axis_size("gx")
    size_y = lax.axis_size("gy")
    temp, ident, chip = prior_kelvin_state, substance_identifier, chip_touch_indicator
    vmem = pl.BlockSpec(memory_space=pltpu.VMEM)

    def params(mib):
        return pltpu.CompilerParams(vmem_limit_bytes=mib * MIB)


    anywhere = pl.BlockSpec(memory_space=pltpu.HBM)

    def arr(*shape, dtype=f32):
        return jax.ShapeDtypeStruct(shape, dtype)

    def buf(*shape, dtype=f32):
        return pltpu.VMEM(shape, dtype)

    def in_hbm(*arrays):
        return [pltpu.with_memory_space_constraint(a, pltpu.HBM) for a in arrays]

    i32 = jnp.int32
    xa, xb, ya, yb, sites = pl.pallas_call(
        pack_kernel,
        name="pack",
        in_specs=[anywhere] * 4,
        out_specs=[vmem] * 5,
        out_shape=[
            arr(11, NY, NZ),
            arr(11, NY, NZ),
            arr(PX + PAIRS, TILE, NZ),
            arr(PX + PAIRS, TILE, NZ),
            arr(size_y, TILE, NZ, dtype=i32),
        ],
        scratch_shapes=[
            buf(NX, TILE, NZ),
            buf(NX, TILE, NZ),
            buf(NX, TILE, NZ, dtype=i32),
            buf(NX, TILE, NZ, dtype=i32),
            buf(NX, TILE, NZ, dtype=i32),
            buf(NX, TILE, NZ, dtype=i32),
            buf(HIGH, NY, NZ),
            buf(HIGH, NY, NZ),
            buf(HIGH, NY, NZ, dtype=i32),
            buf(HIGH, NY, NZ, dtype=i32),
            buf(HIGH, NY, NZ, dtype=i32),
            buf(HIGH, NY, NZ, dtype=i32),
            buf(TILE, NZ, dtype=i32),
            pltpu.SemaphoreType.DMA((13,)),
        ],
        compiler_params=params(10),
    )(*in_hbm(temp, ident, chip, clearance_point_indices.reshape(TILE, NZ)))
    sites = lax.all_to_all(sites, "gy", 0, 0)

    xa = lax.ppermute(xa, "gx", swaps(size_x, 1))
    xb = lax.ppermute(xb, "gx", swaps(size_x, 0))
    ya, yb, sites = pl.pallas_call(
        corner_kernel,
        name="corners",
        in_specs=[vmem] * 5,
        out_specs=[vmem] * 3,
        out_shape=[
            arr(PX + PAIRS, TILE, NZ),
            arr(PX + PAIRS, TILE, NZ),
            arr(size_y, TILE, NZ, dtype=i32),
        ],
        input_output_aliases={0: 0, 1: 1, 4: 2},
        compiler_params=params(8),
    )(ya, yb, xa, xb, sites)
    ya = lax.ppermute(ya, "gy", swaps(size_y, 1))
    yb = lax.ppermute(yb, "gy", swaps(size_y, 0))

    tables = (
        substance_reference_diffusivity,
        substance_diffusivity_gradient,
        substance_storage_coefficient,
    )
    padded = arr(PX, PY, NZ)
    *own, hot, row, place, table_tiles = pl.pallas_call(
        own_kernel,
        name="own_cells",
        in_specs=[anywhere] * 6 + [vmem] * 3,
        out_specs=[vmem] * 10,
        out_shape=[padded] * 5
        + [
            arr(TILE, NZ),
            arr(size_y, NZ, TILE * NZ, dtype=bf16),
            arr(size_y, TILE, NZ, dtype=i32),
            arr(size_y, TILE, NZ, dtype=i32),
            arr(12, TILE, NZ),
        ],
        scratch_shapes=[
            buf(NX, NY, NZ),
            buf(NX, NY, NZ, dtype=i32),
            buf(NX, NY, NZ, dtype=i32),
            pltpu.SMEM((4,), f32),
            pltpu.SMEM((4,), f32),
            pltpu.SMEM((4,), f32),
            pltpu.SemaphoreType.DMA((6,)),
        ],
        compiler_params=params(14),
    )(*in_hbm(*tables, temp, ident, chip), xa, xb, sites)

    start, _, _, _, _, w0, w1, w2, send = pl.pallas_call(
        krylov_kernel,
        name="krylov",
        in_specs=[vmem] * 9,
        out_specs=[vmem] * 9,
        out_shape=[padded] * 8 + [arr(size_x, BLOCK, HALF, NZ)],
        input_output_aliases={1: 0, 2: 1, 3: 2, 4: 3, 5: 4},
        scratch_shapes=[buf(PX, PY, NZ)] * 3,
        compiler_params=params(24),
    )(table_tiles, *own, ya, yb)
    table = lax.all_to_all(send, "gx", 0, 0)
    found = pl.pallas_call(
        lookup_kernel,
        name="lookup",
        in_specs=[vmem] * 4,
        out_specs=vmem,
        out_shape=arr(size_y, BLOCK, HALF, NZ),
        scratch_shapes=[
            buf(NZ * (FIELDS - 1), 2 * NZ, dtype=bf16),
            buf(size_x, TILE, NZ),
        ],
        compiler_params=params(20),
    )(hot, row, place, table)
    got = lax.all_to_all(found, "gy", 0, 0)
    temperature, growth = pl.pallas_call(
        final_kernel,
        name="finish",
        in_specs=[vmem, anywhere, vmem, vmem, vmem, vmem],
        out_specs=[anywhere, vmem],
        out_shape=[arr(NX, NY, NZ), arr(TILE, NZ)],
        scratch_shapes=[
            buf(TILE, NZ),
            buf(NX, NY, NZ),
            pltpu.SemaphoreType.DMA(()),
            pltpu.SemaphoreType.DMA((4,)),
        ],
        compiler_params=params(12),
    )(got, *in_hbm(clearance_face_pressure.reshape(TILE, NZ)), start, w0, w1, w2)
    return temperature, growth.reshape(-1)


def solution(mesh):
    in_specs = (
        P("gx", "gy", None),
        P("gx", "gy", None),
        P("gx", "gy", None),
        P(),
        P(),
        P(),
        P(("gx", "gy")),
        P(("gx", "gy")),
    )
    out_specs = (P("gx", "gy", None), P(("gx", "gy")))
    return jax.shard_map(local, mesh=mesh, in_specs=in_specs, out_specs=out_specs, check_vma=False)
```

```python
import jax
import jax.numpy as jnp
from jax import lax
from jax.experimental import pallas as pl
from jax.experimental.pallas import tpu as pltpu
from jax.sharding import PartitionSpec as P

clock_advance = 2.0
interface_warming_rate = 3.0
usui_rate = 3.0
usui_energy = 4.0
kelvin_shift_amount = 2.0

LOW = 3
HIGH = 4
NX = 32
NY = 32
NZ = 128
PX = NX + HIGH + LOW
PY = NY + 8
FIELDS = 4
TILE = 8
HALF = 4
BLOCK = 2 * FIELDS + 1
PAIRS = 20
MIB = 1024 * 1024
f32 = jnp.float32
bf16 = jnp.bfloat16


def swaps(count, first):
    low = range(first, count - 1, 2)
    return [(i, i + 1) for i in low] + [(i + 1, i) for i in low]


def sublane(shape):
    return lax.broadcasted_iota(jnp.int32, shape, len(shape) - 2)


def lane(shape):
    return lax.broadcasted_iota(jnp.int32, shape, len(shape) - 1)


def first_tile(sub, temp, ident):
    return jnp.where(sub < 4, temp, pltpu.roll(ident, 4, 0))


def last_tile(sub, temp, ident, chip):
    return jnp.where(
        sub >= 5, temp, jnp.where(sub >= 2, pltpu.roll(ident, 5, 0), pltpu.roll(chip, 2, 0))
    )


def pack_kernel(
    t_hbm,
    id_hbm,
    chip_hbm,
    site_hbm,
    xa,
    xb,
    ya,
    yb,
    yc,
    sites,
    t_a,
    t_b,
    i_a,
    i_b,
    c_a,
    c_b,
    t_p,
    t_m,
    i_p,
    i_m,
    c_p,
    c_m,
    site_ref,
    sems,
):
    copies = []
    for k, (src, dst) in enumerate(
        (
            (t_hbm.at[pl.ds(0, HIGH)], t_p),
            (id_hbm.at[pl.ds(0, HIGH)], i_p),
            (chip_hbm.at[pl.ds(0, HIGH)], c_p),
            (t_hbm.at[pl.ds(NX - HIGH, HIGH)], t_m),
            (id_hbm.at[pl.ds(NX - HIGH, HIGH)], i_m),
            (chip_hbm.at[pl.ds(NX - HIGH, HIGH)], c_m),
            (t_hbm.at[:, pl.ds(0, TILE)], t_a),
            (id_hbm.at[:, pl.ds(0, TILE)], i_a),
            (chip_hbm.at[:, pl.ds(0, TILE)], c_a),
            (t_hbm.at[:, pl.ds(NY - TILE, TILE)], t_b),
            (id_hbm.at[:, pl.ds(NY - TILE, TILE)], i_b),
            (chip_hbm.at[:, pl.ds(NY - TILE, TILE)], c_b),
            (site_hbm, site_ref),
        )
    ):
        copies.append(pltpu.make_async_copy(src, dst, sems.at[k]))
        copies[-1].start()
    for copy in copies[:6]:
        copy.wait()

    def x_sides(low, high):
        for k in range(HIGH):
            low[k] = t_p[k]
            low[4 + k] = i_p[k].astype(f32)
            if k < 3:
                low[8 + k] = c_p[k].astype(f32)
                high[k] = t_m[1 + k]
                high[3 + k] = i_m[1 + k].astype(f32)
            if k < 2:
                high[6 + k] = c_m[2 + k].astype(f32)

    even_x = lax.rem(lax.axis_index("gx"), 2) == 0
    even_y = lax.rem(lax.axis_index("gy"), 2) == 0

    @pl.when(even_x)
    def _():
        x_sides(xa, xb)

    @pl.when(jnp.logical_not(even_x))
    def _():
        x_sides(xb, xa)

    for copy in copies[6:]:
        copy.wait()
    sub = sublane((TILE, NZ))

    def own(q, _):
        low = first_tile(sub, t_a[q], i_a[q].astype(f32))
        high = last_tile(sub, t_b[q], i_b[q].astype(f32), c_b[q].astype(f32))
        ya[q] = jnp.where(even_y, low, high)
        yb[q] = jnp.where(even_y, high, low)
        return 0

    lax.fori_loop(0, NX, own, 0, unroll=8)
    for j in range(PAIRS):
        tile = c_a[j].astype(f32)
        if j + PAIRS < NX:
            tile = jnp.where(sub < 4, tile, pltpu.roll(c_a[j + PAIRS].astype(f32), 4, 0))
        yc[j] = tile
    for k in range(sites.shape[0]):
        sites[k] = site_ref[...]


def corner_kernel(ya_in, yb_in, yc_in, xa_ref, xb_ref, sites_in, ya, yb, yc, sites_out):
    del ya_in, yb_in, yc_in, sites_in, sites_out
    even_x = lax.rem(lax.axis_index("gx"), 2) == 0
    even_y = lax.rem(lax.axis_index("gy"), 2) == 0
    sub = sublane((TILE, NZ))
    zero = jnp.zeros((TILE, NZ), f32)
    first = pl.ds(0, TILE)
    last = pl.ds(NY - TILE, TILE)

    def high_side(k, rows):
        return jnp.where(even_x, xb_ref[k, rows, :], xa_ref[k, rows, :])

    def low_side(k, rows):
        return jnp.where(even_x, xa_ref[k, rows, :], xb_ref[k, rows, :])

    for k in range(HIGH + LOW):
        q = NX + k
        if k < HIGH:
            side, places = high_side, (k, 4 + k, 8 + k if k < 3 else None)
        else:
            j = k - HIGH
            side, places = low_side, (j, 3 + j, 5 + j if j else None)
        temp, ident, chip = places
        low = first_tile(sub, side(temp, first), side(ident, first))
        high = last_tile(
            sub, side(temp, last), side(ident, last), zero if chip is None else side(chip, last)
        )
        ya[q] = jnp.where(even_y, low, high)
        yb[q] = jnp.where(even_y, high, low)
        if chip is not None:
            place = q - PAIRS
            yc[place] = jnp.where(sub < 4, yc[place], pltpu.roll(side(chip, first), 4, 0))


def pick(ident, table):
    low = jnp.where(ident == 1, table(1), table(0))
    high = jnp.where(ident == 3, table(3), table(2))
    return jnp.where(ident >= 2, high, low)


def up_z(v):
    return pltpu.roll(v, NZ - 1, 1)


def down_z(v):
    return pltpu.roll(v, 1, 1)


def cells(temp, ident, chip, tables, inside=None):
    ref_ref, grad_ref, store_ref = tables
    conduct = pick(ident, ref_ref) * (
        1.0 + pick(ident, grad_ref) * jnp.tanh(temp - kelvin_shift_amount)
    )
    if inside is not None:
        conduct = conduct * inside
    lanes = lane(temp.shape)
    inner_z = jnp.where(lanes < NZ - 1, 1.0, 0.0).astype(f32)
    edge_z = jnp.where((lanes == 0) | (lanes == NZ - 1), 1.0, 0.0).astype(f32)
    e_z = (conduct + up_z(conduct)) * inner_z
    f_z = e_z * (up_z(temp) - temp)
    c_b = conduct * edge_z
    diag = (pick(ident, store_ref) + c_b) + (e_z + down_z(e_z))
    resid = (clock_advance * interface_warming_rate * chip - c_b * temp) + (f_z - down_z(f_z))
    return conduct, diag, resid, e_z


def surface(read, terms):
    rows = sublane((TILE, NZ))
    diagonal = sublane((NZ, NZ)) == lane((NZ, NZ))
    first = jnp.where(sublane((NZ, NZ)) == 0, 1.0, 0.0).astype(bf16)
    total = jnp.zeros((TILE, NZ), f32)
    for s in range(TILE):
        rest = read(s)
        line = jnp.zeros((NZ, NZ), f32)
        for _ in range(terms):
            part = rest.astype(bf16)
            line = line + jnp.dot(part, first, preferred_element_type=f32)
            rest = rest - part.astype(f32)
        line = jnp.sum(jnp.where(diagonal, line, 0.0), axis=0, keepdims=True)
        total = jnp.where(rows == s, line, total)
    return total


def own_rows(ref):
    per = NX // TILE
    return lambda s: jnp.concatenate([ref[per * s + i, :NY, :] for i in range(per)], axis=0)


def own_kernel(
    ref_hbm,
    grad_hbm,
    store_hbm,
    t_hbm,
    id_hbm,
    chip_hbm,
    xa_ref,
    xb_ref,
    site_ref,
    tp,
    cp,
    dp,
    rp,
    ez,
    surf_ref,
    hot_ref,
    row_ref,
    lane_ref,
    table_ref,
    t_ref,
    id_ref,
    chip_ref,
    ref_ref,
    grad_ref,
    store_ref,
    sems,
):
    ix = lax.axis_index("gx")
    iy = lax.axis_index("gy")

    copies = [
        pltpu.make_async_copy(src, dst, sems.at[k])
        for k, (src, dst) in enumerate(
            (
                (ref_hbm, ref_ref),
                (grad_hbm, grad_ref),
                (store_hbm, store_ref),
                (t_hbm, t_ref),
                (id_hbm, id_ref),
                (chip_hbm, chip_ref),
            )
        )
    ]
    for copy in copies:
        copy.start()

    width = NY * lax.axis_size("gy")
    subs = sublane((NZ, NZ))

    def places(b, _):
        site = site_ref[b]
        row = site // width
        col = site - row * width
        here = (col // NY) == iy
        cell = (row % NX) * NY + col % NY
        row_of = jnp.where(here, (row // NX) * TILE + cell // NZ, -1)
        row_ref[b] = row_of
        lane_ref[b] = cell % NZ
        for s in range(TILE):
            hit = subs == jnp.broadcast_to(row_of[s : s + 1], (NZ, NZ))
            hot_ref[b, :, NZ * s : NZ * (s + 1)] = jnp.where(hit, 1.0, 0.0).astype(bf16)
        return 0

    lax.fori_loop(0, site_ref.shape[0], places, 0, unroll=2)
    for copy in copies:
        copy.wait()

    tables = [lambda k, ref=ref: ref[k] for ref in (ref_ref, grad_ref, store_ref)]
    for j, table in enumerate(tables):
        for k in range(4):
            table_ref[4 * j + k] = jnp.full((TILE, NZ), table(k), f32)

    def put(q, temp, ident, chip, inside=None):
        conduct, diag, resid, e_z = cells(temp, ident, chip, tables, inside)
        tp[q, :NY, :] = temp
        cp[q, :NY, :] = conduct
        dp[q, :NY, :] = diag
        rp[q, :NY, :] = resid
        ez[q, :NY, :] = e_z

    def own_plane(q, _):
        put(q, t_ref[q], id_ref[q], chip_ref[q].astype(f32))
        return 0

    lax.fori_loop(0, NX, own_plane, 0, unroll=4)

    even_x = lax.rem(ix, 2) == 0
    low_x = jnp.where(ix > 0, 1.0, 0.0).astype(f32)
    high_x = jnp.where(ix < lax.axis_size("gx") - 1, 1.0, 0.0).astype(f32)
    zero_plane = jnp.zeros((NY, NZ), f32)

    def high_plane(k):
        return jnp.where(even_x, xb_ref[k], xa_ref[k])

    def low_plane(k):
        return jnp.where(even_x, xa_ref[k], xb_ref[k])

    for k in range(HIGH):
        chip = high_plane(8 + k) if k < 3 else zero_plane
        put(NX + k, high_plane(k), high_plane(4 + k), chip, high_x)
    for k in range(LOW):
        chip = low_plane(5 + k) if k > 0 else zero_plane
        put(NX + HIGH + k, low_plane(k), low_plane(3 + k), chip, low_x)

    surf_ref[...] = surface(own_rows(t_ref), 3)


def krylov_kernel(
    table_ref,
    tp_in,
    cp_in,
    dp_in,
    rp_in,
    ez_in,
    surf_ref,
    ya_ref,
    yb_ref,
    yca_ref,
    ycb_ref,
    tp,
    cp,
    dp,
    rp,
    ez,
    w0_ref,
    w1_ref,
    w2_ref,
    send_ref,
    ex,
    ey,
    dinv,
):
    del tp_in, cp_in, dp_in, rp_in, ez_in
    tables = [lambda k, j=j: table_ref[4 * j + k] for j in range(3)]
    ix = lax.axis_index("gx")
    iy = lax.axis_index("gy")
    last_x = lax.axis_size("gx") - 1
    last_y = lax.axis_size("gy") - 1
    sub = sublane((TILE, NZ))
    one = jnp.ones((), f32)
    low_x = jnp.where(ix > 0, 1.0, 0.0).astype(f32)
    high_x = jnp.where(ix < last_x, 1.0, 0.0).astype(f32)
    low_y = jnp.where(iy > 0, 1.0, 0.0).astype(f32)
    high_y = jnp.where(iy < last_y, 1.0, 0.0).astype(f32)
    rows_halo = jnp.where(sub < 4, high_y, low_y)

    even_y = lax.rem(iy, 2) == 0

    def high_row(q):
        return jnp.where(even_y, yb_ref[q], ya_ref[q])

    def low_row(q):
        return jnp.where(even_y, ya_ref[q], yb_ref[q])

    def chip_row(j):
        return jnp.where(even_y, ycb_ref[j], yca_ref[j])

    def put_halo(q, chip_high, plane_in):
        high = high_row(q)
        low = low_row(q)
        temp = jnp.where(sub < 4, high, low)
        ident = jnp.where(sub < 4, pltpu.roll(high, 4, 0), pltpu.roll(low, 3, 0))
        chip = jnp.where(sub < 4, chip_high, pltpu.roll(low, 6, 0))
        conduct, diag, resid, e_z = cells(temp, ident, chip, tables, rows_halo * plane_in)
        tp[q, NY:, :] = temp
        cp[q, NY:, :] = conduct
        dp[q, NY:, :] = diag
        rp[q, NY:, :] = resid
        ez[q, NY:, :] = e_z

    def own_halo_first(q, _):
        put_halo(q, chip_row(q), one)
        return 0

    def own_halo_second(q, _):
        put_halo(q, pltpu.roll(chip_row(q - PAIRS), 4, 0), one)
        return 0

    lax.fori_loop(0, PAIRS, own_halo_first, 0, unroll=20)
    lax.fori_loop(PAIRS, NX, own_halo_second, 0, unroll=12)

    zero_tile = jnp.zeros((TILE, NZ), f32)
    for q in range(NX, PX):
        put_halo(q, pltpu.roll(chip_row(q - PAIRS), 4, 0), high_x if q < NX + HIGH else low_x)

    subs = sublane((PY, NZ))
    rows_in = jnp.where(subs < NY, 1.0, jnp.where(subs < NY + 4, high_y, low_y)).astype(f32)

    def up_y(v):
        return pltpu.roll(v, PY - 1, 0)

    def down_y(v):
        return pltpu.roll(v, 1, 0)

    def fold(v):
        return (v[0:8] + v[8:16]) + (v[16:24] + v[24:32])

    def faces(q, nxt, ex_before, fx_before, plane_in):
        c0 = cp[q]
        t0 = tp[q]
        e_x = c0 + cp[nxt]
        f_x = e_x * (tp[nxt] - t0)
        e_y = c0 + up_y(c0)
        f_y = e_y * (up_y(t0) - t0)
        diag = dp[q] + ((e_x + ex_before) + (e_y + down_y(e_y)))
        inverse = (rows_in * plane_in) / diag
        resid = rp[q] + ((f_x - fx_before) + (f_y - down_y(f_y)))
        first = resid * inverse
        ex[q] = e_x
        ey[q] = e_y
        dinv[q] = inverse
        w0_ref[q] = first
        return e_x, f_x, resid, first

    e_first = cp[36] + cp[37]
    carry = (e_first, e_first * (tp[37] - tp[36]))
    for q, nxt in ((37, 38), (38, 0)):
        carry = faces(q, nxt, carry[0], carry[1], low_x)[:2]

    def faces_own(q, state):
        e_b, f_b, m0 = state
        e_x, f_x, resid, first = faces(q, q + 1, e_b, f_b, one)
        return e_x, f_x, m0 + fold(resid[:NY] * first[:NY])

    e_b, f_b, m0 = lax.fori_loop(0, NX, faces_own, (carry[0], carry[1], zero_tile), unroll=16)
    carry = (e_b, f_b)
    for q in (32, 33, 34):
        carry = faces(q, q + 1, carry[0], carry[1], high_x)[:2]

    def neighbours(src, q, nxt, g_before):
        v = src[q]
        e_x = ex[q]
        e_y = ey[q]
        e_z = ez[q]
        total = (e_x * src[nxt] + g_before) + (
            (e_y * up_y(v) + down_y(e_y * v)) + (e_z * up_z(v) + down_z(e_z * v))
        )
        return total, v, e_x * v

    def advance(src, dst, before, prologue, epilogue):
        carry = ex[before] * src[before]
        for q, nxt in prologue:
            total, _, carry = neighbours(src, q, nxt, carry)
            dst[q] = dinv[q] * total

        def step(q, state):
            g, ma, mb = state
            total, v, g = neighbours(src, q, q + 1, g)
            new = dinv[q] * total
            dst[q] = new
            ma = ma + fold(total[:NY] * v[:NY])
            mb = mb + fold(total[:NY] * new[:NY])
            return g, ma, mb

        carry, ma, mb = lax.fori_loop(0, NX, step, (carry, zero_tile, zero_tile), unroll=8)
        for q, nxt in epilogue:
            total, _, carry = neighbours(src, q, nxt, carry)
            dst[q] = dinv[q] * total
        return ma, mb

    m1, m2 = advance(w0_ref, w1_ref, 37, ((38, 0),), ((32, 33), (33, 34)))

    def crossing(q, v, after):
        half = ex[q] * after + (ey[q] * up_y(v) + ez[q] * up_z(v))
        return fold(half[:NY] * v[:NY])

    def second(q, g):
        total, v, g = neighbours(w1_ref, q, q + 1, g)
        new = dinv[q] * total
        w2_ref[q] = new
        return g, new, fold(total[:NY] * v[:NY]), fold(total[:NY] * new[:NY])

    g, before, m3, m4 = second(0, ex[38] * w1_ref[38])

    def step_2(q, state):
        g, before, ma, mb, mc = state
        g, new, a, b = second(q, g)
        return g, new, ma + a, mb + b, mc + crossing(q - 1, before, new)

    g, before, m3, m4, m5 = lax.fori_loop(
        1, NX, step_2, (g, before, m3, m4, zero_tile), unroll=31
    )
    total, _, _ = neighbours(w1_ref, NX, NX + 1, g)
    m5 = m5 + crossing(NX - 1, before, dinv[NX] * total)
    m5 = m5 + m5

    lanes = lane((HALF, NZ))
    moments = jnp.zeros((HALF, NZ), f32)
    for k, m in enumerate((m0, m1, m2, m3, m4, m5)):
        m = jnp.sum(jnp.sum(m, axis=0, keepdims=True), axis=1, keepdims=True)
        moments = jnp.where(lanes == k, jnp.broadcast_to(m, (HALF, NZ)), moments)
    fields = [surf_ref[...]] + [surface(own_rows(w), 2) for w in (w0_ref, w1_ref, w2_ref)]
    halves = [tile[i : i + HALF] for tile in fields for i in (0, HALF)] + [moments]
    for k in range(send_ref.shape[0]):
        for j, half in enumerate(halves):
            send_ref[k, j] = half


def lookup_kernel(hot_ref, row_ref, lane_ref, table_ref, out_ref, parts, start):
    blocks = table_ref.shape[0]
    targets = hot_ref.shape[0]
    sub = sublane((TILE, NZ))
    zero = jnp.zeros((TILE, NZ), f32)
    fields = FIELDS - 1

    def tile(a, f):
        return jnp.concatenate([table_ref[a, 2 * f], table_ref[a, 2 * f + 1]], axis=0)

    for a in range(blocks):
        start[a] = tile(a, 0)
    for f in range(fields):
        rest = jnp.concatenate([tile(a, f + 1) for a in range(blocks)], axis=0).T
        for k in range(2):
            part = rest.astype(bf16)
            parts[NZ * f : NZ * (f + 1), NZ * k : NZ * (k + 1)] = part
            rest = rest - part.astype(f32)

    total = table_ref[0, 2 * FIELDS]
    for a in range(1, blocks):
        total = total + table_ref[a, 2 * FIELDS]

    def one(b, _):
        row_of = row_ref[b]
        lane_of = lane_ref[b]
        found = [zero] * FIELDS
        for pair in range(0, TILE, 2):
            hot = hot_ref[b, :, NZ * pair : NZ * (pair + 2)]
            hot = jnp.concatenate([hot, hot], axis=0)
            lanes = [jnp.broadcast_to(lane_of[pair + i : pair + i + 1], (TILE, NZ)) for i in (0, 1)]
            offset = [e - sub for e in lanes]
            for i in (0, 1):
                rows = jnp.broadcast_to(row_of[pair + i : pair + i + 1], (TILE, NZ)) - sub
                acc = zero
                for a in range(blocks):
                    got = jnp.take_along_axis(start[a], lanes[i], axis=1)
                    acc = jnp.where(rows == a * TILE, got, acc)
                found[0] = jnp.where(
                    sub == pair + i, jnp.sum(acc, axis=0, keepdims=True), found[0]
                )
            for f in range(fields):
                line = jnp.dot(parts[NZ * f : NZ * (f + 1)], hot, preferred_element_type=f32)
                for i in (0, 1):
                    acc = zero
                    for t in range(NZ // TILE):
                        acc = jnp.where(
                            offset[i] == t * TILE,
                            line[TILE * t : TILE * (t + 1), NZ * i : NZ * (i + 1)],
                            acc,
                        )
                    found[f + 1] = jnp.where(
                        sub == pair + i, jnp.sum(acc, axis=0, keepdims=True), found[f + 1]
                    )
        for f in range(FIELDS):
            out_ref[b, 2 * f] = found[f][:HALF]
            out_ref[b, 2 * f + 1] = found[f][HALF:]
        out_ref[b, 2 * FIELDS] = total
        return 0

    lax.fori_loop(0, targets, one, 0, unroll=4)


def cg_coefficients(m):
    a = [m[j] - m[j + 1] for j in range(5)]

    def quadratic(v, h):
        total = None
        for i in range(3):
            for j in range(3):
                if v[i] is None or v[j] is None:
                    continue
                term = v[i] * v[j] * h[i + j]
                total = term if total is None else total + term
        return total

    def add(u, v):
        return v if u is None else u if v is None else u + v

    def scale(s, v):
        return [None if e is None else s * e for e in v]

    one = jnp.ones_like(m[0])
    z = [one, None, None]
    p = [one, None, None]
    rz = m[0]
    x = [None, None, None]
    for step in range(3):
        alpha = rz / quadratic(p, a)
        x = [add(e, g) for e, g in zip(x, scale(alpha, p))]
        if step < 2:
            ap = scale(alpha, p)
            moved = [None] + ap[:2]
            z = [
                add(add(z[i], None if ap[i] is None else -ap[i]), moved[i]) for i in range(3)
            ]
            new = quadratic(z, m)
            p = [add(z[i], e) for i, e in enumerate(scale(new / rz, p))]
            rz = new
    return x


def final_kernel(
    got_ref,
    pressure_hbm,
    t_ref,
    w0_ref,
    w1_ref,
    w2_ref,
    temp_hbm,
    growth_ref,
    pressure_ref,
    temp_ref,
    sem,
    out_sems,
):
    copy = pltpu.make_async_copy(pressure_hbm, pressure_ref, sem)
    copy.start()
    total = got_ref[0]
    for b in range(1, got_ref.shape[0]):
        total = total + got_ref[b]
    m = [total[2 * FIELDS, 0:1, k : k + 1] for k in range(6)]
    fields = [jnp.concatenate([total[2 * f], total[2 * f + 1]], axis=0) for f in range(FIELDS)]
    c = cg_coefficients(m)
    c_tile = [jnp.broadcast_to(e, (TILE, NZ)) for e in c]
    c_plane = [jnp.broadcast_to(e, (NY, NZ)) for e in c]

    def plane(q, _):
        temp_ref[q] = (
            t_ref[q, :NY, :]
            + c_plane[0] * w0_ref[q, :NY, :]
            + c_plane[1] * w1_ref[q, :NY, :]
            + c_plane[2] * w2_ref[q, :NY, :]
        )
        return 0

    outs = []
    step = NX // 4
    for k in range(4):
        lax.fori_loop(step * k, step * (k + 1), plane, 0, unroll=4)
        part = pl.ds(step * k, step)
        outs.append(pltpu.make_async_copy(temp_ref.at[part], temp_hbm.at[part], out_sems.at[k]))
        outs[-1].start()

    flank = fields[0]
    for k in range(3):
        flank = flank + c_tile[k] * fields[k + 1]
    soft = jnp.maximum(flank, 0.0) + jnp.log1p(jnp.exp(-jnp.abs(flank)))
    copy.wait()
    growth_ref[...] = usui_rate * pressure_ref[...] * jnp.exp(-usui_energy / (1.0 + soft))
    for out in outs:
        out.wait()


def local(
    prior_kelvin_state,
    substance_identifier,
    chip_touch_indicator,
    substance_reference_diffusivity,
    substance_diffusivity_gradient,
    substance_storage_coefficient,
    clearance_point_indices,
    clearance_face_pressure,
):
    size_x = lax.axis_size("gx")
    size_y = lax.axis_size("gy")
    temp, ident, chip = prior_kelvin_state, substance_identifier, chip_touch_indicator
    vmem = pl.BlockSpec(memory_space=pltpu.VMEM)

    def params(mib):
        return pltpu.CompilerParams(vmem_limit_bytes=mib * MIB)


    anywhere = pl.BlockSpec(memory_space=pltpu.HBM)

    def arr(*shape, dtype=f32):
        return jax.ShapeDtypeStruct(shape, dtype)

    def buf(*shape, dtype=f32):
        return pltpu.VMEM(shape, dtype)

    def in_hbm(*arrays):
        return [pltpu.with_memory_space_constraint(a, pltpu.HBM) for a in arrays]

    i32 = jnp.int32
    xa, xb, ya, yb, yc, sites = pl.pallas_call(
        pack_kernel,
        name="pack",
        in_specs=[anywhere] * 4,
        out_specs=[vmem] * 6,
        out_shape=[
            arr(11, NY, NZ),
            arr(11, NY, NZ),
            arr(PX, TILE, NZ),
            arr(PX, TILE, NZ),
            arr(PAIRS, TILE, NZ),
            arr(size_y, TILE, NZ, dtype=i32),
        ],
        scratch_shapes=[
            buf(NX, TILE, NZ),
            buf(NX, TILE, NZ),
            buf(NX, TILE, NZ, dtype=i32),
            buf(NX, TILE, NZ, dtype=i32),
            buf(NX, TILE, NZ, dtype=i32),
            buf(NX, TILE, NZ, dtype=i32),
            buf(HIGH, NY, NZ),
            buf(HIGH, NY, NZ),
            buf(HIGH, NY, NZ, dtype=i32),
            buf(HIGH, NY, NZ, dtype=i32),
            buf(HIGH, NY, NZ, dtype=i32),
            buf(HIGH, NY, NZ, dtype=i32),
            buf(TILE, NZ, dtype=i32),
            pltpu.SemaphoreType.DMA((13,)),
        ],
        compiler_params=params(10),
    )(*in_hbm(temp, ident, chip, clearance_point_indices.reshape(TILE, NZ)))
    sites = lax.all_to_all(sites, "gy", 0, 0)

    xa = lax.ppermute(xa, "gx", swaps(size_x, 1))
    xb = lax.ppermute(xb, "gx", swaps(size_x, 0))
    ya, yb, yc, sites = pl.pallas_call(
        corner_kernel,
        name="corners",
        in_specs=[vmem] * 6,
        out_specs=[vmem] * 4,
        out_shape=[
            arr(PX, TILE, NZ),
            arr(PX, TILE, NZ),
            arr(PAIRS, TILE, NZ),
            arr(size_y, TILE, NZ, dtype=i32),
        ],
        input_output_aliases={0: 0, 1: 1, 2: 2, 5: 3},
        compiler_params=params(8),
    )(ya, yb, yc, xa, xb, sites)
    ya = lax.ppermute(ya, "gy", swaps(size_y, 1))
    yca = lax.ppermute(yc, "gy", swaps(size_y, 1))
    yb = lax.ppermute(yb, "gy", swaps(size_y, 0))
    ycb = lax.ppermute(yc, "gy", swaps(size_y, 0))

    tables = (
        substance_reference_diffusivity,
        substance_diffusivity_gradient,
        substance_storage_coefficient,
    )
    padded = arr(PX, PY, NZ)
    *own, hot, row, place, table_tiles = pl.pallas_call(
        own_kernel,
        name="own_cells",
        in_specs=[anywhere] * 6 + [vmem] * 3,
        out_specs=[vmem] * 10,
        out_shape=[padded] * 5
        + [
            arr(TILE, NZ),
            arr(size_y, NZ, TILE * NZ, dtype=bf16),
            arr(size_y, TILE, NZ, dtype=i32),
            arr(size_y, TILE, NZ, dtype=i32),
            arr(12, TILE, NZ),
        ],
        scratch_shapes=[
            buf(NX, NY, NZ),
            buf(NX, NY, NZ, dtype=i32),
            buf(NX, NY, NZ, dtype=i32),
            pltpu.SMEM((4,), f32),
            pltpu.SMEM((4,), f32),
            pltpu.SMEM((4,), f32),
            pltpu.SemaphoreType.DMA((6,)),
        ],
        compiler_params=params(14),
    )(*in_hbm(*tables, temp, ident, chip), xa, xb, sites)

    start, _, _, _, _, w0, w1, w2, send = pl.pallas_call(
        krylov_kernel,
        name="krylov",
        in_specs=[vmem] * 11,
        out_specs=[vmem] * 9,
        out_shape=[padded] * 8 + [arr(size_x, BLOCK, HALF, NZ)],
        input_output_aliases={1: 0, 2: 1, 3: 2, 4: 3, 5: 4},
        scratch_shapes=[buf(PX, PY, NZ)] * 3,
        compiler_params=params(24),
    )(table_tiles, *own, ya, yb, yca, ycb)
    table = lax.all_to_all(send, "gx", 0, 0)
    found = pl.pallas_call(
        lookup_kernel,
        name="lookup",
        in_specs=[vmem] * 4,
        out_specs=vmem,
        out_shape=arr(size_y, BLOCK, HALF, NZ),
        scratch_shapes=[
            buf(NZ * (FIELDS - 1), 2 * NZ, dtype=bf16),
            buf(size_x, TILE, NZ),
        ],
        compiler_params=params(20),
    )(hot, row, place, table)
    got = lax.all_to_all(found, "gy", 0, 0)
    temperature, growth = pl.pallas_call(
        final_kernel,
        name="finish",
        in_specs=[vmem, anywhere, vmem, vmem, vmem, vmem],
        out_specs=[anywhere, vmem],
        out_shape=[arr(NX, NY, NZ), arr(TILE, NZ)],
        scratch_shapes=[
            buf(TILE, NZ),
            buf(NX, NY, NZ),
            pltpu.SemaphoreType.DMA(()),
            pltpu.SemaphoreType.DMA((4,)),
        ],
        compiler_params=params(12),
    )(got, *in_hbm(clearance_face_pressure.reshape(TILE, NZ)), start, w0, w1, w2)
    return temperature, growth.reshape(-1)


def solution(mesh):
    in_specs = (
        P("gx", "gy", None),
        P("gx", "gy", None),
        P("gx", "gy", None),
        P(),
        P(),
        P(),
        P(("gx", "gy")),
        P(("gx", "gy")),
    )
    out_specs = (P("gx", "gy", None), P(("gx", "gy")))
    return jax.shard_map(local, mesh=mesh, in_specs=in_specs, out_specs=out_specs, check_vma=False)
```

```python
import jax
import jax.numpy as jnp
from jax import lax
from jax.experimental import pallas as pl
from jax.experimental.pallas import tpu as pltpu
from jax.sharding import PartitionSpec as P

clock_advance = 2.0
interface_warming_rate = 3.0
usui_rate = 3.0
usui_energy = 4.0
kelvin_shift_amount = 2.0

LOW = 3
HIGH = 4
NX = 32
NY = 32
NZ = 128
PX = NX + HIGH + LOW
PY = NY + 8
FIELDS = 4
TILE = 8
PART = 2
PARTS = TILE // PART
BLOCK = PARTS * FIELDS + 1
PAIRS = 20
MIB = 1024 * 1024
f32 = jnp.float32
bf16 = jnp.bfloat16


def swaps(count, first):
    low = range(first, count - 1, 2)
    return [(i, i + 1) for i in low] + [(i + 1, i) for i in low]


def sublane(shape):
    return lax.broadcasted_iota(jnp.int32, shape, len(shape) - 2)


def lane(shape):
    return lax.broadcasted_iota(jnp.int32, shape, len(shape) - 1)


def first_tile(sub, temp, ident):
    return jnp.where(sub < 4, temp, pltpu.roll(ident, 4, 0))


def last_tile(sub, temp, ident, chip):
    return jnp.where(
        sub >= 5, temp, jnp.where(sub >= 2, pltpu.roll(ident, 5, 0), pltpu.roll(chip, 2, 0))
    )


def pack_kernel(
    t_hbm,
    id_hbm,
    chip_hbm,
    site_hbm,
    xa,
    xb,
    ya,
    yb,
    sites,
    t_a,
    t_b,
    i_a,
    i_b,
    c_a,
    c_b,
    t_p,
    t_m,
    i_p,
    i_m,
    c_p,
    c_m,
    site_ref,
    sems,
):
    copies = []
    for k, (src, dst) in enumerate(
        (
            (t_hbm.at[pl.ds(0, HIGH)], t_p),
            (id_hbm.at[pl.ds(0, HIGH)], i_p),
            (chip_hbm.at[pl.ds(0, HIGH)], c_p),
            (t_hbm.at[pl.ds(NX - HIGH, HIGH)], t_m),
            (id_hbm.at[pl.ds(NX - HIGH, HIGH)], i_m),
            (chip_hbm.at[pl.ds(NX - HIGH, HIGH)], c_m),
            (t_hbm.at[:, pl.ds(0, TILE)], t_a),
            (id_hbm.at[:, pl.ds(0, TILE)], i_a),
            (chip_hbm.at[:, pl.ds(0, TILE)], c_a),
            (t_hbm.at[:, pl.ds(NY - TILE, TILE)], t_b),
            (id_hbm.at[:, pl.ds(NY - TILE, TILE)], i_b),
            (chip_hbm.at[:, pl.ds(NY - TILE, TILE)], c_b),
            (site_hbm, site_ref),
        )
    ):
        copies.append(pltpu.make_async_copy(src, dst, sems.at[k]))
        copies[-1].start()
    for copy in copies[:6]:
        copy.wait()

    def x_sides(low, high):
        for k in range(HIGH):
            low[k] = t_p[k]
            low[4 + k] = i_p[k].astype(f32)
            if k < 3:
                low[8 + k] = c_p[k].astype(f32)
                high[k] = t_m[1 + k]
                high[3 + k] = i_m[1 + k].astype(f32)
            if k < 2:
                high[6 + k] = c_m[2 + k].astype(f32)

    even_x = lax.rem(lax.axis_index("gx"), 2) == 0
    even_y = lax.rem(lax.axis_index("gy"), 2) == 0

    @pl.when(even_x)
    def _():
        x_sides(xa, xb)

    @pl.when(jnp.logical_not(even_x))
    def _():
        x_sides(xb, xa)

    for copy in copies[6:]:
        copy.wait()
    sub = sublane((TILE, NZ))

    def own(q, _):
        low = first_tile(sub, t_a[q], i_a[q].astype(f32))
        high = last_tile(sub, t_b[q], i_b[q].astype(f32), c_b[q].astype(f32))
        ya[q] = jnp.where(even_y, low, high)
        yb[q] = jnp.where(even_y, high, low)
        return 0

    lax.fori_loop(0, NX, own, 0, unroll=8)
    for j in range(PAIRS):
        tile = c_a[j].astype(f32)
        if j + PAIRS < NX:
            tile = jnp.where(sub < 4, tile, pltpu.roll(c_a[j + PAIRS].astype(f32), 4, 0))
        ya[PX + j] = tile
        yb[PX + j] = tile
    for k in range(sites.shape[0]):
        sites[k] = site_ref[...]


def corner_kernel(ya_in, yb_in, xa_ref, xb_ref, sites_in, ya, yb, sites_out):
    del ya_in, yb_in, sites_in, sites_out
    even_x = lax.rem(lax.axis_index("gx"), 2) == 0
    even_y = lax.rem(lax.axis_index("gy"), 2) == 0
    sub = sublane((TILE, NZ))
    zero = jnp.zeros((TILE, NZ), f32)
    first = pl.ds(0, TILE)
    last = pl.ds(NY - TILE, TILE)

    def high_side(k, rows):
        return jnp.where(even_x, xb_ref[k, rows, :], xa_ref[k, rows, :])

    def low_side(k, rows):
        return jnp.where(even_x, xa_ref[k, rows, :], xb_ref[k, rows, :])

    for k in range(HIGH + LOW):
        q = NX + k
        if k < HIGH:
            side, places = high_side, (k, 4 + k, 8 + k if k < 3 else None)
        else:
            j = k - HIGH
            side, places = low_side, (j, 3 + j, 5 + j if j else None)
        temp, ident, chip = places
        low = first_tile(sub, side(temp, first), side(ident, first))
        high = last_tile(
            sub, side(temp, last), side(ident, last), zero if chip is None else side(chip, last)
        )
        ya[q] = jnp.where(even_y, low, high)
        yb[q] = jnp.where(even_y, high, low)
        if chip is not None:
            place = PX + q - PAIRS
            tile = jnp.where(sub < 4, ya[place], pltpu.roll(side(chip, first), 4, 0))
            ya[place] = tile
            yb[place] = tile


def pick(ident, table):
    low = jnp.where(ident == 1, table(1), table(0))
    high = jnp.where(ident == 3, table(3), table(2))
    return jnp.where(ident >= 2, high, low)


def up_z(v):
    return pltpu.roll(v, NZ - 1, 1)


def down_z(v):
    return pltpu.roll(v, 1, 1)


def cells(temp, ident, chip, tables, inside=None):
    ref_ref, grad_ref, store_ref = tables
    conduct = pick(ident, ref_ref) * (
        1.0 + pick(ident, grad_ref) * jnp.tanh(temp - kelvin_shift_amount)
    )
    if inside is not None:
        conduct = conduct * inside
    lanes = lane(temp.shape)
    inner_z = jnp.where(lanes < NZ - 1, 1.0, 0.0).astype(f32)
    edge_z = jnp.where((lanes == 0) | (lanes == NZ - 1), 1.0, 0.0).astype(f32)
    e_z = (conduct + up_z(conduct)) * inner_z
    f_z = e_z * (up_z(temp) - temp)
    c_b = conduct * edge_z
    diag = (pick(ident, store_ref) + c_b) + (e_z + down_z(e_z))
    resid = (clock_advance * interface_warming_rate * chip - c_b * temp) + (f_z - down_z(f_z))
    return conduct, diag, resid, e_z


def surface(read, terms):
    rows = sublane((TILE, NZ))
    diagonal = sublane((NZ, NZ)) == lane((NZ, NZ))
    first = jnp.where(sublane((NZ, NZ)) == 0, 1.0, 0.0).astype(bf16)
    total = jnp.zeros((TILE, NZ), f32)
    for s in range(TILE):
        rest = read(s)
        line = jnp.zeros((NZ, NZ), f32)
        for _ in range(terms):
            part = rest.astype(bf16)
            line = line + jnp.dot(part, first, preferred_element_type=f32)
            rest = rest - part.astype(f32)
        line = jnp.sum(jnp.where(diagonal, line, 0.0), axis=0, keepdims=True)
        total = jnp.where(rows == s, line, total)
    return total


def own_rows(ref):
    per = NX // TILE
    return lambda s: jnp.concatenate([ref[per * s + i, :NY, :] for i in range(per)], axis=0)


def own_kernel(
    ref_hbm,
    grad_hbm,
    store_hbm,
    t_hbm,
    id_hbm,
    chip_hbm,
    xa_ref,
    xb_ref,
    site_ref,
    tp,
    cp,
    dp,
    rp,
    ez,
    surf_ref,
    hot_ref,
    row_ref,
    lane_ref,
    table_ref,
    t_ref,
    id_ref,
    chip_ref,
    ref_ref,
    grad_ref,
    store_ref,
    sems,
):
    ix = lax.axis_index("gx")
    iy = lax.axis_index("gy")

    copies = [
        pltpu.make_async_copy(src, dst, sems.at[k])
        for k, (src, dst) in enumerate(
            (
                (ref_hbm, ref_ref),
                (grad_hbm, grad_ref),
                (store_hbm, store_ref),
                (t_hbm, t_ref),
                (id_hbm, id_ref),
                (chip_hbm, chip_ref),
            )
        )
    ]
    for copy in copies:
        copy.start()

    width = NY * lax.axis_size("gy")
    subs = sublane((NZ, NZ))

    def places(b, _):
        site = site_ref[b]
        row = site // width
        col = site - row * width
        here = (col // NY) == iy
        cell = (row % NX) * NY + col % NY
        row_of = jnp.where(here, (row // NX) * TILE + cell // NZ, -1)
        row_ref[b] = row_of
        lane_ref[b] = cell % NZ
        for s in range(TILE):
            hit = subs == jnp.broadcast_to(row_of[s : s + 1], (NZ, NZ))
            hot_ref[b, :, NZ * s : NZ * (s + 1)] = jnp.where(hit, 1.0, 0.0).astype(bf16)
        return 0

    lax.fori_loop(0, site_ref.shape[0], places, 0, unroll=2)
    for copy in copies:
        copy.wait()

    tables = [lambda k, ref=ref: ref[k] for ref in (ref_ref, grad_ref, store_ref)]
    for j, table in enumerate(tables):
        for k in range(4):
            table_ref[4 * j + k] = jnp.full((TILE, NZ), table(k), f32)

    def put(q, temp, ident, chip, inside=None):
        conduct, diag, resid, e_z = cells(temp, ident, chip, tables, inside)
        tp[q, :NY, :] = temp
        cp[q, :NY, :] = conduct
        dp[q, :NY, :] = diag
        rp[q, :NY, :] = resid
        ez[q, :NY, :] = e_z

    def own_plane(q, _):
        put(q, t_ref[q], id_ref[q], chip_ref[q].astype(f32))
        return 0

    lax.fori_loop(0, NX, own_plane, 0, unroll=4)

    even_x = lax.rem(ix, 2) == 0
    low_x = jnp.where(ix > 0, 1.0, 0.0).astype(f32)
    high_x = jnp.where(ix < lax.axis_size("gx") - 1, 1.0, 0.0).astype(f32)
    zero_plane = jnp.zeros((NY, NZ), f32)

    def high_plane(k):
        return jnp.where(even_x, xb_ref[k], xa_ref[k])

    def low_plane(k):
        return jnp.where(even_x, xa_ref[k], xb_ref[k])

    for k in range(HIGH):
        chip = high_plane(8 + k) if k < 3 else zero_plane
        put(NX + k, high_plane(k), high_plane(4 + k), chip, high_x)
    for k in range(LOW):
        chip = low_plane(5 + k) if k > 0 else zero_plane
        put(NX + HIGH + k, low_plane(k), low_plane(3 + k), chip, low_x)

    surf_ref[...] = surface(own_rows(t_ref), 3)


def krylov_kernel(
    table_ref,
    tp_in,
    cp_in,
    dp_in,
    rp_in,
    ez_in,
    surf_ref,
    ya_ref,
    yb_ref,
    tp,
    cp,
    dp,
    rp,
    ez,
    w0_ref,
    w1_ref,
    w2_ref,
    send_ref,
    ex,
    ey,
    dinv,
):
    del tp_in, cp_in, dp_in, rp_in, ez_in
    tables = [lambda k, j=j: table_ref[4 * j + k] for j in range(3)]
    ix = lax.axis_index("gx")
    iy = lax.axis_index("gy")
    last_x = lax.axis_size("gx") - 1
    last_y = lax.axis_size("gy") - 1
    sub = sublane((TILE, NZ))
    one = jnp.ones((), f32)
    low_x = jnp.where(ix > 0, 1.0, 0.0).astype(f32)
    high_x = jnp.where(ix < last_x, 1.0, 0.0).astype(f32)
    low_y = jnp.where(iy > 0, 1.0, 0.0).astype(f32)
    high_y = jnp.where(iy < last_y, 1.0, 0.0).astype(f32)
    rows_halo = jnp.where(sub < 4, high_y, low_y)

    even_y = lax.rem(iy, 2) == 0

    def high_row(q):
        return jnp.where(even_y, yb_ref[q], ya_ref[q])

    def low_row(q):
        return jnp.where(even_y, ya_ref[q], yb_ref[q])

    def put_halo(q, chip_high, plane_in):
        high = high_row(q)
        low = low_row(q)
        temp = jnp.where(sub < 4, high, low)
        ident = jnp.where(sub < 4, pltpu.roll(high, 4, 0), pltpu.roll(low, 3, 0))
        chip = jnp.where(sub < 4, chip_high, pltpu.roll(low, 6, 0))
        conduct, diag, resid, e_z = cells(temp, ident, chip, tables, rows_halo * plane_in)
        tp[q, NY:, :] = temp
        cp[q, NY:, :] = conduct
        dp[q, NY:, :] = diag
        rp[q, NY:, :] = resid
        ez[q, NY:, :] = e_z

    def own_halo_first(q, _):
        put_halo(q, high_row(PX + q), one)
        return 0

    def own_halo_second(q, _):
        put_halo(q, pltpu.roll(high_row(PX + q - PAIRS), 4, 0), one)
        return 0

    lax.fori_loop(0, PAIRS, own_halo_first, 0, unroll=20)
    lax.fori_loop(PAIRS, NX, own_halo_second, 0, unroll=12)

    zero_tile = jnp.zeros((TILE, NZ), f32)
    for q in range(NX, PX):
        put_halo(q, pltpu.roll(high_row(PX + q - PAIRS), 4, 0), high_x if q < NX + HIGH else low_x)

    subs = sublane((PY, NZ))
    rows_in = jnp.where(subs < NY, 1.0, jnp.where(subs < NY + 4, high_y, low_y)).astype(f32)

    def up_y(v):
        return pltpu.roll(v, PY - 1, 0)

    def down_y(v):
        return pltpu.roll(v, 1, 0)

    def fold(v):
        return (v[0:8] + v[8:16]) + (v[16:24] + v[24:32])

    def faces(q, nxt, ex_before, fx_before, plane_in):
        c0 = cp[q]
        t0 = tp[q]
        e_x = c0 + cp[nxt]
        f_x = e_x * (tp[nxt] - t0)
        e_y = c0 + up_y(c0)
        f_y = e_y * (up_y(t0) - t0)
        diag = dp[q] + ((e_x + ex_before) + (e_y + down_y(e_y)))
        inverse = (rows_in * plane_in) / diag
        resid = rp[q] + ((f_x - fx_before) + (f_y - down_y(f_y)))
        first = resid * inverse
        ex[q] = e_x
        ey[q] = e_y
        dinv[q] = inverse
        w0_ref[q] = first
        return e_x, f_x, resid, first

    e_first = cp[36] + cp[37]
    carry = (e_first, e_first * (tp[37] - tp[36]))
    for q, nxt in ((37, 38), (38, 0)):
        carry = faces(q, nxt, carry[0], carry[1], low_x)[:2]

    def faces_own(q, state):
        e_b, f_b, m0 = state
        e_x, f_x, resid, first = faces(q, q + 1, e_b, f_b, one)
        return e_x, f_x, m0 + fold(resid[:NY] * first[:NY])

    e_b, f_b, m0 = lax.fori_loop(0, NX, faces_own, (carry[0], carry[1], zero_tile), unroll=16)
    carry = (e_b, f_b)
    for q in (32, 33, 34):
        carry = faces(q, q + 1, carry[0], carry[1], high_x)[:2]

    def neighbours(src, q, nxt, g_before):
        v = src[q]
        e_x = ex[q]
        e_y = ey[q]
        e_z = ez[q]
        total = (e_x * src[nxt] + g_before) + (
            (e_y * up_y(v) + down_y(e_y * v)) + (e_z * up_z(v) + down_z(e_z * v))
        )
        return total, v, e_x * v

    def advance(src, dst, before, prologue, epilogue):
        carry = ex[before] * src[before]
        for q, nxt in prologue:
            total, _, carry = neighbours(src, q, nxt, carry)
            dst[q] = dinv[q] * total

        def step(q, state):
            g, ma, mb = state
            total, v, g = neighbours(src, q, q + 1, g)
            new = dinv[q] * total
            dst[q] = new
            ma = ma + fold(total[:NY] * v[:NY])
            mb = mb + fold(total[:NY] * new[:NY])
            return g, ma, mb

        carry, ma, mb = lax.fori_loop(0, NX, step, (carry, zero_tile, zero_tile), unroll=8)
        for q, nxt in epilogue:
            total, _, carry = neighbours(src, q, nxt, carry)
            dst[q] = dinv[q] * total
        return ma, mb

    m1, m2 = advance(w0_ref, w1_ref, 37, ((38, 0),), ((32, 33), (33, 34)))

    def crossing(q, v, after):
        half = ex[q] * after + (ey[q] * up_y(v) + ez[q] * up_z(v))
        return fold(half[:NY] * v[:NY])

    def second(q, g):
        total, v, g = neighbours(w1_ref, q, q + 1, g)
        new = dinv[q] * total
        w2_ref[q] = new
        return g, new, fold(total[:NY] * v[:NY]), fold(total[:NY] * new[:NY])

    g, before, m3, m4 = second(0, ex[38] * w1_ref[38])

    def step_2(q, state):
        g, before, ma, mb, mc = state
        g, new, a, b = second(q, g)
        return g, new, ma + a, mb + b, mc + crossing(q - 1, before, new)

    g, before, m3, m4, m5 = lax.fori_loop(
        1, NX, step_2, (g, before, m3, m4, zero_tile), unroll=31
    )
    total, _, _ = neighbours(w1_ref, NX, NX + 1, g)
    m5 = m5 + crossing(NX - 1, before, dinv[NX] * total)
    m5 = m5 + m5

    lanes = lane((PART, NZ))
    moments = jnp.zeros((PART, NZ), f32)
    for k, m in enumerate((m0, m1, m2, m3, m4, m5)):
        m = jnp.sum(jnp.sum(m, axis=0, keepdims=True), axis=1, keepdims=True)
        moments = jnp.where(lanes == k, jnp.broadcast_to(m, (PART, NZ)), moments)
    fields = [surf_ref[...]] + [surface(own_rows(w), 2) for w in (w0_ref, w1_ref, w2_ref)]
    pieces = [tile[i : i + PART] for tile in fields for i in range(0, TILE, PART)] + [moments]
    for k in range(send_ref.shape[0]):
        for j, piece in enumerate(pieces):
            send_ref[k, j] = piece


def lookup_kernel(hot_ref, row_ref, lane_ref, table_ref, out_ref, parts, start):
    blocks = table_ref.shape[0]
    targets = hot_ref.shape[0]
    sub = sublane((TILE, NZ))
    zero = jnp.zeros((TILE, NZ), f32)
    fields = FIELDS - 1

    def tile(a, f):
        return jnp.concatenate([table_ref[a, PARTS * f + i] for i in range(PARTS)], axis=0)

    for a in range(blocks):
        start[a] = tile(a, 0)
    for f in range(fields):
        rest = jnp.concatenate([tile(a, f + 1) for a in range(blocks)], axis=0).T
        for k in range(2):
            part = rest.astype(bf16)
            parts[NZ * f : NZ * (f + 1), NZ * k : NZ * (k + 1)] = part
            rest = rest - part.astype(f32)

    total = table_ref[0, PARTS * FIELDS]
    for a in range(1, blocks):
        total = total + table_ref[a, PARTS * FIELDS]

    def one(b, _):
        row_of = row_ref[b]
        lane_of = lane_ref[b]
        found = [zero] * FIELDS
        for pair in range(0, TILE, 2):
            hot = hot_ref[b, :, NZ * pair : NZ * (pair + 2)]
            hot = jnp.concatenate([hot, hot], axis=0)
            lanes = [jnp.broadcast_to(lane_of[pair + i : pair + i + 1], (TILE, NZ)) for i in (0, 1)]
            offset = [e - sub for e in lanes]
            for i in (0, 1):
                rows = jnp.broadcast_to(row_of[pair + i : pair + i + 1], (TILE, NZ)) - sub
                acc = zero
                for a in range(blocks):
                    got = jnp.take_along_axis(start[a], lanes[i], axis=1)
                    acc = jnp.where(rows == a * TILE, got, acc)
                found[0] = jnp.where(
                    sub == pair + i, jnp.sum(acc, axis=0, keepdims=True), found[0]
                )
            for f in range(fields):
                line = jnp.dot(parts[NZ * f : NZ * (f + 1)], hot, preferred_element_type=f32)
                for i in (0, 1):
                    acc = zero
                    for t in range(NZ // TILE):
                        acc = jnp.where(
                            offset[i] == t * TILE,
                            line[TILE * t : TILE * (t + 1), NZ * i : NZ * (i + 1)],
                            acc,
                        )
                    found[f + 1] = jnp.where(
                        sub == pair + i, jnp.sum(acc, axis=0, keepdims=True), found[f + 1]
                    )
        for f in range(FIELDS):
            for i in range(PARTS):
                out_ref[b, PARTS * f + i] = found[f][PART * i : PART * (i + 1)]
        out_ref[b, PARTS * FIELDS] = total
        return 0

    lax.fori_loop(0, targets, one, 0, unroll=8)


def cg_coefficients(m):
    a = [m[j] - m[j + 1] for j in range(5)]

    def quadratic(v, h):
        total = None
        for i in range(3):
            for j in range(3):
                if v[i] is None or v[j] is None:
                    continue
                term = v[i] * v[j] * h[i + j]
                total = term if total is None else total + term
        return total

    def add(u, v):
        return v if u is None else u if v is None else u + v

    def scale(s, v):
        return [None if e is None else s * e for e in v]

    one = jnp.ones_like(m[0])
    z = [one, None, None]
    p = [one, None, None]
    rz = m[0]
    x = [None, None, None]
    for step in range(3):
        alpha = rz / quadratic(p, a)
        x = [add(e, g) for e, g in zip(x, scale(alpha, p))]
        if step < 2:
            ap = scale(alpha, p)
            moved = [None] + ap[:2]
            z = [
                add(add(z[i], None if ap[i] is None else -ap[i]), moved[i]) for i in range(3)
            ]
            new = quadratic(z, m)
            p = [add(z[i], e) for i, e in enumerate(scale(new / rz, p))]
            rz = new
    return x


def final_kernel(
    got_ref,
    pressure_hbm,
    t_ref,
    w0_ref,
    w1_ref,
    w2_ref,
    temp_hbm,
    growth_ref,
    pressure_ref,
    temp_ref,
    sem,
    out_sems,
):
    copy = pltpu.make_async_copy(pressure_hbm, pressure_ref, sem)
    copy.start()
    total = got_ref[0]
    for b in range(1, got_ref.shape[0]):
        total = total + got_ref[b]
    m = [total[PARTS * FIELDS, 0:1, k : k + 1] for k in range(6)]
    fields = [
        jnp.concatenate([total[PARTS * f + i] for i in range(PARTS)], axis=0)
        for f in range(FIELDS)
    ]
    c = cg_coefficients(m)
    c_tile = [jnp.broadcast_to(e, (TILE, NZ)) for e in c]
    c_plane = [jnp.broadcast_to(e, (NY, NZ)) for e in c]

    def plane(q, _):
        temp_ref[q] = (
            t_ref[q, :NY, :]
            + c_plane[0] * w0_ref[q, :NY, :]
            + c_plane[1] * w1_ref[q, :NY, :]
            + c_plane[2] * w2_ref[q, :NY, :]
        )
        return 0

    outs = []
    step = NX // 4
    for k in range(4):
        lax.fori_loop(step * k, step * (k + 1), plane, 0, unroll=4)
        part = pl.ds(step * k, step)
        outs.append(pltpu.make_async_copy(temp_ref.at[part], temp_hbm.at[part], out_sems.at[k]))
        outs[-1].start()

    flank = fields[0]
    for k in range(3):
        flank = flank + c_tile[k] * fields[k + 1]
    soft = jnp.maximum(flank, 0.0) + jnp.log1p(jnp.exp(-jnp.abs(flank)))
    copy.wait()
    growth_ref[...] = usui_rate * pressure_ref[...] * jnp.exp(-usui_energy / (1.0 + soft))
    for out in outs:
        out.wait()


def local(
    prior_kelvin_state,
    substance_identifier,
    chip_touch_indicator,
    substance_reference_diffusivity,
    substance_diffusivity_gradient,
    substance_storage_coefficient,
    clearance_point_indices,
    clearance_face_pressure,
):
    size_x = lax.axis_size("gx")
    size_y = lax.axis_size("gy")
    temp, ident, chip = prior_kelvin_state, substance_identifier, chip_touch_indicator
    vmem = pl.BlockSpec(memory_space=pltpu.VMEM)

    def params(mib):
        return pltpu.CompilerParams(vmem_limit_bytes=mib * MIB)


    anywhere = pl.BlockSpec(memory_space=pltpu.HBM)

    def arr(*shape, dtype=f32):
        return jax.ShapeDtypeStruct(shape, dtype)

    def buf(*shape, dtype=f32):
        return pltpu.VMEM(shape, dtype)

    def in_hbm(*arrays):
        return [pltpu.with_memory_space_constraint(a, pltpu.HBM) for a in arrays]

    i32 = jnp.int32
    xa, xb, ya, yb, sites = pl.pallas_call(
        pack_kernel,
        name="pack",
        in_specs=[anywhere] * 4,
        out_specs=[vmem] * 5,
        out_shape=[
            arr(11, NY, NZ),
            arr(11, NY, NZ),
            arr(PX + PAIRS, TILE, NZ),
            arr(PX + PAIRS, TILE, NZ),
            arr(size_y, TILE, NZ, dtype=i32),
        ],
        scratch_shapes=[
            buf(NX, TILE, NZ),
            buf(NX, TILE, NZ),
            buf(NX, TILE, NZ, dtype=i32),
            buf(NX, TILE, NZ, dtype=i32),
            buf(NX, TILE, NZ, dtype=i32),
            buf(NX, TILE, NZ, dtype=i32),
            buf(HIGH, NY, NZ),
            buf(HIGH, NY, NZ),
            buf(HIGH, NY, NZ, dtype=i32),
            buf(HIGH, NY, NZ, dtype=i32),
            buf(HIGH, NY, NZ, dtype=i32),
            buf(HIGH, NY, NZ, dtype=i32),
            buf(TILE, NZ, dtype=i32),
            pltpu.SemaphoreType.DMA((13,)),
        ],
        compiler_params=params(10),
    )(*in_hbm(temp, ident, chip, clearance_point_indices.reshape(TILE, NZ)))
    sites = lax.all_to_all(sites, "gy", 0, 0)

    xa = lax.ppermute(xa, "gx", swaps(size_x, 1))
    xb = lax.ppermute(xb, "gx", swaps(size_x, 0))
    ya, yb, sites = pl.pallas_call(
        corner_kernel,
        name="corners",
        in_specs=[vmem] * 5,
        out_specs=[vmem] * 3,
        out_shape=[
            arr(PX + PAIRS, TILE, NZ),
            arr(PX + PAIRS, TILE, NZ),
            arr(size_y, TILE, NZ, dtype=i32),
        ],
        input_output_aliases={0: 0, 1: 1, 4: 2},
        compiler_params=params(8),
    )(ya, yb, xa, xb, sites)
    ya = lax.ppermute(ya, "gy", swaps(size_y, 1))
    yb = lax.ppermute(yb, "gy", swaps(size_y, 0))

    tables = (
        substance_reference_diffusivity,
        substance_diffusivity_gradient,
        substance_storage_coefficient,
    )
    padded = arr(PX, PY, NZ)
    *own, hot, row, place, table_tiles = pl.pallas_call(
        own_kernel,
        name="own_cells",
        in_specs=[anywhere] * 6 + [vmem] * 3,
        out_specs=[vmem] * 10,
        out_shape=[padded] * 5
        + [
            arr(TILE, NZ),
            arr(size_y, NZ, TILE * NZ, dtype=bf16),
            arr(size_y, TILE, NZ, dtype=i32),
            arr(size_y, TILE, NZ, dtype=i32),
            arr(12, TILE, NZ),
        ],
        scratch_shapes=[
            buf(NX, NY, NZ),
            buf(NX, NY, NZ, dtype=i32),
            buf(NX, NY, NZ, dtype=i32),
            pltpu.SMEM((4,), f32),
            pltpu.SMEM((4,), f32),
            pltpu.SMEM((4,), f32),
            pltpu.SemaphoreType.DMA((6,)),
        ],
        compiler_params=params(14),
    )(*in_hbm(*tables, temp, ident, chip), xa, xb, sites)

    start, _, _, _, _, w0, w1, w2, send = pl.pallas_call(
        krylov_kernel,
        name="krylov",
        in_specs=[vmem] * 9,
        out_specs=[vmem] * 9,
        out_shape=[padded] * 8 + [arr(size_x, BLOCK, PART, NZ)],
        input_output_aliases={1: 0, 2: 1, 3: 2, 4: 3, 5: 4},
        scratch_shapes=[buf(PX, PY, NZ)] * 3,
        compiler_params=params(24),
    )(table_tiles, *own, ya, yb)
    table = lax.all_to_all(send, "gx", 0, 0)
    found = pl.pallas_call(
        lookup_kernel,
        name="lookup",
        in_specs=[vmem] * 4,
        out_specs=vmem,
        out_shape=arr(size_y, BLOCK, PART, NZ),
        scratch_shapes=[
            buf(NZ * (FIELDS - 1), 2 * NZ, dtype=bf16),
            buf(size_x, TILE, NZ),
        ],
        compiler_params=params(20),
    )(hot, row, place, table)
    got = lax.all_to_all(found, "gy", 0, 0)
    temperature, growth = pl.pallas_call(
        final_kernel,
        name="finish",
        in_specs=[vmem, anywhere, vmem, vmem, vmem, vmem],
        out_specs=[anywhere, vmem],
        out_shape=[arr(NX, NY, NZ), arr(TILE, NZ)],
        scratch_shapes=[
            buf(TILE, NZ),
            buf(NX, NY, NZ),
            pltpu.SemaphoreType.DMA(()),
            pltpu.SemaphoreType.DMA((4,)),
        ],
        compiler_params=params(12),
    )(got, *in_hbm(clearance_face_pressure.reshape(TILE, NZ)), start, w0, w1, w2)
    return temperature, growth.reshape(-1)


def solution(mesh):
    in_specs = (
        P("gx", "gy", None),
        P("gx", "gy", None),
        P("gx", "gy", None),
        P(),
        P(),
        P(),
        P(("gx", "gy")),
        P(("gx", "gy")),
    )
    out_specs = (P("gx", "gy", None), P(("gx", "gy")))
    return jax.shard_map(local, mesh=mesh, in_specs=in_specs, out_specs=out_specs, check_vma=False)
```

```python
import jax
import jax.numpy as jnp
from jax import lax
from jax.experimental import pallas as pl
from jax.experimental.pallas import tpu as pltpu
from jax.sharding import PartitionSpec as P

clock_advance = 2.0
interface_warming_rate = 3.0
usui_rate = 3.0
usui_energy = 4.0
kelvin_shift_amount = 2.0

LOW = 3
HIGH = 4
NX = 32
NY = 32
NZ = 128
PX = NX + HIGH + LOW
PY = NY + 8
FIELDS = 4
TILE = 8
PART = 2
PARTS = TILE // PART
BLOCK = PARTS * FIELDS + 1
PAIRS = 20
MIB = 1024 * 1024
f32 = jnp.float32
bf16 = jnp.bfloat16


def swaps(count, first):
    low = range(first, count - 1, 2)
    return [(i, i + 1) for i in low] + [(i + 1, i) for i in low]


def sublane(shape):
    return lax.broadcasted_iota(jnp.int32, shape, len(shape) - 2)


def lane(shape):
    return lax.broadcasted_iota(jnp.int32, shape, len(shape) - 1)


def first_tile(sub, temp, ident):
    return jnp.where(sub < 4, temp, pltpu.roll(ident, 4, 0))


def last_tile(sub, temp, ident, chip):
    return jnp.where(
        sub >= 5, temp, jnp.where(sub >= 2, pltpu.roll(ident, 5, 0), pltpu.roll(chip, 2, 0))
    )


def pack_kernel(
    t_hbm,
    id_hbm,
    chip_hbm,
    site_hbm,
    xa,
    xb,
    ya,
    yb,
    sites,
    t_a,
    t_b,
    i_a,
    i_b,
    c_a,
    c_b,
    t_p,
    t_m,
    i_p,
    i_m,
    c_p,
    c_m,
    site_ref,
    sems,
):
    copies = []
    for k, (src, dst) in enumerate(
        (
            (t_hbm.at[pl.ds(0, HIGH)], t_p),
            (id_hbm.at[pl.ds(0, HIGH)], i_p),
            (chip_hbm.at[pl.ds(0, HIGH)], c_p),
            (t_hbm.at[pl.ds(NX - HIGH, HIGH)], t_m),
            (id_hbm.at[pl.ds(NX - HIGH, HIGH)], i_m),
            (chip_hbm.at[pl.ds(NX - HIGH, HIGH)], c_m),
            (t_hbm.at[:, pl.ds(0, TILE)], t_a),
            (id_hbm.at[:, pl.ds(0, TILE)], i_a),
            (chip_hbm.at[:, pl.ds(0, TILE)], c_a),
            (t_hbm.at[:, pl.ds(NY - TILE, TILE)], t_b),
            (id_hbm.at[:, pl.ds(NY - TILE, TILE)], i_b),
            (chip_hbm.at[:, pl.ds(NY - TILE, TILE)], c_b),
            (site_hbm, site_ref),
        )
    ):
        copies.append(pltpu.make_async_copy(src, dst, sems.at[k]))
        copies[-1].start()
    for copy in copies[:6]:
        copy.wait()

    def x_sides(low, high):
        for k in range(HIGH):
            low[k] = t_p[k]
            low[4 + k] = i_p[k].astype(f32)
            if k < 3:
                low[8 + k] = c_p[k].astype(f32)
                high[k] = t_m[1 + k]
                high[3 + k] = i_m[1 + k].astype(f32)
            if k < 2:
                high[6 + k] = c_m[2 + k].astype(f32)

    even_x = lax.rem(lax.axis_index("gx"), 2) == 0
    even_y = lax.rem(lax.axis_index("gy"), 2) == 0

    @pl.when(even_x)
    def _():
        x_sides(xa, xb)

    @pl.when(jnp.logical_not(even_x))
    def _():
        x_sides(xb, xa)

    for copy in copies[6:]:
        copy.wait()
    sub = sublane((TILE, NZ))

    def own(q, _):
        low = first_tile(sub, t_a[q], i_a[q].astype(f32))
        high = last_tile(sub, t_b[q], i_b[q].astype(f32), c_b[q].astype(f32))
        ya[q] = jnp.where(even_y, low, high)
        yb[q] = jnp.where(even_y, high, low)
        return 0

    lax.fori_loop(0, NX, own, 0, unroll=8)
    for j in range(PAIRS):
        tile = c_a[j].astype(f32)
        if j + PAIRS < NX:
            tile = jnp.where(sub < 4, tile, pltpu.roll(c_a[j + PAIRS].astype(f32), 4, 0))
        ya[PX + j] = tile
        yb[PX + j] = tile
    for k in range(sites.shape[0]):
        sites[k] = site_ref[...]


def corner_kernel(ya_in, yb_in, xa_ref, xb_ref, sites_in, ya, yb, sites_out):
    del ya_in, yb_in, sites_in, sites_out
    even_x = lax.rem(lax.axis_index("gx"), 2) == 0
    even_y = lax.rem(lax.axis_index("gy"), 2) == 0
    sub = sublane((TILE, NZ))
    zero = jnp.zeros((TILE, NZ), f32)
    first = pl.ds(0, TILE)
    last = pl.ds(NY - TILE, TILE)

    def high_side(k, rows):
        return jnp.where(even_x, xb_ref[k, rows, :], xa_ref[k, rows, :])

    def low_side(k, rows):
        return jnp.where(even_x, xa_ref[k, rows, :], xb_ref[k, rows, :])

    for k in range(HIGH + LOW):
        q = NX + k
        if k < HIGH:
            side, places = high_side, (k, 4 + k, 8 + k if k < 3 else None)
        else:
            j = k - HIGH
            side, places = low_side, (j, 3 + j, 5 + j if j else None)
        temp, ident, chip = places
        low = first_tile(sub, side(temp, first), side(ident, first))
        high = last_tile(
            sub, side(temp, last), side(ident, last), zero if chip is None else side(chip, last)
        )
        ya[q] = jnp.where(even_y, low, high)
        yb[q] = jnp.where(even_y, high, low)
        if chip is not None:
            place = PX + q - PAIRS
            tile = jnp.where(sub < 4, ya[place], pltpu.roll(side(chip, first), 4, 0))
            ya[place] = tile
            yb[place] = tile


def pick(ident, table):
    low = jnp.where(ident == 1, table(1), table(0))
    high = jnp.where(ident == 3, table(3), table(2))
    return jnp.where(ident >= 2, high, low)


def up_z(v):
    return pltpu.roll(v, NZ - 1, 1)


def down_z(v):
    return pltpu.roll(v, 1, 1)


def cells(temp, ident, chip, tables, inside=None):
    ref_ref, grad_ref, store_ref = tables
    conduct = pick(ident, ref_ref) * (
        1.0 + pick(ident, grad_ref) * jnp.tanh(temp - kelvin_shift_amount)
    )
    if inside is not None:
        conduct = conduct * inside
    lanes = lane(temp.shape)
    inner_z = jnp.where(lanes < NZ - 1, 1.0, 0.0).astype(f32)
    edge_z = jnp.where((lanes == 0) | (lanes == NZ - 1), 1.0, 0.0).astype(f32)
    e_z = (conduct + up_z(conduct)) * inner_z
    f_z = e_z * (up_z(temp) - temp)
    c_b = conduct * edge_z
    diag = (pick(ident, store_ref) + c_b) + (e_z + down_z(e_z))
    resid = (clock_advance * interface_warming_rate * chip - c_b * temp) + (f_z - down_z(f_z))
    return conduct, diag, resid, e_z


def surface(read, terms):
    rows = sublane((TILE, NZ))
    diagonal = sublane((NZ, NZ)) == lane((NZ, NZ))
    first = jnp.where(sublane((NZ, NZ)) == 0, 1.0, 0.0).astype(bf16)
    total = jnp.zeros((TILE, NZ), f32)
    for s in range(TILE):
        rest = read(s)
        line = jnp.zeros((NZ, NZ), f32)
        for _ in range(terms):
            part = rest.astype(bf16)
            line = line + jnp.dot(part, first, preferred_element_type=f32)
            rest = rest - part.astype(f32)
        line = jnp.sum(jnp.where(diagonal, line, 0.0), axis=0, keepdims=True)
        total = jnp.where(rows == s, line, total)
    return total


def own_rows(ref):
    per = NX // TILE
    return lambda s: jnp.concatenate([ref[per * s + i, :NY, :] for i in range(per)], axis=0)


def own_kernel(
    ref_hbm,
    grad_hbm,
    store_hbm,
    t_hbm,
    id_hbm,
    chip_hbm,
    xa_ref,
    xb_ref,
    site_ref,
    tp,
    cp,
    dp,
    rp,
    ez,
    surf_ref,
    hot_ref,
    row_ref,
    lane_ref,
    table_ref,
    t_ref,
    id_ref,
    chip_ref,
    ref_ref,
    grad_ref,
    store_ref,
    sems,
):
    ix = lax.axis_index("gx")
    iy = lax.axis_index("gy")

    copies = [
        pltpu.make_async_copy(src, dst, sems.at[k])
        for k, (src, dst) in enumerate(
            (
                (ref_hbm, ref_ref),
                (grad_hbm, grad_ref),
                (store_hbm, store_ref),
                (t_hbm, t_ref),
                (id_hbm, id_ref),
                (chip_hbm, chip_ref),
            )
        )
    ]
    for copy in copies:
        copy.start()

    width = NY * lax.axis_size("gy")
    subs = sublane((NZ, NZ))

    def places(b, _):
        site = site_ref[b]
        row = site // width
        col = site - row * width
        here = (col // NY) == iy
        cell = (row % NX) * NY + col % NY
        row_of = jnp.where(here, (row // NX) * TILE + cell // NZ, -1)
        row_ref[b] = row_of
        lane_ref[b] = cell % NZ
        for s in range(TILE):
            hit = subs == jnp.broadcast_to(row_of[s : s + 1], (NZ, NZ))
            hot_ref[b, :, NZ * s : NZ * (s + 1)] = jnp.where(hit, 1.0, 0.0).astype(bf16)
        return 0

    lax.fori_loop(0, site_ref.shape[0], places, 0, unroll=2)
    for copy in copies:
        copy.wait()

    tables = [lambda k, ref=ref: ref[k] for ref in (ref_ref, grad_ref, store_ref)]
    for j, table in enumerate(tables):
        for k in range(4):
            table_ref[4 * j + k] = jnp.full((TILE, NZ), table(k), f32)

    def put(q, temp, ident, chip, inside=None):
        conduct, diag, resid, e_z = cells(temp, ident, chip, tables, inside)
        tp[q, :NY, :] = temp
        cp[q, :NY, :] = conduct
        dp[q, :NY, :] = diag
        rp[q, :NY, :] = resid
        ez[q, :NY, :] = e_z

    def own_plane(q, _):
        put(q, t_ref[q], id_ref[q], chip_ref[q].astype(f32))
        return 0

    lax.fori_loop(0, NX, own_plane, 0, unroll=4)

    even_x = lax.rem(ix, 2) == 0
    low_x = jnp.where(ix > 0, 1.0, 0.0).astype(f32)
    high_x = jnp.where(ix < lax.axis_size("gx") - 1, 1.0, 0.0).astype(f32)
    zero_plane = jnp.zeros((NY, NZ), f32)

    def high_plane(k):
        return jnp.where(even_x, xb_ref[k], xa_ref[k])

    def low_plane(k):
        return jnp.where(even_x, xa_ref[k], xb_ref[k])

    for k in range(HIGH):
        chip = high_plane(8 + k) if k < 3 else zero_plane
        put(NX + k, high_plane(k), high_plane(4 + k), chip, high_x)
    for k in range(LOW):
        chip = low_plane(5 + k) if k > 0 else zero_plane
        put(NX + HIGH + k, low_plane(k), low_plane(3 + k), chip, low_x)

    surf_ref[...] = surface(own_rows(t_ref), 3)


def krylov_kernel(
    table_ref,
    tp_in,
    cp_in,
    dp_in,
    rp_in,
    ez_in,
    surf_ref,
    ya_ref,
    yb_ref,
    tp,
    cp,
    dp,
    rp,
    ez,
    w0_ref,
    w1_ref,
    w2_ref,
    send_ref,
    ex,
    ey,
    dinv,
):
    del tp_in, cp_in, dp_in, rp_in, ez_in
    tables = [lambda k, j=j: table_ref[4 * j + k] for j in range(3)]
    ix = lax.axis_index("gx")
    iy = lax.axis_index("gy")
    last_x = lax.axis_size("gx") - 1
    last_y = lax.axis_size("gy") - 1
    sub = sublane((TILE, NZ))
    one = jnp.ones((), f32)
    low_x = jnp.where(ix > 0, 1.0, 0.0).astype(f32)
    high_x = jnp.where(ix < last_x, 1.0, 0.0).astype(f32)
    low_y = jnp.where(iy > 0, 1.0, 0.0).astype(f32)
    high_y = jnp.where(iy < last_y, 1.0, 0.0).astype(f32)
    rows_halo = jnp.where(sub < 4, high_y, low_y)

    even_y = lax.rem(iy, 2) == 0

    def high_row(q):
        return jnp.where(even_y, yb_ref[q], ya_ref[q])

    def low_row(q):
        return jnp.where(even_y, ya_ref[q], yb_ref[q])

    def put_halo(q, chip_high, plane_in):
        high = high_row(q)
        low = low_row(q)
        temp = jnp.where(sub < 4, high, low)
        ident = jnp.where(sub < 4, pltpu.roll(high, 4, 0), pltpu.roll(low, 3, 0))
        chip = jnp.where(sub < 4, chip_high, pltpu.roll(low, 6, 0))
        conduct, diag, resid, e_z = cells(temp, ident, chip, tables, rows_halo * plane_in)
        tp[q, NY:, :] = temp
        cp[q, NY:, :] = conduct
        dp[q, NY:, :] = diag
        rp[q, NY:, :] = resid
        ez[q, NY:, :] = e_z

    def own_halo_first(q, _):
        put_halo(q, high_row(PX + q), one)
        return 0

    def own_halo_second(q, _):
        put_halo(q, pltpu.roll(high_row(PX + q - PAIRS), 4, 0), one)
        return 0

    lax.fori_loop(0, PAIRS, own_halo_first, 0, unroll=20)
    lax.fori_loop(PAIRS, NX, own_halo_second, 0, unroll=12)

    zero_tile = jnp.zeros((TILE, NZ), f32)
    for q in range(NX, PX):
        put_halo(q, pltpu.roll(high_row(PX + q - PAIRS), 4, 0), high_x if q < NX + HIGH else low_x)

    subs = sublane((PY, NZ))
    rows_in = jnp.where(subs < NY, 1.0, jnp.where(subs < NY + 4, high_y, low_y)).astype(f32)

    def up_y(v):
        return pltpu.roll(v, PY - 1, 0)

    def down_y(v):
        return pltpu.roll(v, 1, 0)

    def fold(v):
        return (v[0:8] + v[8:16]) + (v[16:24] + v[24:32])

    def faces(q, nxt, ex_before, fx_before, plane_in):
        c0 = cp[q]
        t0 = tp[q]
        e_x = c0 + cp[nxt]
        f_x = e_x * (tp[nxt] - t0)
        e_y = c0 + up_y(c0)
        f_y = e_y * (up_y(t0) - t0)
        diag = dp[q] + ((e_x + ex_before) + (e_y + down_y(e_y)))
        inverse = (rows_in * plane_in) / diag
        resid = rp[q] + ((f_x - fx_before) + (f_y - down_y(f_y)))
        first = resid * inverse
        ex[q] = e_x
        ey[q] = e_y
        dinv[q] = inverse
        w0_ref[q] = first
        return e_x, f_x, resid, first

    e_first = cp[36] + cp[37]
    carry = (e_first, e_first * (tp[37] - tp[36]))
    for q, nxt in ((37, 38), (38, 0)):
        carry = faces(q, nxt, carry[0], carry[1], low_x)[:2]

    def faces_own(q, state):
        e_b, f_b, m0 = state
        e_x, f_x, resid, first = faces(q, q + 1, e_b, f_b, one)
        return e_x, f_x, m0 + fold(resid[:NY] * first[:NY])

    e_b, f_b, m0 = lax.fori_loop(0, NX, faces_own, (carry[0], carry[1], zero_tile), unroll=16)
    carry = (e_b, f_b)
    for q in (32, 33, 34):
        carry = faces(q, q + 1, carry[0], carry[1], high_x)[:2]

    def neighbours(src, q, nxt, g_before):
        v = src[q]
        e_x = ex[q]
        e_y = ey[q]
        e_z = ez[q]
        total = (e_x * src[nxt] + g_before) + (
            (e_y * up_y(v) + down_y(e_y * v)) + (e_z * up_z(v) + down_z(e_z * v))
        )
        return total, v, e_x * v

    def advance(src, dst, before, prologue, epilogue):
        carry = ex[before] * src[before]
        for q, nxt in prologue:
            total, _, carry = neighbours(src, q, nxt, carry)
            dst[q] = dinv[q] * total

        def step(q, state):
            g, ma, mb = state
            total, v, g = neighbours(src, q, q + 1, g)
            new = dinv[q] * total
            dst[q] = new
            ma = ma + fold(total[:NY] * v[:NY])
            mb = mb + fold(total[:NY] * new[:NY])
            return g, ma, mb

        carry, ma, mb = lax.fori_loop(0, NX, step, (carry, zero_tile, zero_tile), unroll=16)
        for q, nxt in epilogue:
            total, _, carry = neighbours(src, q, nxt, carry)
            dst[q] = dinv[q] * total
        return ma, mb

    m1, m2 = advance(w0_ref, w1_ref, 37, ((38, 0),), ((32, 33), (33, 34)))

    def crossing(q, v, after):
        half = ex[q] * after + (ey[q] * up_y(v) + ez[q] * up_z(v))
        return fold(half[:NY] * v[:NY])

    def second(q, g):
        total, v, g = neighbours(w1_ref, q, q + 1, g)
        new = dinv[q] * total
        w2_ref[q] = new
        return g, new, fold(total[:NY] * v[:NY]), fold(total[:NY] * new[:NY])

    g, before, m3, m4 = second(0, ex[38] * w1_ref[38])

    def step_2(q, state):
        g, before, ma, mb, mc = state
        g, new, a, b = second(q, g)
        return g, new, ma + a, mb + b, mc + crossing(q - 1, before, new)

    g, before, m3, m4, m5 = lax.fori_loop(
        1, NX, step_2, (g, before, m3, m4, zero_tile), unroll=31
    )
    total, _, _ = neighbours(w1_ref, NX, NX + 1, g)
    m5 = m5 + crossing(NX - 1, before, dinv[NX] * total)
    m5 = m5 + m5

    lanes = lane((PART, NZ))
    moments = jnp.zeros((PART, NZ), f32)
    for k, m in enumerate((m0, m1, m2, m3, m4, m5)):
        m = jnp.sum(jnp.sum(m, axis=0, keepdims=True), axis=1, keepdims=True)
        moments = jnp.where(lanes == k, jnp.broadcast_to(m, (PART, NZ)), moments)
    fields = [surf_ref[...]] + [surface(own_rows(w), 2) for w in (w0_ref, w1_ref, w2_ref)]
    pieces = [tile[i : i + PART] for tile in fields for i in range(0, TILE, PART)] + [moments]
    for k in range(send_ref.shape[0]):
        for j, piece in enumerate(pieces):
            send_ref[k, j] = piece


def lookup_kernel(hot_ref, row_ref, lane_ref, table_ref, out_ref, parts, start):
    blocks = table_ref.shape[0]
    targets = hot_ref.shape[0]
    sub = sublane((TILE, NZ))
    zero = jnp.zeros((TILE, NZ), f32)
    fields = FIELDS - 1

    def tile(a, f):
        return jnp.concatenate([table_ref[a, PARTS * f + i] for i in range(PARTS)], axis=0)

    for a in range(blocks):
        start[a] = tile(a, 0)
    for f in range(fields):
        rest = jnp.concatenate([tile(a, f + 1) for a in range(blocks)], axis=0).T
        for k in range(2):
            part = rest.astype(bf16)
            parts[NZ * f : NZ * (f + 1), NZ * k : NZ * (k + 1)] = part
            rest = rest - part.astype(f32)

    total = table_ref[0, PARTS * FIELDS]
    for a in range(1, blocks):
        total = total + table_ref[a, PARTS * FIELDS]

    def one(b, _):
        row_of = row_ref[b]
        lane_of = lane_ref[b]
        found = [zero] * FIELDS
        for pair in range(0, TILE, 2):
            hot = hot_ref[b, :, NZ * pair : NZ * (pair + 2)]
            hot = jnp.concatenate([hot, hot], axis=0)
            lanes = [jnp.broadcast_to(lane_of[pair + i : pair + i + 1], (TILE, NZ)) for i in (0, 1)]
            offset = [e - sub for e in lanes]
            for i in (0, 1):
                rows = jnp.broadcast_to(row_of[pair + i : pair + i + 1], (TILE, NZ)) - sub
                acc = zero
                for a in range(blocks):
                    got = jnp.take_along_axis(start[a], lanes[i], axis=1)
                    acc = jnp.where(rows == a * TILE, got, acc)
                found[0] = jnp.where(
                    sub == pair + i, jnp.sum(acc, axis=0, keepdims=True), found[0]
                )
            for f in range(fields):
                line = jnp.dot(parts[NZ * f : NZ * (f + 1)], hot, preferred_element_type=f32)
                for i in (0, 1):
                    acc = zero
                    for t in range(NZ // TILE):
                        acc = jnp.where(
                            offset[i] == t * TILE,
                            line[TILE * t : TILE * (t + 1), NZ * i : NZ * (i + 1)],
                            acc,
                        )
                    found[f + 1] = jnp.where(
                        sub == pair + i, jnp.sum(acc, axis=0, keepdims=True), found[f + 1]
                    )
        for f in range(FIELDS):
            for i in range(PARTS):
                out_ref[b, PARTS * f + i] = found[f][PART * i : PART * (i + 1)]
        out_ref[b, PARTS * FIELDS] = total
        return 0

    lax.fori_loop(0, targets, one, 0, unroll=16)


def cg_coefficients(m):
    a = [m[j] - m[j + 1] for j in range(5)]

    def quadratic(v, h):
        total = None
        for i in range(3):
            for j in range(3):
                if v[i] is None or v[j] is None:
                    continue
                term = v[i] * v[j] * h[i + j]
                total = term if total is None else total + term
        return total

    def add(u, v):
        return v if u is None else u if v is None else u + v

    def scale(s, v):
        return [None if e is None else s * e for e in v]

    one = jnp.ones_like(m[0])
    z = [one, None, None]
    p = [one, None, None]
    rz = m[0]
    x = [None, None, None]
    for step in range(3):
        alpha = rz / quadratic(p, a)
        x = [add(e, g) for e, g in zip(x, scale(alpha, p))]
        if step < 2:
            ap = scale(alpha, p)
            moved = [None] + ap[:2]
            z = [
                add(add(z[i], None if ap[i] is None else -ap[i]), moved[i]) for i in range(3)
            ]
            new = quadratic(z, m)
            p = [add(z[i], e) for i, e in enumerate(scale(new / rz, p))]
            rz = new
    return x


def final_kernel(
    got_ref,
    pressure_hbm,
    t_ref,
    w0_ref,
    w1_ref,
    w2_ref,
    temp_hbm,
    growth_ref,
    pressure_ref,
    temp_ref,
    sem,
    out_sems,
):
    copy = pltpu.make_async_copy(pressure_hbm, pressure_ref, sem)
    copy.start()
    total = got_ref[0]
    for b in range(1, got_ref.shape[0]):
        total = total + got_ref[b]
    m = [total[PARTS * FIELDS, 0:1, k : k + 1] for k in range(6)]
    fields = [
        jnp.concatenate([total[PARTS * f + i] for i in range(PARTS)], axis=0)
        for f in range(FIELDS)
    ]
    c = cg_coefficients(m)
    c_tile = [jnp.broadcast_to(e, (TILE, NZ)) for e in c]
    c_plane = [jnp.broadcast_to(e, (NY, NZ)) for e in c]

    def plane(q, _):
        temp_ref[q] = (
            t_ref[q, :NY, :]
            + c_plane[0] * w0_ref[q, :NY, :]
            + c_plane[1] * w1_ref[q, :NY, :]
            + c_plane[2] * w2_ref[q, :NY, :]
        )
        return 0

    outs = []
    step = NX // 4
    for k in range(4):
        lax.fori_loop(step * k, step * (k + 1), plane, 0, unroll=4)
        part = pl.ds(step * k, step)
        outs.append(pltpu.make_async_copy(temp_ref.at[part], temp_hbm.at[part], out_sems.at[k]))
        outs[-1].start()

    flank = fields[0]
    for k in range(3):
        flank = flank + c_tile[k] * fields[k + 1]
    soft = jnp.maximum(flank, 0.0) + jnp.log1p(jnp.exp(-jnp.abs(flank)))
    copy.wait()
    growth_ref[...] = usui_rate * pressure_ref[...] * jnp.exp(-usui_energy / (1.0 + soft))
    for out in outs:
        out.wait()


def local(
    prior_kelvin_state,
    substance_identifier,
    chip_touch_indicator,
    substance_reference_diffusivity,
    substance_diffusivity_gradient,
    substance_storage_coefficient,
    clearance_point_indices,
    clearance_face_pressure,
):
    size_x = lax.axis_size("gx")
    size_y = lax.axis_size("gy")
    temp, ident, chip = prior_kelvin_state, substance_identifier, chip_touch_indicator
    vmem = pl.BlockSpec(memory_space=pltpu.VMEM)

    def params(mib):
        return pltpu.CompilerParams(vmem_limit_bytes=mib * MIB)


    anywhere = pl.BlockSpec(memory_space=pltpu.HBM)

    def arr(*shape, dtype=f32):
        return jax.ShapeDtypeStruct(shape, dtype)

    def buf(*shape, dtype=f32):
        return pltpu.VMEM(shape, dtype)

    def in_hbm(*arrays):
        return [pltpu.with_memory_space_constraint(a, pltpu.HBM) for a in arrays]

    i32 = jnp.int32
    xa, xb, ya, yb, sites = pl.pallas_call(
        pack_kernel,
        name="pack",
        in_specs=[anywhere] * 4,
        out_specs=[vmem] * 5,
        out_shape=[
            arr(11, NY, NZ),
            arr(11, NY, NZ),
            arr(PX + PAIRS, TILE, NZ),
            arr(PX + PAIRS, TILE, NZ),
            arr(size_y, TILE, NZ, dtype=i32),
        ],
        scratch_shapes=[
            buf(NX, TILE, NZ),
            buf(NX, TILE, NZ),
            buf(NX, TILE, NZ, dtype=i32),
            buf(NX, TILE, NZ, dtype=i32),
            buf(NX, TILE, NZ, dtype=i32),
            buf(NX, TILE, NZ, dtype=i32),
            buf(HIGH, NY, NZ),
            buf(HIGH, NY, NZ),
            buf(HIGH, NY, NZ, dtype=i32),
            buf(HIGH, NY, NZ, dtype=i32),
            buf(HIGH, NY, NZ, dtype=i32),
            buf(HIGH, NY, NZ, dtype=i32),
            buf(TILE, NZ, dtype=i32),
            pltpu.SemaphoreType.DMA((13,)),
        ],
        compiler_params=params(10),
    )(*in_hbm(temp, ident, chip, clearance_point_indices.reshape(TILE, NZ)))
    sites = lax.all_to_all(sites, "gy", 0, 0)

    xa = lax.ppermute(xa, "gx", swaps(size_x, 1))
    xb = lax.ppermute(xb, "gx", swaps(size_x, 0))
    ya, yb, sites = pl.pallas_call(
        corner_kernel,
        name="corners",
        in_specs=[vmem] * 5,
        out_specs=[vmem] * 3,
        out_shape=[
            arr(PX + PAIRS, TILE, NZ),
            arr(PX + PAIRS, TILE, NZ),
            arr(size_y, TILE, NZ, dtype=i32),
        ],
        input_output_aliases={0: 0, 1: 1, 4: 2},
        compiler_params=params(8),
    )(ya, yb, xa, xb, sites)
    ya = lax.ppermute(ya, "gy", swaps(size_y, 1))
    yb = lax.ppermute(yb, "gy", swaps(size_y, 0))

    tables = (
        substance_reference_diffusivity,
        substance_diffusivity_gradient,
        substance_storage_coefficient,
    )
    padded = arr(PX, PY, NZ)
    *own, hot, row, place, table_tiles = pl.pallas_call(
        own_kernel,
        name="own_cells",
        in_specs=[anywhere] * 6 + [vmem] * 3,
        out_specs=[vmem] * 10,
        out_shape=[padded] * 5
        + [
            arr(TILE, NZ),
            arr(size_y, NZ, TILE * NZ, dtype=bf16),
            arr(size_y, TILE, NZ, dtype=i32),
            arr(size_y, TILE, NZ, dtype=i32),
            arr(12, TILE, NZ),
        ],
        scratch_shapes=[
            buf(NX, NY, NZ),
            buf(NX, NY, NZ, dtype=i32),
            buf(NX, NY, NZ, dtype=i32),
            pltpu.SMEM((4,), f32),
            pltpu.SMEM((4,), f32),
            pltpu.SMEM((4,), f32),
            pltpu.SemaphoreType.DMA((6,)),
        ],
        compiler_params=params(14),
    )(*in_hbm(*tables, temp, ident, chip), xa, xb, sites)

    start, _, _, _, _, w0, w1, w2, send = pl.pallas_call(
        krylov_kernel,
        name="krylov",
        in_specs=[vmem] * 9,
        out_specs=[vmem] * 9,
        out_shape=[padded] * 8 + [arr(size_x, BLOCK, PART, NZ)],
        input_output_aliases={1: 0, 2: 1, 3: 2, 4: 3, 5: 4},
        scratch_shapes=[buf(PX, PY, NZ)] * 3,
        compiler_params=params(24),
    )(table_tiles, *own, ya, yb)
    table = lax.all_to_all(send, "gx", 0, 0)
    found = pl.pallas_call(
        lookup_kernel,
        name="lookup",
        in_specs=[vmem] * 4,
        out_specs=vmem,
        out_shape=arr(size_y, BLOCK, PART, NZ),
        scratch_shapes=[
            buf(NZ * (FIELDS - 1), 2 * NZ, dtype=bf16),
            buf(size_x, TILE, NZ),
        ],
        compiler_params=params(20),
    )(hot, row, place, table)
    got = lax.all_to_all(found, "gy", 0, 0)
    temperature, growth = pl.pallas_call(
        final_kernel,
        name="finish",
        in_specs=[vmem, anywhere, vmem, vmem, vmem, vmem],
        out_specs=[anywhere, vmem],
        out_shape=[arr(NX, NY, NZ), arr(TILE, NZ)],
        scratch_shapes=[
            buf(TILE, NZ),
            buf(NX, NY, NZ),
            pltpu.SemaphoreType.DMA(()),
            pltpu.SemaphoreType.DMA((4,)),
        ],
        compiler_params=params(12),
    )(got, *in_hbm(clearance_face_pressure.reshape(TILE, NZ)), start, w0, w1, w2)
    return temperature, growth.reshape(-1)


def solution(mesh):
    in_specs = (
        P("gx", "gy", None),
        P("gx", "gy", None),
        P("gx", "gy", None),
        P(),
        P(),
        P(),
        P(("gx", "gy")),
        P(("gx", "gy")),
    )
    out_specs = (P("gx", "gy", None), P(("gx", "gy")))
    return jax.shard_map(local, mesh=mesh, in_specs=in_specs, out_specs=out_specs, check_vma=False)
```

```python
import jax
import jax.numpy as jnp
from jax import lax
from jax.experimental import pallas as pl
from jax.experimental.pallas import tpu as pltpu
from jax.sharding import PartitionSpec as P

clock_advance = 2.0
interface_warming_rate = 3.0
usui_rate = 3.0
usui_energy = 4.0
kelvin_shift_amount = 2.0

LOW = 3
HIGH = 4
NX = 32
NY = 32
NZ = 128
PX = NX + HIGH + LOW
PY = NY + 8
FIELDS = 4
TILE = 8
PART = 1
PARTS = TILE // PART
BLOCK = PARTS * FIELDS + 1
PAIRS = 20
MIB = 1024 * 1024
f32 = jnp.float32
bf16 = jnp.bfloat16


def swaps(count, first):
    low = range(first, count - 1, 2)
    return [(i, i + 1) for i in low] + [(i + 1, i) for i in low]


def sublane(shape):
    return lax.broadcasted_iota(jnp.int32, shape, len(shape) - 2)


def lane(shape):
    return lax.broadcasted_iota(jnp.int32, shape, len(shape) - 1)


def first_tile(sub, temp, ident):
    return jnp.where(sub < 4, temp, pltpu.roll(ident, 4, 0))


def last_tile(sub, temp, ident, chip):
    return jnp.where(
        sub >= 5, temp, jnp.where(sub >= 2, pltpu.roll(ident, 5, 0), pltpu.roll(chip, 2, 0))
    )


def pack_kernel(
    t_hbm,
    id_hbm,
    chip_hbm,
    site_hbm,
    xa,
    xb,
    ya,
    yb,
    sites,
    t_a,
    t_b,
    i_a,
    i_b,
    c_a,
    c_b,
    t_p,
    t_m,
    i_p,
    i_m,
    c_p,
    c_m,
    site_ref,
    sems,
):
    copies = []
    for k, (src, dst) in enumerate(
        (
            (t_hbm.at[pl.ds(0, HIGH)], t_p),
            (id_hbm.at[pl.ds(0, HIGH)], i_p),
            (chip_hbm.at[pl.ds(0, HIGH)], c_p),
            (t_hbm.at[pl.ds(NX - HIGH, HIGH)], t_m),
            (id_hbm.at[pl.ds(NX - HIGH, HIGH)], i_m),
            (chip_hbm.at[pl.ds(NX - HIGH, HIGH)], c_m),
            (t_hbm.at[:, pl.ds(0, TILE)], t_a),
            (id_hbm.at[:, pl.ds(0, TILE)], i_a),
            (chip_hbm.at[:, pl.ds(0, TILE)], c_a),
            (t_hbm.at[:, pl.ds(NY - TILE, TILE)], t_b),
            (id_hbm.at[:, pl.ds(NY - TILE, TILE)], i_b),
            (chip_hbm.at[:, pl.ds(NY - TILE, TILE)], c_b),
            (site_hbm, site_ref),
        )
    ):
        copies.append(pltpu.make_async_copy(src, dst, sems.at[k]))
        copies[-1].start()
    for copy in copies[:6]:
        copy.wait()

    def x_sides(low, high):
        for k in range(HIGH):
            low[k] = t_p[k]
            low[4 + k] = i_p[k].astype(f32)
            if k < 3:
                low[8 + k] = c_p[k].astype(f32)
                high[k] = t_m[1 + k]
                high[3 + k] = i_m[1 + k].astype(f32)
            if k < 2:
                high[6 + k] = c_m[2 + k].astype(f32)

    even_x = lax.rem(lax.axis_index("gx"), 2) == 0
    even_y = lax.rem(lax.axis_index("gy"), 2) == 0

    @pl.when(even_x)
    def _():
        x_sides(xa, xb)

    @pl.when(jnp.logical_not(even_x))
    def _():
        x_sides(xb, xa)

    for copy in copies[6:]:
        copy.wait()
    sub = sublane((TILE, NZ))

    def own(q, _):
        low = first_tile(sub, t_a[q], i_a[q].astype(f32))
        high = last_tile(sub, t_b[q], i_b[q].astype(f32), c_b[q].astype(f32))
        ya[q] = jnp.where(even_y, low, high)
        yb[q] = jnp.where(even_y, high, low)
        return 0

    lax.fori_loop(0, NX, own, 0, unroll=8)
    for j in range(PAIRS):
        tile = c_a[j].astype(f32)
        if j + PAIRS < NX:
            tile = jnp.where(sub < 4, tile, pltpu.roll(c_a[j + PAIRS].astype(f32), 4, 0))
        ya[PX + j] = tile
        yb[PX + j] = tile
    for k in range(sites.shape[0]):
        sites[k] = site_ref[...]


def corner_kernel(ya_in, yb_in, xa_ref, xb_ref, sites_in, ya, yb, sites_out):
    del ya_in, yb_in, sites_in, sites_out
    even_x = lax.rem(lax.axis_index("gx"), 2) == 0
    even_y = lax.rem(lax.axis_index("gy"), 2) == 0
    sub = sublane((TILE, NZ))
    zero = jnp.zeros((TILE, NZ), f32)
    first = pl.ds(0, TILE)
    last = pl.ds(NY - TILE, TILE)

    def high_side(k, rows):
        return jnp.where(even_x, xb_ref[k, rows, :], xa_ref[k, rows, :])

    def low_side(k, rows):
        return jnp.where(even_x, xa_ref[k, rows, :], xb_ref[k, rows, :])

    for k in range(HIGH + LOW):
        q = NX + k
        if k < HIGH:
            side, places = high_side, (k, 4 + k, 8 + k if k < 3 else None)
        else:
            j = k - HIGH
            side, places = low_side, (j, 3 + j, 5 + j if j else None)
        temp, ident, chip = places
        low = first_tile(sub, side(temp, first), side(ident, first))
        high = last_tile(
            sub, side(temp, last), side(ident, last), zero if chip is None else side(chip, last)
        )
        ya[q] = jnp.where(even_y, low, high)
        yb[q] = jnp.where(even_y, high, low)
        if chip is not None:
            place = PX + q - PAIRS
            tile = jnp.where(sub < 4, ya[place], pltpu.roll(side(chip, first), 4, 0))
            ya[place] = tile
            yb[place] = tile


def pick(ident, table):
    low = jnp.where(ident == 1, table(1), table(0))
    high = jnp.where(ident == 3, table(3), table(2))
    return jnp.where(ident >= 2, high, low)


def up_z(v):
    return pltpu.roll(v, NZ - 1, 1)


def down_z(v):
    return pltpu.roll(v, 1, 1)


def cells(temp, ident, chip, tables, inside=None):
    ref_ref, grad_ref, store_ref = tables
    conduct = pick(ident, ref_ref) * (
        1.0 + pick(ident, grad_ref) * jnp.tanh(temp - kelvin_shift_amount)
    )
    if inside is not None:
        conduct = conduct * inside
    lanes = lane(temp.shape)
    inner_z = jnp.where(lanes < NZ - 1, 1.0, 0.0).astype(f32)
    edge_z = jnp.where((lanes == 0) | (lanes == NZ - 1), 1.0, 0.0).astype(f32)
    e_z = (conduct + up_z(conduct)) * inner_z
    f_z = e_z * (up_z(temp) - temp)
    c_b = conduct * edge_z
    diag = (pick(ident, store_ref) + c_b) + (e_z + down_z(e_z))
    resid = (clock_advance * interface_warming_rate * chip - c_b * temp) + (f_z - down_z(f_z))
    return conduct, diag, resid, e_z


def surface(read, terms):
    rows = sublane((TILE, NZ))
    diagonal = sublane((NZ, NZ)) == lane((NZ, NZ))
    first = jnp.where(sublane((NZ, NZ)) == 0, 1.0, 0.0).astype(bf16)
    total = jnp.zeros((TILE, NZ), f32)
    for s in range(TILE):
        rest = read(s)
        line = jnp.zeros((NZ, NZ), f32)
        for _ in range(terms):
            part = rest.astype(bf16)
            line = line + jnp.dot(part, first, preferred_element_type=f32)
            rest = rest - part.astype(f32)
        line = jnp.sum(jnp.where(diagonal, line, 0.0), axis=0, keepdims=True)
        total = jnp.where(rows == s, line, total)
    return total


def own_rows(ref):
    per = NX // TILE
    return lambda s: jnp.concatenate([ref[per * s + i, :NY, :] for i in range(per)], axis=0)


def own_kernel(
    ref_hbm,
    grad_hbm,
    store_hbm,
    t_hbm,
    id_hbm,
    chip_hbm,
    xa_ref,
    xb_ref,
    site_ref,
    tp,
    cp,
    dp,
    rp,
    ez,
    surf_ref,
    hot_ref,
    row_ref,
    lane_ref,
    table_ref,
    t_ref,
    id_ref,
    chip_ref,
    ref_ref,
    grad_ref,
    store_ref,
    sems,
):
    ix = lax.axis_index("gx")
    iy = lax.axis_index("gy")

    copies = [
        pltpu.make_async_copy(src, dst, sems.at[k])
        for k, (src, dst) in enumerate(
            (
                (ref_hbm, ref_ref),
                (grad_hbm, grad_ref),
                (store_hbm, store_ref),
                (t_hbm, t_ref),
                (id_hbm, id_ref),
                (chip_hbm, chip_ref),
            )
        )
    ]
    for copy in copies:
        copy.start()

    width = NY * lax.axis_size("gy")
    subs = sublane((NZ, NZ))

    def places(b, _):
        site = site_ref[b]
        row = site // width
        col = site - row * width
        here = (col // NY) == iy
        cell = (row % NX) * NY + col % NY
        row_of = jnp.where(here, (row // NX) * TILE + cell // NZ, -1)
        row_ref[b] = row_of
        lane_ref[b] = cell % NZ
        for s in range(TILE):
            hit = subs == jnp.broadcast_to(row_of[s : s + 1], (NZ, NZ))
            hot_ref[b, :, NZ * s : NZ * (s + 1)] = jnp.where(hit, 1.0, 0.0).astype(bf16)
        return 0

    lax.fori_loop(0, site_ref.shape[0], places, 0, unroll=2)
    for copy in copies:
        copy.wait()

    tables = [lambda k, ref=ref: ref[k] for ref in (ref_ref, grad_ref, store_ref)]
    for j, table in enumerate(tables):
        for k in range(4):
            table_ref[4 * j + k] = jnp.full((TILE, NZ), table(k), f32)

    def put(q, temp, ident, chip, inside=None):
        conduct, diag, resid, e_z = cells(temp, ident, chip, tables, inside)
        tp[q, :NY, :] = temp
        cp[q, :NY, :] = conduct
        dp[q, :NY, :] = diag
        rp[q, :NY, :] = resid
        ez[q, :NY, :] = e_z

    def own_plane(q, _):
        put(q, t_ref[q], id_ref[q], chip_ref[q].astype(f32))
        return 0

    lax.fori_loop(0, NX, own_plane, 0, unroll=4)

    even_x = lax.rem(ix, 2) == 0
    low_x = jnp.where(ix > 0, 1.0, 0.0).astype(f32)
    high_x = jnp.where(ix < lax.axis_size("gx") - 1, 1.0, 0.0).astype(f32)
    zero_plane = jnp.zeros((NY, NZ), f32)

    def high_plane(k):
        return jnp.where(even_x, xb_ref[k], xa_ref[k])

    def low_plane(k):
        return jnp.where(even_x, xa_ref[k], xb_ref[k])

    for k in range(HIGH):
        chip = high_plane(8 + k) if k < 3 else zero_plane
        put(NX + k, high_plane(k), high_plane(4 + k), chip, high_x)
    for k in range(LOW):
        chip = low_plane(5 + k) if k > 0 else zero_plane
        put(NX + HIGH + k, low_plane(k), low_plane(3 + k), chip, low_x)

    surf_ref[...] = surface(own_rows(t_ref), 3)


def krylov_kernel(
    table_ref,
    tp_in,
    cp_in,
    dp_in,
    rp_in,
    ez_in,
    surf_ref,
    ya_ref,
    yb_ref,
    tp,
    cp,
    dp,
    rp,
    ez,
    w0_ref,
    w1_ref,
    w2_ref,
    send_ref,
    ex,
    ey,
    dinv,
):
    del tp_in, cp_in, dp_in, rp_in, ez_in
    tables = [lambda k, j=j: table_ref[4 * j + k] for j in range(3)]
    ix = lax.axis_index("gx")
    iy = lax.axis_index("gy")
    last_x = lax.axis_size("gx") - 1
    last_y = lax.axis_size("gy") - 1
    sub = sublane((TILE, NZ))
    one = jnp.ones((), f32)
    low_x = jnp.where(ix > 0, 1.0, 0.0).astype(f32)
    high_x = jnp.where(ix < last_x, 1.0, 0.0).astype(f32)
    low_y = jnp.where(iy > 0, 1.0, 0.0).astype(f32)
    high_y = jnp.where(iy < last_y, 1.0, 0.0).astype(f32)
    rows_halo = jnp.where(sub < 4, high_y, low_y)

    even_y = lax.rem(iy, 2) == 0

    def high_row(q):
        return jnp.where(even_y, yb_ref[q], ya_ref[q])

    def low_row(q):
        return jnp.where(even_y, ya_ref[q], yb_ref[q])

    def put_halo(q, chip_high, plane_in):
        high = high_row(q)
        low = low_row(q)
        temp = jnp.where(sub < 4, high, low)
        ident = jnp.where(sub < 4, pltpu.roll(high, 4, 0), pltpu.roll(low, 3, 0))
        chip = jnp.where(sub < 4, chip_high, pltpu.roll(low, 6, 0))
        conduct, diag, resid, e_z = cells(temp, ident, chip, tables, rows_halo * plane_in)
        tp[q, NY:, :] = temp
        cp[q, NY:, :] = conduct
        dp[q, NY:, :] = diag
        rp[q, NY:, :] = resid
        ez[q, NY:, :] = e_z

    def own_halo_first(q, _):
        put_halo(q, high_row(PX + q), one)
        return 0

    def own_halo_second(q, _):
        put_halo(q, pltpu.roll(high_row(PX + q - PAIRS), 4, 0), one)
        return 0

    lax.fori_loop(0, PAIRS, own_halo_first, 0, unroll=20)
    lax.fori_loop(PAIRS, NX, own_halo_second, 0, unroll=12)

    zero_tile = jnp.zeros((TILE, NZ), f32)
    for q in range(NX, PX):
        put_halo(q, pltpu.roll(high_row(PX + q - PAIRS), 4, 0), high_x if q < NX + HIGH else low_x)

    subs = sublane((PY, NZ))
    rows_in = jnp.where(subs < NY, 1.0, jnp.where(subs < NY + 4, high_y, low_y)).astype(f32)

    def up_y(v):
        return pltpu.roll(v, PY - 1, 0)

    def down_y(v):
        return pltpu.roll(v, 1, 0)

    def fold(v):
        return (v[0:8] + v[8:16]) + (v[16:24] + v[24:32])

    def faces(q, nxt, ex_before, fx_before, plane_in):
        c0 = cp[q]
        t0 = tp[q]
        e_x = c0 + cp[nxt]
        f_x = e_x * (tp[nxt] - t0)
        e_y = c0 + up_y(c0)
        f_y = e_y * (up_y(t0) - t0)
        diag = dp[q] + ((e_x + ex_before) + (e_y + down_y(e_y)))
        inverse = (rows_in * plane_in) / diag
        resid = rp[q] + ((f_x - fx_before) + (f_y - down_y(f_y)))
        first = resid * inverse
        ex[q] = e_x
        ey[q] = e_y
        dinv[q] = inverse
        w0_ref[q] = first
        return e_x, f_x, resid, first

    e_first = cp[36] + cp[37]
    carry = (e_first, e_first * (tp[37] - tp[36]))
    for q, nxt in ((37, 38), (38, 0)):
        carry = faces(q, nxt, carry[0], carry[1], low_x)[:2]

    def faces_own(q, state):
        e_b, f_b, m0 = state
        e_x, f_x, resid, first = faces(q, q + 1, e_b, f_b, one)
        return e_x, f_x, m0 + fold(resid[:NY] * first[:NY])

    e_b, f_b, m0 = lax.fori_loop(0, NX, faces_own, (carry[0], carry[1], zero_tile), unroll=16)
    carry = (e_b, f_b)
    for q in (32, 33, 34):
        carry = faces(q, q + 1, carry[0], carry[1], high_x)[:2]

    def neighbours(src, q, nxt, g_before):
        v = src[q]
        e_x = ex[q]
        e_y = ey[q]
        e_z = ez[q]
        total = (e_x * src[nxt] + g_before) + (
            (e_y * up_y(v) + down_y(e_y * v)) + (e_z * up_z(v) + down_z(e_z * v))
        )
        return total, v, e_x * v

    def advance(src, dst, before, prologue, epilogue):
        carry = ex[before] * src[before]
        for q, nxt in prologue:
            total, _, carry = neighbours(src, q, nxt, carry)
            dst[q] = dinv[q] * total

        def step(q, state):
            g, ma, mb = state
            total, v, g = neighbours(src, q, q + 1, g)
            new = dinv[q] * total
            dst[q] = new
            ma = ma + fold(total[:NY] * v[:NY])
            mb = mb + fold(total[:NY] * new[:NY])
            return g, ma, mb

        carry, ma, mb = lax.fori_loop(0, NX, step, (carry, zero_tile, zero_tile), unroll=8)
        for q, nxt in epilogue:
            total, _, carry = neighbours(src, q, nxt, carry)
            dst[q] = dinv[q] * total
        return ma, mb

    m1, m2 = advance(w0_ref, w1_ref, 37, ((38, 0),), ((32, 33), (33, 34)))

    def crossing(q, v, after):
        half = ex[q] * after + (ey[q] * up_y(v) + ez[q] * up_z(v))
        return fold(half[:NY] * v[:NY])

    def second(q, g):
        total, v, g = neighbours(w1_ref, q, q + 1, g)
        new = dinv[q] * total
        w2_ref[q] = new
        return g, new, fold(total[:NY] * v[:NY]), fold(total[:NY] * new[:NY])

    g, before, m3, m4 = second(0, ex[38] * w1_ref[38])

    def step_2(q, state):
        g, before, ma, mb, mc = state
        g, new, a, b = second(q, g)
        return g, new, ma + a, mb + b, mc + crossing(q - 1, before, new)

    g, before, m3, m4, m5 = lax.fori_loop(
        1, NX, step_2, (g, before, m3, m4, zero_tile), unroll=31
    )
    total, _, _ = neighbours(w1_ref, NX, NX + 1, g)
    m5 = m5 + crossing(NX - 1, before, dinv[NX] * total)
    m5 = m5 + m5

    lanes = lane((PART, NZ))
    moments = jnp.zeros((PART, NZ), f32)
    for k, m in enumerate((m0, m1, m2, m3, m4, m5)):
        m = jnp.sum(jnp.sum(m, axis=0, keepdims=True), axis=1, keepdims=True)
        moments = jnp.where(lanes == k, jnp.broadcast_to(m, (PART, NZ)), moments)
    fields = [surf_ref[...]] + [surface(own_rows(w), 2) for w in (w0_ref, w1_ref, w2_ref)]
    pieces = [tile[i : i + PART] for tile in fields for i in range(0, TILE, PART)] + [moments]
    for k in range(send_ref.shape[0]):
        for j, piece in enumerate(pieces):
            send_ref[k, j] = piece


def lookup_kernel(hot_ref, row_ref, lane_ref, table_ref, out_ref, parts, start):
    blocks = table_ref.shape[0]
    targets = hot_ref.shape[0]
    sub = sublane((TILE, NZ))
    zero = jnp.zeros((TILE, NZ), f32)
    fields = FIELDS - 1

    def tile(a, f):
        return jnp.concatenate([table_ref[a, PARTS * f + i] for i in range(PARTS)], axis=0)

    for a in range(blocks):
        start[a] = tile(a, 0)
    for f in range(fields):
        rest = jnp.concatenate([tile(a, f + 1) for a in range(blocks)], axis=0).T
        for k in range(2):
            part = rest.astype(bf16)
            parts[NZ * f : NZ * (f + 1), NZ * k : NZ * (k + 1)] = part
            rest = rest - part.astype(f32)

    total = table_ref[0, PARTS * FIELDS]
    for a in range(1, blocks):
        total = total + table_ref[a, PARTS * FIELDS]

    def one(b, _):
        row_of = row_ref[b]
        lane_of = lane_ref[b]
        found = [zero] * FIELDS
        for pair in range(0, TILE, 2):
            hot = hot_ref[b, :, NZ * pair : NZ * (pair + 2)]
            hot = jnp.concatenate([hot, hot], axis=0)
            lanes = [jnp.broadcast_to(lane_of[pair + i : pair + i + 1], (TILE, NZ)) for i in (0, 1)]
            offset = [e - sub for e in lanes]
            for i in (0, 1):
                rows = jnp.broadcast_to(row_of[pair + i : pair + i + 1], (TILE, NZ)) - sub
                acc = zero
                for a in range(blocks):
                    got = jnp.take_along_axis(start[a], lanes[i], axis=1)
                    acc = jnp.where(rows == a * TILE, got, acc)
                found[0] = jnp.where(
                    sub == pair + i, jnp.sum(acc, axis=0, keepdims=True), found[0]
                )
            for f in range(fields):
                line = jnp.dot(parts[NZ * f : NZ * (f + 1)], hot, preferred_element_type=f32)
                for i in (0, 1):
                    acc = zero
                    for t in range(NZ // TILE):
                        acc = jnp.where(
                            offset[i] == t * TILE,
                            line[TILE * t : TILE * (t + 1), NZ * i : NZ * (i + 1)],
                            acc,
                        )
                    found[f + 1] = jnp.where(
                        sub == pair + i, jnp.sum(acc, axis=0, keepdims=True), found[f + 1]
                    )
        for f in range(FIELDS):
            for i in range(PARTS):
                out_ref[b, PARTS * f + i] = found[f][PART * i : PART * (i + 1)]
        out_ref[b, PARTS * FIELDS] = total
        return 0

    lax.fori_loop(0, targets, one, 0, unroll=8)


def cg_coefficients(m):
    a = [m[j] - m[j + 1] for j in range(5)]

    def product(*factors):
        out = None
        for e in factors:
            if e is None:
                return None
            out = e if out is None else out * e
        return out

    def quadratic(v, h):
        v0, v1, v2 = v
        twice = None if v0 is None else v0 + v0
        cross = None if v1 is None else v1 + v1
        left = add(product(v0, v0, h[0]), product(twice, v1, h[1]))
        middle = product(add(product(twice, v2), product(v1, v1)), h[2])
        right = add(product(cross, v2, h[3]), product(v2, v2, h[4]))
        return add(add(left, middle), right)

    def add(u, v):
        return v if u is None else u if v is None else u + v

    def scale(s, v):
        return [None if e is None else s * e for e in v]

    one = jnp.ones_like(m[0])
    z = [one, None, None]
    p = [one, None, None]
    rz = m[0]
    x = [None, None, None]
    for step in range(3):
        alpha = rz / quadratic(p, a)
        x = [add(e, g) for e, g in zip(x, scale(alpha, p))]
        if step < 2:
            ap = scale(alpha, p)
            moved = [None] + ap[:2]
            z = [
                add(add(z[i], None if ap[i] is None else -ap[i]), moved[i]) for i in range(3)
            ]
            new = quadratic(z, m)
            p = [add(z[i], e) for i, e in enumerate(scale(new / rz, p))]
            rz = new
    return x


def final_kernel(
    got_ref,
    pressure_hbm,
    t_ref,
    w0_ref,
    w1_ref,
    w2_ref,
    temp_hbm,
    growth_ref,
    pressure_ref,
    temp_ref,
    sem,
    out_sems,
):
    copy = pltpu.make_async_copy(pressure_hbm, pressure_ref, sem)
    copy.start()
    total = got_ref[0]
    for b in range(1, got_ref.shape[0]):
        total = total + got_ref[b]
    m = [total[PARTS * FIELDS, 0:1, k : k + 1] for k in range(6)]
    fields = [
        jnp.concatenate([total[PARTS * f + i] for i in range(PARTS)], axis=0)
        for f in range(FIELDS)
    ]
    c = cg_coefficients(m)
    c_tile = [jnp.broadcast_to(e, (TILE, NZ)) for e in c]
    c_plane = [jnp.broadcast_to(e, (NY, NZ)) for e in c]

    def plane(q, _):
        temp_ref[q] = (
            t_ref[q, :NY, :]
            + c_plane[0] * w0_ref[q, :NY, :]
            + c_plane[1] * w1_ref[q, :NY, :]
            + c_plane[2] * w2_ref[q, :NY, :]
        )
        return 0

    outs = []
    step = NX // 4
    for k in range(4):
        lax.fori_loop(step * k, step * (k + 1), plane, 0, unroll=4)
        part = pl.ds(step * k, step)
        outs.append(pltpu.make_async_copy(temp_ref.at[part], temp_hbm.at[part], out_sems.at[k]))
        outs[-1].start()

    flank = fields[0]
    for k in range(3):
        flank = flank + c_tile[k] * fields[k + 1]
    soft = jnp.maximum(flank, 0.0) + jnp.log1p(jnp.exp(-jnp.abs(flank)))
    copy.wait()
    growth_ref[...] = usui_rate * pressure_ref[...] * jnp.exp(-usui_energy / (1.0 + soft))
    for out in outs:
        out.wait()


def local(
    prior_kelvin_state,
    substance_identifier,
    chip_touch_indicator,
    substance_reference_diffusivity,
    substance_diffusivity_gradient,
    substance_storage_coefficient,
    clearance_point_indices,
    clearance_face_pressure,
):
    size_x = lax.axis_size("gx")
    size_y = lax.axis_size("gy")
    temp, ident, chip = prior_kelvin_state, substance_identifier, chip_touch_indicator
    vmem = pl.BlockSpec(memory_space=pltpu.VMEM)

    def params(mib):
        return pltpu.CompilerParams(vmem_limit_bytes=mib * MIB)


    anywhere = pl.BlockSpec(memory_space=pltpu.HBM)

    def arr(*shape, dtype=f32):
        return jax.ShapeDtypeStruct(shape, dtype)

    def buf(*shape, dtype=f32):
        return pltpu.VMEM(shape, dtype)

    def in_hbm(*arrays):
        return [pltpu.with_memory_space_constraint(a, pltpu.HBM) for a in arrays]

    i32 = jnp.int32
    xa, xb, ya, yb, sites = pl.pallas_call(
        pack_kernel,
        name="pack",
        in_specs=[anywhere] * 4,
        out_specs=[vmem] * 5,
        out_shape=[
            arr(11, NY, NZ),
            arr(11, NY, NZ),
            arr(PX + PAIRS, TILE, NZ),
            arr(PX + PAIRS, TILE, NZ),
            arr(size_y, TILE, NZ, dtype=i32),
        ],
        scratch_shapes=[
            buf(NX, TILE, NZ),
            buf(NX, TILE, NZ),
            buf(NX, TILE, NZ, dtype=i32),
            buf(NX, TILE, NZ, dtype=i32),
            buf(NX, TILE, NZ, dtype=i32),
            buf(NX, TILE, NZ, dtype=i32),
            buf(HIGH, NY, NZ),
            buf(HIGH, NY, NZ),
            buf(HIGH, NY, NZ, dtype=i32),
            buf(HIGH, NY, NZ, dtype=i32),
            buf(HIGH, NY, NZ, dtype=i32),
            buf(HIGH, NY, NZ, dtype=i32),
            buf(TILE, NZ, dtype=i32),
            pltpu.SemaphoreType.DMA((13,)),
        ],
        compiler_params=params(10),
    )(*in_hbm(temp, ident, chip, clearance_point_indices.reshape(TILE, NZ)))
    sites = lax.all_to_all(sites, "gy", 0, 0)

    xa = lax.ppermute(xa, "gx", swaps(size_x, 1))
    xb = lax.ppermute(xb, "gx", swaps(size_x, 0))
    ya, yb, sites = pl.pallas_call(
        corner_kernel,
        name="corners",
        in_specs=[vmem] * 5,
        out_specs=[vmem] * 3,
        out_shape=[
            arr(PX + PAIRS, TILE, NZ),
            arr(PX + PAIRS, TILE, NZ),
            arr(size_y, TILE, NZ, dtype=i32),
        ],
        input_output_aliases={0: 0, 1: 1, 4: 2},
        compiler_params=params(8),
    )(ya, yb, xa, xb, sites)
    ya = lax.ppermute(ya, "gy", swaps(size_y, 1))
    yb = lax.ppermute(yb, "gy", swaps(size_y, 0))

    tables = (
        substance_reference_diffusivity,
        substance_diffusivity_gradient,
        substance_storage_coefficient,
    )
    padded = arr(PX, PY, NZ)
    *own, hot, row, place, table_tiles = pl.pallas_call(
        own_kernel,
        name="own_cells",
        in_specs=[anywhere] * 6 + [vmem] * 3,
        out_specs=[vmem] * 10,
        out_shape=[padded] * 5
        + [
            arr(TILE, NZ),
            arr(size_y, NZ, TILE * NZ, dtype=bf16),
            arr(size_y, TILE, NZ, dtype=i32),
            arr(size_y, TILE, NZ, dtype=i32),
            arr(12, TILE, NZ),
        ],
        scratch_shapes=[
            buf(NX, NY, NZ),
            buf(NX, NY, NZ, dtype=i32),
            buf(NX, NY, NZ, dtype=i32),
            pltpu.SMEM((4,), f32),
            pltpu.SMEM((4,), f32),
            pltpu.SMEM((4,), f32),
            pltpu.SemaphoreType.DMA((6,)),
        ],
        compiler_params=params(14),
    )(*in_hbm(*tables, temp, ident, chip), xa, xb, sites)

    start, _, _, _, _, w0, w1, w2, send = pl.pallas_call(
        krylov_kernel,
        name="krylov",
        in_specs=[vmem] * 9,
        out_specs=[vmem] * 9,
        out_shape=[padded] * 8 + [arr(size_x, BLOCK, PART, NZ)],
        input_output_aliases={1: 0, 2: 1, 3: 2, 4: 3, 5: 4},
        scratch_shapes=[buf(PX, PY, NZ)] * 3,
        compiler_params=params(24),
    )(table_tiles, *own, ya, yb)
    table = lax.all_to_all(send, "gx", 0, 0)
    found = pl.pallas_call(
        lookup_kernel,
        name="lookup",
        in_specs=[vmem] * 4,
        out_specs=vmem,
        out_shape=arr(size_y, BLOCK, PART, NZ),
        scratch_shapes=[
            buf(NZ * (FIELDS - 1), 2 * NZ, dtype=bf16),
            buf(size_x, TILE, NZ),
        ],
        compiler_params=params(20),
    )(hot, row, place, table)
    got = lax.all_to_all(found, "gy", 0, 0)
    temperature, growth = pl.pallas_call(
        final_kernel,
        name="finish",
        in_specs=[vmem, anywhere, vmem, vmem, vmem, vmem],
        out_specs=[anywhere, vmem],
        out_shape=[arr(NX, NY, NZ), arr(TILE, NZ)],
        scratch_shapes=[
            buf(TILE, NZ),
            buf(NX, NY, NZ),
            pltpu.SemaphoreType.DMA(()),
            pltpu.SemaphoreType.DMA((4,)),
        ],
        compiler_params=params(12),
    )(got, *in_hbm(clearance_face_pressure.reshape(TILE, NZ)), start, w0, w1, w2)
    return temperature, growth.reshape(-1)


def solution(mesh):
    in_specs = (
        P("gx", "gy", None),
        P("gx", "gy", None),
        P("gx", "gy", None),
        P(),
        P(),
        P(),
        P(("gx", "gy")),
        P(("gx", "gy")),
    )
    out_specs = (P("gx", "gy", None), P(("gx", "gy")))
    return jax.shard_map(local, mesh=mesh, in_specs=in_specs, out_specs=out_specs, check_vma=False)
```
